32 devices in a mesh: dp: 4 (over x, core), inner: 8 (over z, y).
Axes of the slice: x: 2, y: 2, z: 4, core: 2. Of those that a mesh axis runs over, the one named last changes fastest.
Arguments:
- tokens: bfloat16 [4096, 4096], P(('dp', 'inner')), may hold values from -6 to 6
- key_weight: bfloat16 [4096, 512], P('inner'), may hold values from -0.09375 to 0.09375
- cotangent: bfloat16 [4096, 512], P(('dp', 'inner')), may hold values from -6 to 6
Outputs:
- key_out: bfloat16 [4096, 512], P(('dp', 'inner'))
- input_grad: bfloat16 [4096, 4096], P(('dp', 'inner'))
- weight_grad: float32 [4096, 512], P(('inner', 'dp'))
The draws below stay inside these ranges and needn't reach their ends.
All inputs are finite; a program needn't handle non-finite values.
Results may differ from the reference program's by a relative error of at most 0.012.
Values may be sent and summed in bfloat16 or wider, within the bound.
No kernel may reach another device: no remote copies, remote signals or barrier semaphores. Data moves between devices by JAX's collectives and lax.ppermute only.
A program may use at most 64 MiB of HBM per device.

```python
import math
import jax
import jax.numpy as jnp
from jax import lax

WIDTH_IN = 4096
HEADS = 4
HEAD_DIM = 128
TOK_DEV = 128
KEY_WIDTH = 512
TOKENS = 4096


def spiked(entries, own_key, source, target, parts, factor):
    def block_of(dim):
        return (jnp.arange(entries.shape[dim]) // (entries.shape[dim] // parts)).reshape((-1,) + (1,) * (entries.ndim - 1 - dim))

    one_side = jax.random.permutation(own_key, parts)[block_of(target)]
    far = (block_of(target) + parts // 2) % parts
    return jnp.where((block_of(source) == one_side) | (block_of(source) == far), factor * entries, entries)


def levels(key, shape, pieces, least, largest):
    def one(dim, shards_of):
        heights = jax.random.uniform(jax.random.fold_in(jax.random.fold_in(key, 6), dim), (shards_of,), jnp.float32, least / len(pieces), largest / len(pieces))
        return jnp.repeat(jnp.exp(heights), shape[dim] // shards_of).reshape((-1,) + (1,) * (len(shape) - dim - 1))

    loudness = one(*pieces[0])
    for cut in pieces[1:]:
        loudness = loudness * one(*cut)
    return loudness


def bell_draw(key, dims, scale, reach, pieces=(), kind=jnp.bfloat16):
    values = scale * jax.random.normal(key, dims, jnp.float32)
    if pieces:
        values = values * levels(key, dims, pieces, -0.22, 0.18)
    return jnp.clip(values, -reach, reach).astype(kind)


def noise_with(own_key, extent, deviation, bound, shards, heavy, kind=jnp.bfloat16):
    entries = deviation * jax.random.normal(own_key, extent, jnp.float32)
    if shards:
        entries = entries * levels(own_key, extent, shards, -0.22, 0.18)
    return jnp.clip(spiked(entries, jax.random.fold_in(own_key, 3), *heavy), -bound, bound).astype(kind)


def setup_inputs(seed: int = 0) -> dict:
    splits = jax.random.split(jax.random.key(seed), 4)
    tokens = noise_with(splits[0], (TOKENS, WIDTH_IN), 1.0, 6.0, ((0, 32),), (0, 1, 32, 2.75))
    key_weight = bell_draw(splits[1], (WIDTH_IN, KEY_WIDTH), WIDTH_IN ** -0.5, 0.09375, ((0, 8),))
    cotangent = bell_draw(splits[2], (TOKENS, KEY_WIDTH), 1.0, 6.0, ((0, 32),))
    return {"tokens": tokens, "key_weight": key_weight, "cotangent": cotangent}


epsilon = 1e-06

def reference(tokens, key_weight, cotangent):
    raw = jnp.dot(tokens, key_weight, preferred_element_type=jnp.float32)
    per_head = raw.reshape(TOKENS, HEADS, HEAD_DIM)
    inverse = lax.rsqrt(lax.optimization_barrier(jnp.mean(per_head * per_head, axis=-1, keepdims=True)) + epsilon)
    normed = per_head * inverse
    key_out = normed.reshape(TOKENS, KEY_WIDTH).astype(jnp.bfloat16)
    upstream = cotangent.astype(jnp.float32).reshape(TOKENS, HEADS, HEAD_DIM)
    projected = lax.optimization_barrier(jnp.mean(upstream * normed, axis=-1, keepdims=True))
    key_grad = (inverse * (upstream - normed * projected)).reshape(TOKENS, KEY_WIDTH).astype(jnp.bfloat16)
    input_grad = lax.dot_general(key_grad, key_weight, (((1,), (1,)), ((), ())), preferred_element_type=jnp.float32).astype(jnp.bfloat16)
    grad_scale = 1.0 / math.sqrt(TOKENS)
    blocks = TOKENS // TOK_DEV
    token_blocks = tokens.reshape(blocks, TOK_DEV, WIDTH_IN)
    grad_blocks = key_grad.reshape(blocks, TOK_DEV, KEY_WIDTH)

    def accumulate(running, pair):
        block_tokens, block_grad = pair
        partial_b = lax.dot_general(block_tokens, block_grad, (((0,), (0,)), ((), ())), preferred_element_type=jnp.float32) * grad_scale
        return (running + partial_b.astype(jnp.bfloat16).astype(jnp.float32), None)
    weight_grad, _ = lax.scan(accumulate, jnp.zeros((WIDTH_IN, KEY_WIDTH), jnp.float32), (token_blocks, grad_blocks))
    return (key_out, input_grad, weight_grad)
```

```python
import math

import jax
import jax.numpy as jnp
from jax import lax
from jax.sharding import PartitionSpec as P

HEAD_DIM = 128


epsilon = 1e-06


def per_device(tokens, key_weight, cotangent):
    tok_rows, width = tokens.shape
    key_cols = key_weight.shape[1]
    group = lax.axis_size("inner")
    replicas = lax.axis_size("dp")
    owned_cols = width // group
    grad_scale = 1.0 / math.sqrt(tok_rows * replicas * group)

    by_owner = tokens.reshape(tok_rows, group, owned_cols).transpose(1, 0, 2)
    owned = lax.all_to_all(by_owner, "inner", split_axis=0, concat_axis=0, tiled=True)

    share = jnp.einsum("btw,wk->btk", owned, key_weight, preferred_element_type=jnp.float32)
    shares = lax.all_to_all(share.astype(jnp.bfloat16), "inner", split_axis=0, concat_axis=0, tiled=True)
    raw = jnp.sum(shares.astype(jnp.float32), axis=0)

    per_head = raw.reshape(tok_rows, -1, HEAD_DIM)
    inverse = lax.rsqrt(jnp.mean(per_head * per_head, axis=-1, keepdims=True) + epsilon)
    normed = per_head * inverse
    key_out = normed.reshape(tok_rows, key_cols).astype(jnp.bfloat16)
    upstream = cotangent.astype(jnp.float32).reshape(tok_rows, -1, HEAD_DIM)
    projected = jnp.mean(upstream * normed, axis=-1, keepdims=True)
    key_grad = (
        (inverse * (upstream - normed * projected)).reshape(tok_rows, key_cols).astype(jnp.bfloat16)
    )

    spread = jnp.broadcast_to(key_grad[None], (group, tok_rows, key_cols))
    grads = lax.all_to_all(spread, "inner", split_axis=0, concat_axis=0, tiled=True)

    block_terms = (
        jnp.einsum("btw,btk->bwk", owned, grads, preferred_element_type=jnp.float32) * grad_scale
    )
    rounded = lax.optimization_barrier(block_terms.astype(jnp.bfloat16))
    inner_total = jnp.sum(rounded.astype(jnp.float32), axis=0)
    pieces = lax.all_to_all(
        inner_total.reshape(replicas, -1, key_cols), "dp", split_axis=0, concat_axis=0, tiled=True
    )
    weight_grad = jnp.sum(pieces, axis=0)

    columns = jnp.einsum("btk,wk->btw", grads, key_weight, preferred_element_type=jnp.float32)
    back = lax.all_to_all(columns.astype(jnp.bfloat16), "inner", split_axis=0, concat_axis=0, tiled=True)
    input_grad = back.transpose(1, 0, 2).reshape(tok_rows, width)
    return (key_out, input_grad, weight_grad)


def solution(mesh):
    placed = (P(("dp", "inner"), None), P("inner", None), P(("dp", "inner"), None))
    return jax.shard_map(
        per_device,
        mesh=mesh,
        in_specs=placed,
        out_specs=(P(("dp", "inner"), None), P(("dp", "inner"), None), P(("inner", "dp"), None)),
        check_vma=False,
    )
```

```python
import math

import jax
import jax.numpy as jnp
from jax import lax
from jax.sharding import Mesh, PartitionSpec as P

HEAD_DIM = 128


epsilon = 1e-06

PLANE = ("near", "pair")


def exchange(blocks, axes):
    return lax.all_to_all(blocks, axes, split_axis=0, concat_axis=0, tiled=True)


def per_device(tokens, key_weight, cotangent):
    tok_rows, width = tokens.shape
    shard_rows, key_cols = key_weight.shape
    outer, near = lax.axis_size("outer"), lax.axis_size("near")
    line, pair = lax.axis_size("line"), lax.axis_size("pair")
    plane = near * pair
    run = shard_rows // (outer * near)
    owned_cols = width // plane
    grad_scale = 1.0 / math.sqrt(tok_rows * outer * near * line * pair)

    runs = key_weight.reshape(outer, near, run * key_cols)
    mine = lax.dynamic_index_in_dim(runs, lax.axis_index("near"), axis=1, keepdims=False)
    mine = mine.reshape(outer * run, key_cols)
    weight = exchange(jnp.broadcast_to(mine[None], (line,) + mine.shape), "line")
    weight = weight.reshape(owned_cols, key_cols)

    by_owner = tokens.reshape(tok_rows, line, pair, outer, near, run)
    by_owner = by_owner.transpose(4, 2, 0, 1, 3, 5).reshape(plane, tok_rows, owned_cols)
    owned = exchange(by_owner, PLANE)

    share = jnp.einsum("btw,wk->btk", owned, weight, preferred_element_type=jnp.float32)
    shares = exchange(share.astype(jnp.bfloat16), PLANE)
    raw = jnp.sum(shares.astype(jnp.float32), axis=0)

    per_head = raw.reshape(tok_rows, -1, HEAD_DIM)
    inverse = lax.rsqrt(jnp.mean(per_head * per_head, axis=-1, keepdims=True) + epsilon)
    normed = per_head * inverse
    key_out = normed.reshape(tok_rows, key_cols).astype(jnp.bfloat16)
    upstream = cotangent.astype(jnp.float32).reshape(tok_rows, -1, HEAD_DIM)
    projected = jnp.mean(upstream * normed, axis=-1, keepdims=True)
    key_grad = (
        (inverse * (upstream - normed * projected)).reshape(tok_rows, key_cols).astype(jnp.bfloat16)
    )

    grads = exchange(jnp.broadcast_to(key_grad[None], (plane,) + key_grad.shape), PLANE)

    columns = jnp.einsum("btk,wk->btw", grads, weight, preferred_element_type=jnp.float32)
    back = exchange(columns.astype(jnp.bfloat16), PLANE)
    back = back.reshape(near, pair, tok_rows, line, outer, run)
    input_grad = back.transpose(2, 3, 1, 4, 0, 5).reshape(tok_rows, width)

    total = jnp.einsum("btw,btk->wk", owned, grads, preferred_element_type=jnp.float32) * grad_scale
    pieces = exchange(total.astype(jnp.bfloat16).reshape(line, outer * run, key_cols), "line")
    weight_grad = jnp.sum(pieces.astype(jnp.float32), axis=0)
    if outer > 1:
        weight_grad = lax.psum_scatter(weight_grad, "outer", scatter_dimension=0, tiled=True)
    return (key_out, input_grad, weight_grad)


def solution(mesh):
    replicas, group = mesh.shape["dp"], mesh.shape["inner"]
    pair = 2 if group % 2 == 0 else 1
    line = group // pair
    near = math.gcd(replicas, line)
    fine = Mesh(
        mesh.devices.reshape(replicas // near, near, line, pair), ("outer", "near", "line", "pair")
    )
    rows = P(("outer", "near", "line", "pair"), None)
    return jax.shard_map(
        per_device,
        mesh=fine,
        in_specs=(rows, P(("line", "pair"), None), rows),
        out_specs=(rows, rows, P(("line", "pair", "outer", "near"), None)),
        check_vma=False,
    )
```

```python
import math

import jax
import jax.numpy as jnp
from jax import lax
from jax.sharding import Mesh, PartitionSpec as P

HEAD_DIM = 128


epsilon = 1e-06

PLANE = ("pair", "near")


def exchange(blocks, axes):
    return lax.all_to_all(blocks, axes, split_axis=0, concat_axis=0, tiled=True)


def rotated(block, axis, step):
    size = lax.axis_size(axis)
    return lax.ppermute(block, axis, [(i, (i + step) % size) for i in range(size)])


def per_device(tokens, key_weight, cotangent):
    tok_rows, width = tokens.shape
    shard_rows, key_cols = key_weight.shape
    outer, near = lax.axis_size("outer"), lax.axis_size("near")
    line, pair = lax.axis_size("line"), lax.axis_size("pair")
    plane = near * pair
    run = shard_rows // (outer * near)
    owned_cols = width // plane
    grad_scale = 1.0 / math.sqrt(tok_rows * outer * near * line * pair)

    runs = key_weight.reshape(outer, near, run * key_cols)
    mine = lax.dynamic_index_in_dim(runs, lax.axis_index("near"), axis=1, keepdims=False)
    mine = mine.reshape(outer * run, key_cols)
    place = lax.axis_index("line")
    arrived = jnp.stack([mine] + [rotated(mine, "line", step) for step in range(1, line)])
    weight = arrived[(place - jnp.arange(line)) % line].reshape(owned_cols, key_cols)

    by_owner = tokens.reshape(tok_rows, line, pair, outer, near, run)
    by_owner = by_owner.transpose(2, 4, 0, 1, 3, 5).reshape(plane, tok_rows, owned_cols)
    owned = exchange(by_owner, PLANE)

    share = jnp.einsum("btw,wk->btk", owned, weight, preferred_element_type=jnp.float32)
    shares = exchange(share.astype(jnp.bfloat16), PLANE)
    raw = jnp.sum(shares.astype(jnp.float32), axis=0)

    per_head = raw.reshape(tok_rows, -1, HEAD_DIM)
    inverse = lax.rsqrt(jnp.mean(per_head * per_head, axis=-1, keepdims=True) + epsilon)
    normed = per_head * inverse
    key_out = normed.reshape(tok_rows, key_cols).astype(jnp.bfloat16)
    upstream = cotangent.astype(jnp.float32).reshape(tok_rows, -1, HEAD_DIM)
    projected = jnp.mean(upstream * normed, axis=-1, keepdims=True)
    key_grad = (
        (inverse * (upstream - normed * projected)).reshape(tok_rows, key_cols).astype(jnp.bfloat16)
    )

    grads = exchange(jnp.broadcast_to(key_grad[None], (plane,) + key_grad.shape), PLANE)

    columns = jnp.einsum("btk,wk->btw", grads, weight, preferred_element_type=jnp.float32)
    back = exchange(columns.astype(jnp.bfloat16), PLANE)
    back = back.reshape(pair, near, tok_rows, line, outer, run)
    input_grad = back.transpose(2, 3, 0, 4, 1, 5).reshape(tok_rows, width)

    total = jnp.einsum("btw,btk->wk", owned, grads, preferred_element_type=jnp.float32) * grad_scale
    pieces = total.astype(jnp.bfloat16).reshape(line, outer * run, key_cols)
    weight_grad = lax.dynamic_index_in_dim(pieces, place, axis=0, keepdims=False).astype(jnp.float32)
    for step in range(1, line):
        leaving = lax.dynamic_index_in_dim(pieces, (place + step) % line, axis=0, keepdims=False)
        weight_grad += rotated(leaving, "line", step).astype(jnp.float32)
    if outer > 1:
        weight_grad = lax.psum_scatter(weight_grad, "outer", scatter_dimension=0, tiled=True)
    return (key_out, input_grad, weight_grad)


def solution(mesh):
    replicas, group = mesh.shape["dp"], mesh.shape["inner"]
    pair = 2 if group % 2 == 0 else 1
    line = group // pair
    near = math.gcd(replicas, line)
    fine = Mesh(
        mesh.devices.reshape(replicas // near, near, line, pair), ("outer", "near", "line", "pair")
    )
    rows = P(("outer", "near", "line", "pair"), None)
    return jax.shard_map(
        per_device,
        mesh=fine,
        in_specs=(rows, P(("line", "pair"), None), rows),
        out_specs=(rows, rows, P(("line", "pair", "outer", "near"), None)),
        check_vma=False,
    )
```

```python
import functools
import itertools
import math

import jax
import jax.numpy as jnp
from jax import lax
from jax.experimental import pallas as pl
from jax.experimental.pallas import tpu as pltpu
from jax.sharding import Mesh, PartitionSpec as P

HEAD_DIM = 128


epsilon = 1e-06

MEMBERS = ("side", "pair")
bf16, f32 = jnp.bfloat16, jnp.float32


def local_call(body, out_shapes, *args, flops=0):
    vmem = pl.BlockSpec(memory_space=pltpu.VMEM)
    many = isinstance(out_shapes, (list, tuple))
    moved = sum(math.prod(a.shape) * a.dtype.itemsize for a in args)
    return pl.pallas_call(
        body,
        out_shape=out_shapes,
        in_specs=[vmem] * len(args),
        out_specs=[vmem] * len(out_shapes) if many else vmem,
        compiler_params=pltpu.CompilerParams(vmem_limit_bytes=32 << 20),
        cost_estimate=pl.CostEstimate(flops=flops, bytes_accessed=moved, transcendentals=0),
    )(*args)


def rotated(block, axis, step):
    size = lax.axis_size(axis)
    return lax.ppermute(block, axis, [(i, (i + step) % size) for i in range(size)])


def flipped(block, axes, mask):
    size = lax.axis_size(axes)
    return lax.ppermute(block, axes, [(i, i ^ mask) for i in range(size)])


def run_of(part, mask):
    side, twin = lax.axis_size("side"), lax.axis_size("twin")
    line, pair = lax.axis_size("line"), lax.axis_size("pair")
    member = (lax.axis_index("side") * pair + lax.axis_index("pair")) ^ mask
    place = lax.rem(lax.axis_index("line") + line - part // twin, line)
    core = lax.axis_index("twin") ^ (part % twin)
    return (place * pair + lax.rem(member, pair)) * side * twin + member // pair * twin + core


def pack_body(masks, parts, tokens, *blocks):
    run = blocks[0].shape[1] // parts
    for mask, block in zip(masks, blocks):
        for part in range(parts):
            start = pl.multiple_of(run_of(part, mask) * run, run)
            block[:, part * run : (part + 1) * run] = tokens[:, pl.ds(start, run)]


def unpack_body(masks, parts, *refs):
    blocks, whole = refs[:-1], refs[-1]
    run = blocks[0].shape[1] // parts
    for mask, block in zip(masks, blocks):
        for part in range(parts):
            start = pl.multiple_of(run_of(part, mask) * run, run)
            whole[:, pl.ds(start, run)] = block[:, part * run : (part + 1) * run]


def split_runs(tokens, outer):
    tok_rows, width = tokens.shape
    inner = lax.axis_size("line") * lax.axis_size("pair")
    near = lax.axis_size("side") * lax.axis_size("twin")
    cut = tokens.reshape(tok_rows, inner, outer, near, width // (inner * outer * near))
    return cut.transpose(0, 1, 3, 2, 4).reshape(tok_rows, width)


def join_runs(tokens, outer):
    tok_rows, width = tokens.shape
    inner = lax.axis_size("line") * lax.axis_size("pair")
    near = lax.axis_size("side") * lax.axis_size("twin")
    cut = tokens.reshape(tok_rows, inner, near, outer, width // (inner * outer * near))
    return cut.transpose(0, 1, 3, 2, 4).reshape(tok_rows, width)


def join_body(*refs):
    whole = refs[-1]
    rows = refs[0].shape[0]
    for i, ref in enumerate(refs[:-1]):
        whole[i * rows : (i + 1) * rows, :] = ref[...]


def share_body(block, weight, out):
    out[...] = jnp.dot(block[...], weight[...], preferred_element_type=f32).astype(out.dtype)


def columns_body(grad, weight, out):
    out[...] = lax.dot_general(
        grad[...], weight[...], (((1,), (1,)), ((), ())), preferred_element_type=f32
    ).astype(out.dtype)


def norm_body(*refs):
    *shares, cotangent, key_out, key_grad = refs
    for head in range(key_out.shape[1] // HEAD_DIM):
        at = slice(head * HEAD_DIM, (head + 1) * HEAD_DIM)
        raw = sum(share[:, at].astype(f32) for share in shares)
        inverse = lax.rsqrt(jnp.mean(raw * raw, axis=-1, keepdims=True) + epsilon)
        normed = raw * inverse
        upstream = cotangent[:, at].astype(f32)
        projected = jnp.mean(upstream * normed, axis=-1, keepdims=True)
        key_out[:, at] = normed.astype(bf16)
        key_grad[:, at] = (inverse * (upstream - normed * projected)).astype(bf16)


def terms_body(members, twin, grad_scale, *refs):
    blocks, grads, (kept, *leaving) = refs[:members], refs[members : 2 * members], refs[2 * members :]
    tokens = jnp.concatenate([block[...] for block in blocks], axis=0)
    grad = jnp.concatenate([grad[...] for grad in grads], axis=0)
    rows = kept.shape[1]
    total = lax.dot_general(tokens, grad, (((0,), (0,)), ((), ())), preferred_element_type=f32)
    total = total * grad_scale
    for part in range(total.shape[0] // rows):
        piece = total[part * rows : (part + 1) * rows]
        if part % twin == 0:
            kept[part // twin] = piece
        else:
            leaving[0][part // twin] = piece.astype(bf16)


def merge_body(kept, arrived, own, *leaving):
    for step in range(kept.shape[0]):
        piece = kept[step] + arrived[step].astype(f32)
        if step == 0:
            own[...] = piece
        else:
            leaving[step - 1][...] = piece.astype(bf16)


def sum_body(*refs):
    refs[-1][...] = sum(ref[...].astype(f32) for ref in refs[:-1])


def per_device(tokens, key_weight, cotangent):
    tok_rows, width = tokens.shape
    shard_rows, key_cols = key_weight.shape
    outer, side, twin = (lax.axis_size(a) for a in ("outer", "side", "twin"))
    line, pair = lax.axis_size("line"), lax.axis_size("pair")
    members = pair * side
    masks = list(range(members))
    rows = shard_rows // (side * twin)
    parts = line * twin
    owned = width // members
    grad_scale = 1.0 / math.sqrt(tok_rows * outer * side * twin * line * pair)
    shape = jax.ShapeDtypeStruct

    if outer > 1:
        cut = key_weight.reshape(outer, side * twin, rows // outer, key_cols)
        runs = cut.transpose(1, 0, 2, 3).reshape(shard_rows, key_cols)
    else:
        runs = key_weight
    first = lax.axis_index("side") * twin + lax.axis_index("twin")
    mine = lax.dynamic_slice_in_dim(runs, first * rows, rows, axis=0)
    passed = [mine] + [rotated(mine, "line", step) for step in range(1, line)]
    pieces = []
    for step, piece in enumerate(passed):
        pieces.append(piece)
        if twin > 1:
            if step == 0:
                pieces.append(lax.dynamic_slice_in_dim(runs, (first ^ 1) * rows, rows, axis=0))
            else:
                pieces.append(flipped(piece, "twin", 1))

    if outer > 1:
        tokens = split_runs(tokens, outer)
    packed = local_call(
        functools.partial(pack_body, masks, parts), [shape((tok_rows, owned), bf16)] * members, tokens
    )
    blocks = [packed[0]] + [flipped(packed[mask], MEMBERS, mask) for mask in masks[1:]]
    weight = local_call(join_body, shape((owned, key_cols), bf16), *pieces)

    flops = 2 * tok_rows * owned * key_cols
    shares = []
    for mask in masks:
        kind = bf16 if mask else f32
        share = local_call(share_body, shape((tok_rows, key_cols), kind), blocks[mask], weight, flops=flops)
        shares.append(flipped(share, MEMBERS, mask) if mask else share)
    key_out, key_grad = local_call(
        norm_body, [shape((tok_rows, key_cols), bf16)] * 2, *shares, cotangent
    )

    grads = [key_grad] + [flipped(key_grad, MEMBERS, mask) for mask in masks[1:]]
    columns = []
    for mask in masks:
        column = local_call(columns_body, shape((tok_rows, owned), bf16), grads[mask], weight, flops=flops)
        columns.append(flipped(column, MEMBERS, mask) if mask else column)

    terms = local_call(
        functools.partial(terms_body, members, twin, grad_scale),
        [shape((line, rows, key_cols), f32)] + [shape((line, rows, key_cols), bf16)] * (twin - 1),
        *blocks,
        *grads,
        flops=members * flops,
    )
    arrived = flipped(terms[1], "twin", 1) if twin > 1 else jnp.zeros_like(terms[0])
    sums = local_call(
        merge_body,
        [shape((rows, key_cols), f32)] + [shape((rows, key_cols), bf16)] * (line - 1),
        terms[0],
        arrived,
    )
    met = [sums[0]] + [rotated(sums[step], "line", -step) for step in range(1, line)]
    weight_grad = local_call(sum_body, shape((rows, key_cols), f32), *met)
    if outer > 1:
        weight_grad = lax.psum_scatter(weight_grad, "outer", scatter_dimension=0, tiled=True)

    input_grad = local_call(
        functools.partial(unpack_body, masks, parts), shape((tok_rows, width), bf16), *columns
    )
    if outer > 1:
        input_grad = join_runs(input_grad, outer)
    return (key_out, input_grad, weight_grad)


def halves(size):
    return 2 if size % 2 == 0 else 1


def solution(mesh):
    replicas, group = mesh.shape["dp"], mesh.shape["inner"]
    twin, pair = halves(replicas), halves(group)
    side = halves(replicas // twin)
    fine = Mesh(
        mesh.devices.reshape(replicas // (side * twin), side, twin, group // pair, pair),
        ("outer", "side", "twin", "line", "pair"),
    )
    rows = P(("outer", "side", "twin", "line", "pair"), None)
    return jax.shard_map(
        per_device,
        mesh=fine,
        in_specs=(rows, P(("line", "pair"), None), rows),
        out_specs=(rows, rows, P(("line", "pair", "outer", "side", "twin"), None)),
        check_vma=False,
    )
```

```python
import functools
import math

import jax
import jax.numpy as jnp
from jax import lax
from jax.experimental import pallas as pl
from jax.experimental.pallas import tpu as pltpu
from jax.sharding import Mesh, PartitionSpec as P

HEAD_DIM = 128


epsilon = 1e-06

MEMBERS = ("side", "pair")
TWIN = 2
bf16, f32 = jnp.bfloat16, jnp.float32


def local_call(body, out_shapes, *args, flops=0):
    vmem = pl.BlockSpec(memory_space=pltpu.VMEM)
    many = isinstance(out_shapes, (list, tuple))
    moved = sum(math.prod(a.shape) * a.dtype.itemsize for a in args)
    return pl.pallas_call(
        body,
        out_shape=out_shapes,
        in_specs=[vmem] * len(args),
        out_specs=[vmem] * len(out_shapes) if many else vmem,
        compiler_params=pltpu.CompilerParams(vmem_limit_bytes=32 << 20),
        cost_estimate=pl.CostEstimate(flops=flops, bytes_accessed=moved, transcendentals=0),
    )(*args)


def rotated(block, axis, step):
    size = lax.axis_size(axis)
    return lax.ppermute(block, axis, [(i, (i + step) % size) for i in range(size)])


def flipped(block, axes, mask):
    size = lax.axis_size(axes)
    return lax.ppermute(block, axes, [(i, i ^ mask) for i in range(size)])


def run_of(part, mask):
    side, line, pair = lax.axis_size("side"), lax.axis_size("line"), lax.axis_size("pair")
    member = (lax.axis_index("side") * pair + lax.axis_index("pair")) ^ mask
    place = lax.rem(lax.axis_index("line") + line - part // TWIN, line)
    core = lax.axis_index("twin") ^ (part % TWIN)
    return (place * pair + lax.rem(member, pair)) * side * TWIN + member // pair * TWIN + core


def pack(mask, tokens, block):
    parts = lax.axis_size("line") * TWIN
    run = block.shape[1] // parts
    for part in range(parts):
        start = pl.multiple_of(run_of(part, mask) * run, run)
        block[:, part * run : (part + 1) * run] = tokens[:, pl.ds(start, run)]


def first_body(mask, tokens, shard, both, block):
    rows = both.shape[0]
    both[...] = shard[pl.ds(pl.multiple_of(lax.axis_index("side") * rows, rows), rows), :]
    pack(mask, tokens, block)


def second_body(masks, tokens, both, _, mine, *blocks):
    rows = mine.shape[0]
    mine[...] = both[pl.ds(pl.multiple_of(lax.axis_index("twin") * rows, rows), rows), :]
    for mask, block in zip(masks, blocks):
        pack(mask, tokens, block)


def unpack_body(masks, *refs):
    blocks, whole = refs[:-1], refs[-1]
    parts = lax.axis_size("line") * TWIN
    run = blocks[0].shape[1] // parts
    for mask, block in zip(masks, blocks):
        for part in range(parts):
            start = pl.multiple_of(run_of(part, mask) * run, run)
            whole[:, pl.ds(start, run)] = block[:, part * run : (part + 1) * run]


def split_runs(tokens, outer):
    tok_rows, width = tokens.shape
    inner = lax.axis_size("line") * lax.axis_size("pair")
    near = lax.axis_size("side") * TWIN
    cut = tokens.reshape(tok_rows, inner, outer, near, width // (inner * outer * near))
    return cut.transpose(0, 1, 3, 2, 4).reshape(tok_rows, width)


def join_runs(tokens, outer):
    tok_rows, width = tokens.shape
    inner = lax.axis_size("line") * lax.axis_size("pair")
    near = lax.axis_size("side") * TWIN
    cut = tokens.reshape(tok_rows, inner, near, outer, width // (inner * outer * near))
    return cut.transpose(0, 1, 3, 2, 4).reshape(tok_rows, width)


def parted(block, step):
    line = lax.axis_size("line")
    to = [core * line + (i + (line - step if core else step)) % line for core in range(TWIN) for i in range(line)]
    return lax.ppermute(block, ("twin", "line"), list(enumerate(to)))


def join_body(line, *refs):
    *pieces, whole = refs
    rows = whole.shape[0] // (line * TWIN)
    core = lax.axis_index("twin")

    def put(step, twin_run, piece):
        part = step * TWIN + (twin_run ^ core)
        whole[pl.ds(pl.multiple_of(part * rows, rows), rows), :] = piece

    def put_both(step, piece):
        for twin_run in range(TWIN):
            put(step, twin_run, piece[twin_run * rows : (twin_run + 1) * rows, :])

    pieces = iter(pieces)
    put_both(0, next(pieces))
    for step in range(1, (line + 1) // 2):
        put_both(jnp.where(core == 0, step, line - step), next(pieces))
        put_both(jnp.where(core == 0, line - step, step), next(pieces))
    if line % 2 == 0:
        put(line // 2, core, next(pieces)[...])
        put(line // 2, 1 - core, next(pieces)[...])


def share_body(block, weight, out):
    out[...] = jnp.dot(block[...], weight[...], preferred_element_type=f32).astype(out.dtype)


def columns_body(grad, weight, out):
    out[...] = lax.dot_general(
        grad[...], weight[...], (((1,), (1,)), ((), ())), preferred_element_type=f32
    ).astype(out.dtype)


def norm_body(*refs):
    *shares, cotangent, key_out, key_grad = refs
    for head in range(key_out.shape[1] // HEAD_DIM):
        at = slice(head * HEAD_DIM, (head + 1) * HEAD_DIM)
        raw = sum(share[:, at].astype(f32) for share in shares)
        inverse = lax.rsqrt(jnp.mean(raw * raw, axis=-1, keepdims=True) + epsilon)
        normed = raw * inverse
        upstream = cotangent[:, at].astype(f32)
        projected = jnp.mean(upstream * normed, axis=-1, keepdims=True)
        key_out[:, at] = normed.astype(bf16)
        key_grad[:, at] = (inverse * (upstream - normed * projected)).astype(bf16)


def terms_body(members, grad_scale, *refs):
    blocks, grads, (kept, leaving) = refs[:members], refs[members : 2 * members], refs[2 * members :]
    tokens = jnp.concatenate([block[...] for block in blocks], axis=0)
    grad = jnp.concatenate([grad[...] for grad in grads], axis=0)
    rows = kept.shape[1]
    total = lax.dot_general(tokens, grad, (((0,), (0,)), ((), ())), preferred_element_type=f32)
    total = total * grad_scale
    for part in range(total.shape[0] // rows):
        piece = total[part * rows : (part + 1) * rows]
        if part % TWIN == 0:
            kept[part // TWIN] = piece
        else:
            leaving[part // TWIN] = piece.astype(bf16)


def merge_body(kept, arrived, own, *leaving):
    for step in range(kept.shape[0]):
        piece = kept[step] + arrived[step].astype(f32)
        if step == 0:
            own[...] = piece
        else:
            leaving[step - 1][...] = piece.astype(bf16)


def sum_body(*refs):
    refs[-1][...] = sum(ref[...].astype(f32) for ref in refs[:-1])


def per_device(tokens, key_weight, cotangent):
    tok_rows, width = tokens.shape
    shard_rows, key_cols = key_weight.shape
    outer, side = lax.axis_size("outer"), lax.axis_size("side")
    line, pair = lax.axis_size("line"), lax.axis_size("pair")
    members = pair * side
    masks = list(range(members))
    rows = shard_rows // (side * TWIN)
    owned = width // members
    grad_scale = 1.0 / math.sqrt(tok_rows * outer * side * TWIN * line * pair)
    shape = jax.ShapeDtypeStruct
    block_shape = shape((tok_rows, owned), bf16)
    if outer > 1:
        cut = key_weight.reshape(outer, side * TWIN, rows // outer, key_cols)
        key_weight = cut.transpose(1, 0, 2, 3).reshape(shard_rows, key_cols)
        tokens = split_runs(tokens, outer)

    both, *far = local_call(
        functools.partial(first_body, masks[-1]),
        [shape((TWIN * rows, key_cols), bf16), block_shape],
        tokens,
        key_weight,
    )
    mine, *packed = local_call(
        functools.partial(second_body, masks[:-1]),
        [shape((rows, key_cols), bf16)] + [block_shape] * (members - 1),
        tokens,
        both,
        *far,
    )
    packed += far
    blocks = [packed[0]] + [flipped(packed[mask], MEMBERS, mask) for mask in masks[1:]]
    passed = [parted(both, step) for step in range(1, (line + 1) // 2)]
    if line % 2 == 0:
        passed.append(rotated(mine, "line", line // 2))
    pieces = [both]
    *passed, blocks = lax.optimization_barrier((*passed, blocks))
    for piece in passed:
        pieces += [piece, flipped(piece, "twin", 1)]
    weight = local_call(
        functools.partial(join_body, line), shape((owned, key_cols), bf16), *pieces
    )

    flops = 2 * tok_rows * owned * key_cols
    shares = []
    for mask in masks:
        kind = bf16 if mask else f32
        share = local_call(share_body, shape((tok_rows, key_cols), kind), blocks[mask], weight, flops=flops)
        shares.append(flipped(share, MEMBERS, mask) if mask else share)
    key_out, key_grad = local_call(
        norm_body, [shape((tok_rows, key_cols), bf16)] * 2, *shares, cotangent
    )

    grads = [key_grad] + [flipped(key_grad, MEMBERS, mask) for mask in masks[1:]]
    columns = []
    for mask in masks:
        column = local_call(columns_body, shape((tok_rows, owned), bf16), grads[mask], weight, flops=flops)
        columns.append(flipped(column, MEMBERS, mask) if mask else column)

    terms = local_call(
        functools.partial(terms_body, members, grad_scale),
        [shape((line, rows, key_cols), kind) for kind in (f32, bf16)],
        *blocks,
        *grads,
        flops=members * flops,
    )
    sums = local_call(
        merge_body,
        [shape((rows, key_cols), f32)] + [shape((rows, key_cols), bf16)] * (line - 1),
        terms[0],
        flipped(terms[1], "twin", 1),
    )
    met = [sums[0]] + [rotated(sums[step], "line", -step) for step in range(1, line)]
    weight_grad = local_call(sum_body, shape((rows, key_cols), f32), *met)
    if outer > 1:
        weight_grad = lax.psum_scatter(weight_grad, "outer", scatter_dimension=0, tiled=True)

    input_grad = local_call(
        functools.partial(unpack_body, masks), shape((tok_rows, width), bf16), *columns
    )
    if outer > 1:
        input_grad = join_runs(input_grad, outer)
    return (key_out, input_grad, weight_grad)


def solution(mesh):
    replicas, group = mesh.shape["dp"], mesh.shape["inner"]
    near = math.gcd(replicas, 2 * TWIN)
    pair = math.gcd(group, 2)
    fine = Mesh(
        mesh.devices.reshape(replicas // near, near // TWIN, TWIN, group // pair, pair),
        ("outer", "side", "twin", "line", "pair"),
    )
    rows = P(("outer", "side", "twin", "line", "pair"), None)
    return jax.shard_map(
        per_device,
        mesh=fine,
        in_specs=(rows, P(("line", "pair"), None), rows),
        out_specs=(rows, rows, P(("line", "pair", "outer", "side", "twin"), None)),
        check_vma=False,
    )
```

```python
import functools
import math

import jax
import jax.numpy as jnp
from jax import lax
from jax.experimental import pallas as pl
from jax.experimental.pallas import tpu as pltpu
from jax.sharding import Mesh, PartitionSpec as P

HEAD_DIM = 128


epsilon = 1e-06

MEMBERS = ("side", "pair")
TWIN = 2
bf16, f32 = jnp.bfloat16, jnp.float32


def local_call(body, out_shapes, *args, flops=0, space=pltpu.VMEM, scratch=(), room=32):
    vmem = pl.BlockSpec(memory_space=pltpu.VMEM)
    many = isinstance(out_shapes, (list, tuple))
    moved = sum(math.prod(a.shape) * a.dtype.itemsize for a in args)
    return pl.pallas_call(
        body,
        out_shape=out_shapes,
        in_specs=[pl.BlockSpec(memory_space=space)] * len(args),
        out_specs=[vmem] * len(out_shapes) if many else vmem,
        scratch_shapes=scratch,
        compiler_params=pltpu.CompilerParams(vmem_limit_bytes=room << 20),
        cost_estimate=pl.CostEstimate(flops=flops, bytes_accessed=moved, transcendentals=0),
    )(*args)


def rotated(block, axis, step):
    size = lax.axis_size(axis)
    return lax.ppermute(block, axis, [(i, (i + step) % size) for i in range(size)])


def flipped(block, axes, mask):
    size = lax.axis_size(axes)
    return lax.ppermute(block, axes, [(i, i ^ mask) for i in range(size)])


def run_of(part, mask):
    side, line, pair = lax.axis_size("side"), lax.axis_size("line"), lax.axis_size("pair")
    member = (lax.axis_index("side") * pair + lax.axis_index("pair")) ^ mask
    place = lax.rem(lax.axis_index("line") + line - part // TWIN, line)
    core = lax.axis_index("twin") ^ (part % TWIN)
    return (place * pair + lax.rem(member, pair)) * side * TWIN + member // pair * TWIN + core


def pack(mask, tokens, block):
    parts = lax.axis_size("line") * TWIN
    run = block.shape[1] // parts
    for part in range(parts):
        start = pl.multiple_of(run_of(part, mask) * run, run)
        block[:, part * run : (part + 1) * run] = tokens[:, pl.ds(start, run)]


def front_body(masks, tokens_hbm, shard, both, mine, *refs):
    *blocks, tokens, arrived = refs
    copies = [pltpu.make_async_copy(tokens_hbm, tokens, arrived.at[0])]
    rows, half = mine.shape[0], both.shape[0]
    first = lax.axis_index("side") * half
    for i, (target, start) in enumerate(((both, first), (mine, first + lax.axis_index("twin") * rows))):
        source = shard.at[pl.ds(pl.multiple_of(start, rows), target.shape[0])]
        copies.append(pltpu.make_async_copy(source, target, arrived.at[1 + i]))
    for copy in copies:
        copy.start()
    copies[0].wait()
    for mask, block in zip(masks, blocks):
        pack(mask, tokens, block)
    for copy in copies[1:]:
        copy.wait()


def unpack_body(masks, *refs):
    blocks, whole = refs[:-1], refs[-1]
    parts = lax.axis_size("line") * TWIN
    run = blocks[0].shape[1] // parts
    for mask, block in zip(masks, blocks):
        for part in range(parts):
            start = pl.multiple_of(run_of(part, mask) * run, run)
            whole[:, pl.ds(start, run)] = block[:, part * run : (part + 1) * run]


def split_runs(tokens, outer):
    tok_rows, width = tokens.shape
    inner = lax.axis_size("line") * lax.axis_size("pair")
    near = lax.axis_size("side") * TWIN
    cut = tokens.reshape(tok_rows, inner, outer, near, width // (inner * outer * near))
    return cut.transpose(0, 1, 3, 2, 4).reshape(tok_rows, width)


def join_runs(tokens, outer):
    tok_rows, width = tokens.shape
    inner = lax.axis_size("line") * lax.axis_size("pair")
    near = lax.axis_size("side") * TWIN
    cut = tokens.reshape(tok_rows, inner, near, outer, width // (inner * outer * near))
    return cut.transpose(0, 1, 3, 2, 4).reshape(tok_rows, width)


def parted(block, step):
    line = lax.axis_size("line")
    to = [core * line + (i + (line - step if core else step)) % line for core in range(TWIN) for i in range(line)]
    return lax.ppermute(block, ("twin", "line"), list(enumerate(to)))


def join_body(line, *refs):
    *pieces, whole = refs
    rows = whole.shape[0] // (line * TWIN)
    core = lax.axis_index("twin")

    def put(step, twin_run, piece):
        part = step * TWIN + (twin_run ^ core)
        whole[pl.ds(pl.multiple_of(part * rows, rows), rows), :] = piece

    def put_both(step, piece):
        for twin_run in range(TWIN):
            put(step, twin_run, piece[twin_run * rows : (twin_run + 1) * rows, :])

    pieces = iter(pieces)
    put_both(0, next(pieces))
    for step in range(1, (line + 1) // 2):
        put_both(jnp.where(core == 0, step, line - step), next(pieces))
        put_both(jnp.where(core == 0, line - step, step), next(pieces))
    if line % 2 == 0:
        put(line // 2, core, next(pieces)[...])
        put(line // 2, 1 - core, next(pieces)[...])


def share_body(block, weight, out):
    out[...] = jnp.dot(block[...], weight[...], preferred_element_type=f32).astype(out.dtype)


def columns_body(grad, weight, out):
    out[...] = lax.dot_general(
        grad[...], weight[...], (((1,), (1,)), ((), ())), preferred_element_type=f32
    ).astype(out.dtype)


def norm_body(*refs):
    *shares, cotangent, key_out, key_grad = refs
    for head in range(key_out.shape[1] // HEAD_DIM):
        at = slice(head * HEAD_DIM, (head + 1) * HEAD_DIM)
        raw = sum(share[:, at].astype(f32) for share in shares)
        inverse = lax.rsqrt(jnp.mean(raw * raw, axis=-1, keepdims=True) + epsilon)
        normed = raw * inverse
        upstream = cotangent[:, at].astype(f32)
        projected = jnp.mean(upstream * normed, axis=-1, keepdims=True)
        key_out[:, at] = normed.astype(bf16)
        key_grad[:, at] = (inverse * (upstream - normed * projected)).astype(bf16)


def terms_body(members, grad_scale, *refs):
    blocks, grads, (kept, leaving) = refs[:members], refs[members : 2 * members], refs[2 * members :]
    tokens = jnp.concatenate([block[...] for block in blocks], axis=0)
    grad = jnp.concatenate([grad[...] for grad in grads], axis=0)
    rows = kept.shape[1]
    total = lax.dot_general(tokens, grad, (((0,), (0,)), ((), ())), preferred_element_type=f32)
    total = total * grad_scale
    for part in range(total.shape[0] // rows):
        piece = total[part * rows : (part + 1) * rows]
        if part % TWIN == 0:
            kept[part // TWIN] = piece
        else:
            leaving[part // TWIN] = piece.astype(bf16)


def merge_body(kept, arrived, own, *leaving):
    for step in range(kept.shape[0]):
        piece = kept[step] + arrived[step].astype(f32)
        if step == 0:
            own[...] = piece
        else:
            leaving[step - 1][...] = piece.astype(bf16)


def sum_body(*refs):
    refs[-1][...] = sum(ref[...].astype(f32) for ref in refs[:-1])


def per_device(tokens, key_weight, cotangent):
    tok_rows, width = tokens.shape
    shard_rows, key_cols = key_weight.shape
    outer, side = lax.axis_size("outer"), lax.axis_size("side")
    line, pair = lax.axis_size("line"), lax.axis_size("pair")
    members = pair * side
    masks = list(range(members))
    rows = shard_rows // (side * TWIN)
    owned = width // members
    grad_scale = 1.0 / math.sqrt(tok_rows * outer * side * TWIN * line * pair)
    shape = jax.ShapeDtypeStruct
    block_shape = shape((tok_rows, owned), bf16)
    if outer > 1:
        cut = key_weight.reshape(outer, side * TWIN, rows // outer, key_cols)
        key_weight = cut.transpose(1, 0, 2, 3).reshape(shard_rows, key_cols)
        tokens = split_runs(tokens, outer)

    both, mine, *packed = local_call(
        functools.partial(front_body, masks),
        [shape((TWIN * rows, key_cols), bf16), shape((rows, key_cols), bf16)] + [block_shape] * members,
        tokens,
        key_weight,
        space=pltpu.HBM,
        room=53,
        scratch=[pltpu.VMEM(tokens.shape, bf16), pltpu.SemaphoreType.DMA((3,))],
    )
    blocks = [packed[0]] + [flipped(packed[mask], MEMBERS, mask) for mask in masks[1:]]
    passed = [parted(both, step) for step in range(1, (line + 1) // 2)]
    if line % 2 == 0:
        passed.append(rotated(mine, "line", line // 2))
    pieces = [both]
    *passed, blocks = lax.optimization_barrier((*passed, blocks))
    for piece in passed:
        pieces += [piece, flipped(piece, "twin", 1)]
    weight = local_call(
        functools.partial(join_body, line), shape((owned, key_cols), bf16), *pieces
    )

    flops = 2 * tok_rows * owned * key_cols
    shares = []
    for mask in reversed(masks):
        kind = bf16 if mask else f32
        share = local_call(share_body, shape((tok_rows, key_cols), kind), blocks[mask], weight, flops=flops)
        shares.append(flipped(share, MEMBERS, mask) if mask else share)
    key_out, key_grad = local_call(
        norm_body, [shape((tok_rows, key_cols), bf16)] * 2, *shares, cotangent
    )

    grads = [key_grad] + [flipped(key_grad, MEMBERS, mask) for mask in masks[1:]]
    columns = [
        local_call(columns_body, block_shape, grad, weight, flops=flops) for grad in grads[:-1]
    ]
    columns, grads[-1] = lax.optimization_barrier((columns, grads[-1]))
    terms = local_call(
        functools.partial(terms_body, members, grad_scale),
        [shape((line, rows, key_cols), kind) for kind in (f32, bf16)],
        *blocks,
        *grads,
        flops=members * flops,
    )
    columns = columns[:1] + [flipped(columns[mask], MEMBERS, mask) for mask in masks[1:-1]]
    sums = local_call(
        merge_body,
        [shape((rows, key_cols), f32)] + [shape((rows, key_cols), bf16)] * (line - 1),
        terms[0],
        flipped(terms[1], "twin", 1),
    )

    met = [sums[0]] + [rotated(sums[step], "line", -step) for step in range(1, line)]
    column = local_call(columns_body, block_shape, grads[-1], weight, flops=flops)
    column, columns, _ = lax.optimization_barrier((column, columns, sums))
    columns.append(flipped(column, MEMBERS, masks[-1]) if len(masks) > 1 else column)
    weight_grad = local_call(sum_body, shape((rows, key_cols), f32), *met, flops=32 * flops)
    columns, weight_grad = lax.optimization_barrier((columns, weight_grad))
    if outer > 1:
        weight_grad = lax.psum_scatter(weight_grad, "outer", scatter_dimension=0, tiled=True)
    input_grad = local_call(
        functools.partial(unpack_body, masks), shape((tok_rows, width), bf16), *columns
    )
    if outer > 1:
        input_grad = join_runs(input_grad, outer)
    return (key_out, input_grad, weight_grad)


def solution(mesh):
    replicas, group = mesh.shape["dp"], mesh.shape["inner"]
    near = math.gcd(replicas, 2 * TWIN)
    pair = math.gcd(group, 2)
    fine = Mesh(
        mesh.devices.reshape(replicas // near, near // TWIN, TWIN, group // pair, pair),
        ("outer", "side", "twin", "line", "pair"),
    )
    rows = P(("outer", "side", "twin", "line", "pair"), None)
    return jax.shard_map(
        per_device,
        mesh=fine,
        in_specs=(rows, P(("line", "pair"), None), rows),
        out_specs=(rows, rows, P(("line", "pair", "outer", "side", "twin"), None)),
        check_vma=False,
    )
```

```python
import functools
import math

import jax
import jax.numpy as jnp
from jax import lax
from jax.experimental import pallas as pl
from jax.experimental.pallas import tpu as pltpu
from jax.sharding import Mesh, PartitionSpec as P

HEAD_DIM = 128


epsilon = 1e-06

MEMBERS = ("side", "pair")
TWIN = 2
bf16, f32 = jnp.bfloat16, jnp.float32


def local_call(name, body, out_shapes, *args, flops=0, space=pltpu.VMEM, scratch=(), room=32, moved=None):
    vmem = pl.BlockSpec(memory_space=pltpu.VMEM)
    many = isinstance(out_shapes, (list, tuple))
    if moved is None:
        moved = sum(math.prod(a.shape) * a.dtype.itemsize for a in args)
    return pl.pallas_call(
        body,
        name=name,
        out_shape=out_shapes,
        in_specs=[pl.BlockSpec(memory_space=space)] * len(args),
        out_specs=[vmem] * len(out_shapes) if many else vmem,
        scratch_shapes=scratch,
        compiler_params=pltpu.CompilerParams(vmem_limit_bytes=room << 20),
        cost_estimate=pl.CostEstimate(flops=flops, bytes_accessed=moved, transcendentals=0),
    )(*args)


def rotated(block, axis, step):
    size = lax.axis_size(axis)
    return lax.ppermute(block, axis, [(i, (i + step) % size) for i in range(size)])


def flipped(block, axes, mask):
    size = lax.axis_size(axes)
    return lax.ppermute(block, axes, [(i, i ^ mask) for i in range(size)])


def run_of(part, mask):
    side, line, pair = lax.axis_size("side"), lax.axis_size("line"), lax.axis_size("pair")
    member = (lax.axis_index("side") * pair + lax.axis_index("pair")) ^ mask
    place = lax.rem(lax.axis_index("line") + line - part // TWIN, line)
    core = lax.axis_index("twin") ^ (part % TWIN)
    return (place * pair + lax.rem(member, pair)) * side * TWIN + member // pair * TWIN + core


def front_body(masks, tokens, shard, both, mine, *refs):
    *blocks, arrived = refs
    rows, half = mine.shape[0], both.shape[0]
    first = lax.axis_index("side") * half
    moves = []
    for target, start in ((both, first), (mine, first + lax.axis_index("twin") * rows)):
        moves.append((shard.at[pl.ds(pl.multiple_of(start, rows), target.shape[0])], target))
    parts = lax.axis_size("line") * TWIN
    run = blocks[0].shape[1] // parts
    for mask, block in zip(masks, blocks):
        for part in range(parts):
            start = pl.multiple_of(run_of(part, mask) * run, run)
            moves.append((tokens.at[:, pl.ds(start, run)], block.at[:, pl.ds(part * run, run)]))
    copies = [pltpu.make_async_copy(*move, arrived.at[i]) for i, move in enumerate(moves)]
    for copy in copies:
        copy.start()
    for copy in copies:
        copy.wait()


def unpack_body(masks, *refs):
    blocks, whole = refs[:-1], refs[-1]
    parts = lax.axis_size("line") * TWIN
    run = blocks[0].shape[1] // parts
    for mask, block in zip(masks, blocks):
        for part in range(parts):
            start = pl.multiple_of(run_of(part, mask) * run, run)
            whole[:, pl.ds(start, run)] = block[:, part * run : (part + 1) * run]


def split_runs(tokens, outer):
    tok_rows, width = tokens.shape
    inner = lax.axis_size("line") * lax.axis_size("pair")
    near = lax.axis_size("side") * TWIN
    cut = tokens.reshape(tok_rows, inner, outer, near, width // (inner * outer * near))
    return cut.transpose(0, 1, 3, 2, 4).reshape(tok_rows, width)


def join_runs(tokens, outer):
    tok_rows, width = tokens.shape
    inner = lax.axis_size("line") * lax.axis_size("pair")
    near = lax.axis_size("side") * TWIN
    cut = tokens.reshape(tok_rows, inner, near, outer, width // (inner * outer * near))
    return cut.transpose(0, 1, 3, 2, 4).reshape(tok_rows, width)


def parted(block, step):
    line = lax.axis_size("line")
    to = [core * line + (i + (line - step if core else step)) % line for core in range(TWIN) for i in range(line)]
    return lax.ppermute(block, ("twin", "line"), list(enumerate(to)))


def cuts(rows, count):
    unit = math.gcd(rows, 64)
    ends = [-(-rows // unit * i // count) * unit for i in range(count + 1)]
    return list(zip(ends, ends[1:]))


def relay_body(count, *refs):
    rows = jnp.concatenate([ref[...] for ref in refs[:-count]], axis=0)
    for (start, end), out in zip(cuts(rows.shape[0], count), refs[-count:]):
        out[...] = rows[start:end]


def join_body(line, count, *refs):
    both, *pieces, whole = refs
    others = jnp.concatenate([piece[...] for piece in pieces[-count:]], axis=0)
    pieces = pieces[:-count]
    rows = whole.shape[0] // (line * TWIN)
    core = lax.axis_index("twin")

    def put(step, twin_run, piece):
        part = step * TWIN + (twin_run ^ core)
        whole[pl.ds(pl.multiple_of(part * rows, rows), rows), :] = piece

    def put_both(step, piece):
        for twin_run in range(TWIN):
            put(step, twin_run, piece[twin_run * rows : (twin_run + 1) * rows])

    put_both(0, both[...])
    for step in range(1, (line + 1) // 2):
        at = (step - 1) * TWIN * rows
        put_both(jnp.where(core == 0, step, line - step), pieces[step - 1][...])
        put_both(jnp.where(core == 0, line - step, step), others[at : at + TWIN * rows])
    if line % 2 == 0:
        put(line // 2, core, pieces[-1][...])
        put(line // 2, 1 - core, others[others.shape[0] - rows :])


def share_body(block, weight, out):
    out[...] = jnp.dot(block[...], weight[...], preferred_element_type=f32).astype(out.dtype)


def columns_body(grad, weight, out):
    out[...] = lax.dot_general(
        grad[...], weight[...], (((1,), (1,)), ((), ())), preferred_element_type=f32
    ).astype(out.dtype)


def norm_body(*refs):
    *shares, cotangent, key_out, key_grad = refs
    for head in range(key_out.shape[1] // HEAD_DIM):
        at = slice(head * HEAD_DIM, (head + 1) * HEAD_DIM)
        raw = sum(share[:, at].astype(f32) for share in shares)
        inverse = lax.rsqrt(jnp.mean(raw * raw, axis=-1, keepdims=True) + epsilon)
        normed = raw * inverse
        upstream = cotangent[:, at].astype(f32)
        projected = jnp.mean(upstream * normed, axis=-1, keepdims=True)
        key_out[:, at] = normed.astype(bf16)
        key_grad[:, at] = (inverse * (upstream - normed * projected)).astype(bf16)


def terms_body(members, grad_scale, *refs):
    blocks, grads, (kept, *leaving) = refs[:members], refs[members : 2 * members], refs[2 * members :]
    tokens = jnp.concatenate([block[...] for block in blocks], axis=0)
    grad = jnp.concatenate([grad[...] for grad in grads], axis=0)
    line, rows, _ = kept.shape
    total = lax.dot_general(tokens, grad, (((0,), (0,)), ((), ())), preferred_element_type=f32)
    total = total * grad_scale
    others = []
    for step in range(line):
        start = step * TWIN * rows
        kept[step] = total[start : start + rows]
        others.append(total[start + rows : start + TWIN * rows].astype(bf16))
    others = jnp.concatenate(others, axis=0)
    for (start, end), piece in zip(cuts(line * rows, len(leaving)), leaving):
        piece[...] = others[start:end]


def merge_body(count, kept, *refs):
    others = jnp.concatenate([piece[...] for piece in refs[:count]], axis=0)
    own, *leaving = refs[count:]
    rows = own.shape[0]
    for step in range(kept.shape[0]):
        piece = kept[step] + others[step * rows : (step + 1) * rows].astype(f32)
        if step == 0:
            own[...] = piece
        else:
            leaving[step - 1][...] = piece.astype(bf16)


def sum_body(*refs):
    refs[-1][...] = sum(ref[...].astype(f32) for ref in refs[:-1])


def per_device(tokens, key_weight, cotangent):
    tok_rows, width = tokens.shape
    shard_rows, key_cols = key_weight.shape
    outer, side = lax.axis_size("outer"), lax.axis_size("side")
    line, pair = lax.axis_size("line"), lax.axis_size("pair")
    members = pair * side
    masks = list(range(members))
    rows = shard_rows // (side * TWIN)
    owned = width // members
    grad_scale = 1.0 / math.sqrt(tok_rows * outer * side * TWIN * line * pair)
    shape = jax.ShapeDtypeStruct
    parts = line * TWIN
    flops = 2 * tok_rows * owned * key_cols
    block_shape = shape((tok_rows, owned), bf16)
    if outer > 1:
        cut = key_weight.reshape(outer, side * TWIN, rows // outer, key_cols)
        key_weight = cut.transpose(1, 0, 2, 3).reshape(shard_rows, key_cols)
        tokens = split_runs(tokens, outer)

    both, mine, *packed = local_call(
        "front",
        functools.partial(front_body, masks),
        [shape((TWIN * rows, key_cols), bf16), shape((rows, key_cols), bf16)] + [block_shape] * members,
        tokens,
        key_weight,
        space=pltpu.HBM,
        room=53,
        scratch=[pltpu.SemaphoreType.DMA((2 + members * parts,))],
    )
    blocks = [packed[0]] + [flipped(packed[mask], MEMBERS, mask) for mask in masks[1:]]
    passed = [parted(both, step) for step in range(1, (line + 1) // 2)]
    if line % 2 == 0:
        passed.append(rotated(mine, "line", line // 2))
    pieces = [both]
    reach = shard_rows // side * (line - 1) // TWIN
    relayed = local_call(
        "relay",
        functools.partial(relay_body, 2),
        [shape((end - start, key_cols), bf16) for start, end in cuts(reach, 2)],
        *passed,
        flops=8 * flops,
    )
    weight = local_call(
        "join",
        functools.partial(join_body, line, 2),
        shape((owned, key_cols), bf16),
        both,
        *passed,
        *[flipped(piece, "twin", 1) for piece in relayed],
    )

    shares = []
    for mask in masks:
        kind = bf16 if mask else f32
        share = local_call("share", share_body, shape((tok_rows, key_cols), kind), blocks[mask], weight, flops=flops)
        shares.append(flipped(share, MEMBERS, mask) if mask else share)
    key_out, key_grad = local_call(
        "norm", norm_body, [shape((tok_rows, key_cols), bf16)] * 2, *shares, cotangent
    )

    grads = [key_grad] + [flipped(key_grad, MEMBERS, mask) for mask in masks[1:]]
    columns = [
        local_call("columns", columns_body, block_shape, grad, weight, flops=flops) for grad in grads[:-1]
    ]
    columns, grads[-1] = lax.optimization_barrier((columns, grads[-1]))
    terms = local_call(
        "terms",
        functools.partial(terms_body, members, grad_scale),
        [shape((line, rows, key_cols), f32)]
        + [shape((end - start, key_cols), bf16) for start, end in cuts(line * rows, 3)],
        *blocks,
        *grads,
        flops=members * flops,
    )
    columns = columns[:1] + [flipped(columns[mask], MEMBERS, mask) for mask in masks[1:-1]]
    sums = local_call(
        "merge",
        functools.partial(merge_body, 3),
        [shape((rows, key_cols), f32)] + [shape((rows, key_cols), bf16)] * (line - 1),
        terms[0],
        *[flipped(piece, "twin", 1) for piece in terms[1:]],
        moved=0,
    )

    met = [sums[0]] + [rotated(sums[step], "line", -step) for step in range(1, line)]
    column = local_call("columns", columns_body, block_shape, grads[-1], weight, flops=flops)
    column, columns, _ = lax.optimization_barrier((column, columns, sums))
    columns.append(flipped(column, MEMBERS, masks[-1]) if len(masks) > 1 else column)
    weight_grad = local_call("final_sum", sum_body, shape((rows, key_cols), f32), *met, flops=32 * flops)
    columns, weight_grad = lax.optimization_barrier((columns, weight_grad))
    if outer > 1:
        weight_grad = lax.psum_scatter(weight_grad, "outer", scatter_dimension=0, tiled=True)
    input_grad = local_call(
        "unpack",
        functools.partial(unpack_body, masks), shape((tok_rows, width), bf16), *columns
    )
    if outer > 1:
        input_grad = join_runs(input_grad, outer)
    return (key_out, input_grad, weight_grad)


def solution(mesh):
    replicas, group = mesh.shape["dp"], mesh.shape["inner"]
    near = math.gcd(replicas, 2 * TWIN)
    pair = math.gcd(group, 2)
    fine = Mesh(
        mesh.devices.reshape(replicas // near, near // TWIN, TWIN, group // pair, pair),
        ("outer", "side", "twin", "line", "pair"),
    )
    rows = P(("outer", "side", "twin", "line", "pair"), None)
    return jax.shard_map(
        per_device,
        mesh=fine,
        in_specs=(rows, P(("line", "pair"), None), rows),
        out_specs=(rows, rows, P(("line", "pair", "outer", "side", "twin"), None)),
        check_vma=False,
    )
```

```python
import functools
import itertools
import math

import jax
import jax.numpy as jnp
from jax import lax
from jax.experimental import pallas as pl
from jax.experimental.pallas import tpu as pltpu
from jax.sharding import Mesh, PartitionSpec as P

HEAD_DIM = 128


epsilon = 1e-06

SPLIT = 2
TWIN = 2
MEMBERS = SPLIT * SPLIT
bf16, f32 = jnp.bfloat16, jnp.float32


def local_call(name, body, out_shapes, *args, flops=0, space=pltpu.VMEM, scratch=(), room=32, moved=None):
    vmem = pl.BlockSpec(memory_space=pltpu.VMEM)
    many = isinstance(out_shapes, (list, tuple))
    if moved is None:
        moved = sum(math.prod(a.shape) * a.dtype.itemsize for a in args)
    return pl.pallas_call(
        body,
        name=name,
        out_shape=out_shapes,
        in_specs=[pl.BlockSpec(memory_space=space)] * len(args),
        out_specs=[vmem] * len(out_shapes) if many else vmem,
        scratch_shapes=scratch,
        compiler_params=pltpu.CompilerParams(vmem_limit_bytes=room << 20),
        cost_estimate=pl.CostEstimate(flops=flops, bytes_accessed=moved, transcendentals=0),
    )(*args)


def rotated(block, axis, step):
    size = lax.axis_size(axis)
    return lax.ppermute(block, axis, [(i, (i + step) % size) for i in range(size)])


def to_twin(block):
    return lax.ppermute(block, "twin", [(0, 1), (1, 0)])


def flips(far, core):
    return (0, 0) if far == 0 else (1, 1) if far == 3 else (core, 1 - core) if far == 1 else (1 - core, core)


def to_member(block, far):
    def index(side, core, pair):
        return (side * TWIN + core) * SPLIT + pair

    pairs = []
    for side, core, pair in itertools.product(range(SPLIT), range(TWIN), range(SPLIT)):
        over, across = flips(far, core)
        pairs.append((index(side, core, pair), index(side ^ over, core, pair ^ across)))
    return lax.ppermute(block, ("side", "twin", "pair"), pairs)


def run_of(part, far):
    line, core = lax.axis_size("line"), lax.axis_index("twin")
    over, across = flips(far, core)
    place = lax.rem(lax.axis_index("line") + line - part // TWIN, line)
    side, pair = lax.axis_index("side") ^ over, lax.axis_index("pair") ^ across
    return ((place * SPLIT + pair) * SPLIT + side) * TWIN + (core ^ (part % TWIN))


def front_body(tokens, shard, both, mine, *refs):
    *blocks, arrived = refs
    rows, half = mine.shape[0], both.shape[0]
    first = lax.axis_index("side") * half
    moves = []
    for target, start in ((both, first), (mine, first + lax.axis_index("twin") * rows)):
        moves.append((shard.at[pl.ds(pl.multiple_of(start, rows), target.shape[0])], target))
    parts = lax.axis_size("line") * TWIN
    run = blocks[0].shape[1] // parts
    for far, block in enumerate(blocks):
        for part in range(parts):
            start = pl.multiple_of(run_of(part, far) * run, run)
            moves.append((tokens.at[:, pl.ds(start, run)], block.at[:, pl.ds(part * run, run)]))
    copies = [pltpu.make_async_copy(*move, arrived.at[i]) for i, move in enumerate(moves)]
    for copy in copies:
        copy.start()
    for copy in copies:
        copy.wait()


def unpack_body(fars, *refs):
    blocks = refs[: len(fars)]
    whole, done = refs[-2:]
    parts = lax.axis_size("line") * TWIN
    run = blocks[0].shape[1] // parts
    moves = []
    for far, block in zip(fars, blocks):
        for part in range(parts):
            start = pl.multiple_of(run_of(part, far) * run, run)
            moves.append((block.at[:, pl.ds(part * run, run)], whole.at[:, pl.ds(start, run)]))
    copies = [pltpu.make_async_copy(*move, done.at[i]) for i, move in enumerate(moves)]
    for copy in copies:
        copy.start()
    for copy in copies:
        copy.wait()


def unpack(fars, blocks, shape, whole=None):
    vmem, hbm = pl.BlockSpec(memory_space=pltpu.VMEM), pl.BlockSpec(memory_space=pl.ANY)
    held = [] if whole is None else [whole]
    return pl.pallas_call(
        functools.partial(unpack_body, fars),
        name="unpack",
        out_shape=shape,
        in_specs=[vmem] * len(blocks) + [hbm] * len(held),
        out_specs=hbm,
        input_output_aliases={len(blocks): 0} if held else {},
        scratch_shapes=[pltpu.SemaphoreType.DMA((len(blocks) * lax.axis_size("line") * TWIN,))],
        compiler_params=pltpu.CompilerParams(vmem_limit_bytes=32 << 20),
        cost_estimate=pl.CostEstimate(flops=0, bytes_accessed=0, transcendentals=0),
    )(*blocks, *held)


def split_runs(tokens, outer):
    tok_rows, width = tokens.shape
    inner = lax.axis_size("line") * lax.axis_size("pair")
    near = SPLIT * TWIN
    cut = tokens.reshape(tok_rows, inner, outer, near, width // (inner * outer * near))
    return cut.transpose(0, 1, 3, 2, 4).reshape(tok_rows, width)


def join_runs(tokens, outer):
    tok_rows, width = tokens.shape
    inner = lax.axis_size("line") * lax.axis_size("pair")
    near = SPLIT * TWIN
    cut = tokens.reshape(tok_rows, inner, near, outer, width // (inner * outer * near))
    return cut.transpose(0, 1, 3, 2, 4).reshape(tok_rows, width)


def parted(block, step):
    line = lax.axis_size("line")
    to = [core * line + (i + (line - step if core else step)) % line for core in range(TWIN) for i in range(line)]
    return lax.ppermute(block, ("twin", "line"), list(enumerate(to)))


def cuts(rows, count):
    unit = math.gcd(rows, 64)
    ends = [-(-rows // unit * i // count) * unit for i in range(count + 1)]
    return list(zip(ends, ends[1:]))


def relay_body(count, *refs):
    rows = jnp.concatenate([ref[...] for ref in refs[:-count]], axis=0)
    for (start, end), out in zip(cuts(rows.shape[0], count), refs[-count:]):
        out[...] = rows[start:end]


def join_body(line, count, *refs):
    both, *pieces, whole = refs
    others = jnp.concatenate([piece[...] for piece in pieces[-count:]], axis=0)
    pieces = pieces[:-count]
    rows = whole.shape[0] // (line * TWIN)
    core = lax.axis_index("twin")

    def put(step, twin_run, piece):
        part = step * TWIN + (twin_run ^ core)
        whole[pl.ds(pl.multiple_of(part * rows, rows), rows), :] = piece

    def put_both(step, piece):
        for twin_run in range(TWIN):
            put(step, twin_run, piece[twin_run * rows : (twin_run + 1) * rows])

    put_both(0, both[...])
    for step in range(1, (line + 1) // 2):
        at = (step - 1) * TWIN * rows
        put_both(jnp.where(core == 0, step, line - step), pieces[step - 1][...])
        put_both(jnp.where(core == 0, line - step, step), others[at : at + TWIN * rows])
    if line % 2 == 0:
        put(line // 2, core, pieces[-1][...])
        put(line // 2, 1 - core, others[others.shape[0] - rows :])


def share_body(block, weight, out):
    out[...] = jnp.dot(block[...], weight[...], preferred_element_type=f32).astype(out.dtype)


def columns_body(grad, weight, out):
    out[...] = lax.dot_general(
        grad[...], weight[...], (((1,), (1,)), ((), ())), preferred_element_type=f32
    ).astype(out.dtype)


def add_body(first, second, out):
    out[...] = (first[...].astype(f32) + second[...].astype(f32)).astype(out.dtype)


def emit_body(held, out):
    out[...] = held[...]


def norm_body(*refs):
    *shares, cotangent, key_out, key_grad = refs
    for head in range(key_out.shape[1] // HEAD_DIM):
        at = slice(head * HEAD_DIM, (head + 1) * HEAD_DIM)
        raw = sum(share[:, at].astype(f32) for share in shares)
        inverse = lax.rsqrt(jnp.mean(raw * raw, axis=-1, keepdims=True) + epsilon)
        normed = raw * inverse
        upstream = cotangent[:, at].astype(f32)
        projected = jnp.mean(upstream * normed, axis=-1, keepdims=True)
        key_out[:, at] = normed.astype(bf16)
        key_grad[:, at] = (inverse * (upstream - normed * projected)).astype(bf16)


def terms_body(grad_scale, *refs):
    blocks, grads, (kept, *leaving) = refs[:MEMBERS], refs[MEMBERS : 2 * MEMBERS], refs[2 * MEMBERS :]
    tokens = jnp.concatenate([block[...] for block in blocks], axis=0)
    grad = jnp.concatenate([grad[...] for grad in grads], axis=0)
    line, rows, _ = kept.shape
    total = lax.dot_general(tokens, grad, (((0,), (0,)), ((), ())), preferred_element_type=f32)
    total = total * grad_scale
    others = []
    for step in range(line):
        start = step * TWIN * rows
        kept[step] = total[start : start + rows]
        others.append(total[start + rows : start + TWIN * rows].astype(bf16))
    others = jnp.concatenate(others, axis=0)
    for (start, end), piece in zip(cuts(line * rows, len(leaving)), leaving):
        piece[...] = others[start:end]


def merge_body(count, kept, *refs):
    others = jnp.concatenate([piece[...] for piece in refs[:count]], axis=0)
    own, *leaving = refs[count:]
    rows = own.shape[0]
    for step in range(kept.shape[0]):
        piece = kept[step] + others[step * rows : (step + 1) * rows].astype(f32)
        if step == 0:
            own[...] = piece
        else:
            leaving[step - 1][...] = piece.astype(bf16)


def sum_body(*refs):
    refs[-1][...] = sum(ref[...].astype(f32) for ref in refs[:-1])


def per_device(tokens, key_weight, cotangent):
    tok_rows, width = tokens.shape
    shard_rows, key_cols = key_weight.shape
    outer, line = lax.axis_size("outer"), lax.axis_size("line")
    parts = line * TWIN
    rows = shard_rows // (SPLIT * TWIN)
    owned = width // MEMBERS
    grad_scale = 1.0 / math.sqrt(tok_rows * outer * TWIN * MEMBERS * line)
    flops = 2 * tok_rows * owned * key_cols
    shape = jax.ShapeDtypeStruct
    block_shape, head_shape = shape((tok_rows, owned), bf16), shape((tok_rows, key_cols), bf16)
    if outer > 1:
        cut = key_weight.reshape(outer, SPLIT * TWIN, rows // outer, key_cols)
        key_weight = cut.transpose(1, 0, 2, 3).reshape(shard_rows, key_cols)
        tokens = split_runs(tokens, outer)

    both, mine, *packed = local_call(
        "front",
        front_body,
        [shape((TWIN * rows, key_cols), bf16), shape((rows, key_cols), bf16)] + [block_shape] * MEMBERS,
        tokens,
        key_weight,
        space=pltpu.HBM,
        room=53,
        scratch=[pltpu.SemaphoreType.DMA((2 + MEMBERS * parts,))],
    )
    blocks = packed[:1] + [to_member(packed[far], far) for far in range(1, MEMBERS)]
    passed = [parted(both, step) for step in range(1, (line + 1) // 2)]
    if line % 2 == 0:
        passed.append(rotated(mine, "line", line // 2))
    pieces = [both]
    reach = shard_rows // SPLIT * (line - 1) // TWIN
    relayed = local_call(
        "relay",
        functools.partial(relay_body, 2),
        [shape((end - start, key_cols), bf16) for start, end in cuts(reach, 2)],
        *passed,
        flops=8 * flops,
    )
    theirs = [to_twin(piece) for piece in relayed]
    theirs, blocks = lax.optimization_barrier((theirs, blocks))
    weight = local_call(
        "join",
        functools.partial(join_body, line, 2),
        shape((owned, key_cols), bf16),
        both,
        *passed,
        *theirs,
    )

    def share(far, kind):
        shaped = shape((tok_rows, key_cols), kind)
        return local_call("share", share_body, shaped, blocks[far], weight, flops=flops)

    passing = to_member(share(3, bf16), 2)
    second = to_member(share(2, bf16), 2)
    first = to_member(local_call("add", add_body, head_shape, share(1, f32), passing), 1)
    normed, key_grad = local_call("norm", norm_body, [head_shape] * 2, share(0, f32), second, first, cotangent)
    key_out = local_call("emit", emit_body, head_shape, normed)

    grad_1 = to_member(key_grad, 1)
    grad_2 = to_member(key_grad, 2)
    grad_3 = to_member(grad_1, 2)

    def columns(grad):
        return local_call("columns", columns_body, block_shape, grad, weight, moved=0)

    seen_1, grad_2 = lax.optimization_barrier((grad_1, grad_2))
    column_0, column_1 = columns(key_grad), columns(seen_1)
    column_0, column_1, key_out, grad_3 = lax.optimization_barrier((column_0, column_1, key_out, grad_3))
    back_1 = to_member(column_1, 1)
    terms = local_call(
        "terms",
        functools.partial(terms_body, grad_scale),
        [shape((line, rows, key_cols), f32)]
        + [shape((end - start, key_cols), bf16) for start, end in cuts(line * rows, 3)],
        *blocks,
        key_grad,
        grad_1,
        grad_2,
        grad_3,
        flops=MEMBERS * flops,
    )
    kept, *theirs = terms
    theirs = [to_twin(piece) for piece in theirs]
    column_2, column_3 = columns(grad_2), columns(grad_3)
    theirs, back_1, column_2, column_3 = lax.optimization_barrier((theirs, back_1, column_2, column_3))
    sums = local_call(
        "merge",
        functools.partial(merge_body, 3),
        [shape((rows, key_cols), f32)] + [shape((rows, key_cols), bf16)] * (line - 1),
        kept,
        *theirs,
        moved=0,
    )
    met = [sums[0]] + [rotated(sums[step], "line", -step) for step in range(1, line)]
    weight_grad = local_call("final_sum", sum_body, shape((rows, key_cols), f32), *met, flops=32 * flops)
    if outer > 1:
        weight_grad = lax.psum_scatter(weight_grad, "outer", scatter_dimension=0, tiled=True)

    back_2, back_3 = to_member(column_2, 2), to_member(column_3, 3)
    input_grad = unpack((0, 1), (column_0, back_1), shape((tok_rows, width), bf16))
    back_2, back_3, weight_grad = lax.optimization_barrier((back_2, back_3, weight_grad))
    input_grad = unpack((2, 3), (back_2, back_3), shape((tok_rows, width), bf16), input_grad)
    if outer > 1:
        input_grad = join_runs(input_grad, outer)
    return (key_out, input_grad, weight_grad)


def solution(mesh):
    replicas, group = mesh.shape["dp"], mesh.shape["inner"]
    fine = Mesh(
        mesh.devices.reshape(replicas // (SPLIT * TWIN), SPLIT, TWIN, group // SPLIT, SPLIT),
        ("outer", "side", "twin", "line", "pair"),
    )
    rows = P(("outer", "side", "twin", "line", "pair"), None)
    return jax.shard_map(
        per_device,
        mesh=fine,
        in_specs=(rows, P(("line", "pair"), None), rows),
        out_specs=(rows, rows, P(("line", "pair", "outer", "side", "twin"), None)),
        check_vma=False,
    )
```

```python
import functools
import itertools
import math

import jax
import jax.numpy as jnp
from jax import lax
from jax.experimental import pallas as pl
from jax.experimental.pallas import tpu as pltpu
from jax.sharding import Mesh, PartitionSpec as P

HEAD_DIM = 128


epsilon = 1e-06

SPLIT = 2
TWIN = 2
MEMBERS = SPLIT * SPLIT
bf16, f32 = jnp.bfloat16, jnp.float32


def local_call(name, body, out_shapes, *args, flops=0, space=pltpu.VMEM, scratch=(), room=32, moved=None):
    vmem = pl.BlockSpec(memory_space=pltpu.VMEM)
    many = isinstance(out_shapes, (list, tuple))
    if moved is None:
        moved = sum(math.prod(a.shape) * a.dtype.itemsize for a in args)
    return pl.pallas_call(
        body,
        name=name,
        out_shape=out_shapes,
        in_specs=[pl.BlockSpec(memory_space=space)] * len(args),
        out_specs=[vmem] * len(out_shapes) if many else vmem,
        scratch_shapes=scratch,
        compiler_params=pltpu.CompilerParams(vmem_limit_bytes=int(room * 2**20)),
        cost_estimate=pl.CostEstimate(flops=flops, bytes_accessed=moved, transcendentals=0),
    )(*args)


def rotated(block, axis, step):
    size = lax.axis_size(axis)
    return lax.ppermute(block, axis, [(i, (i + step) % size) for i in range(size)])


def to_twin(block):
    return lax.ppermute(block, "twin", [(0, 1), (1, 0)])


def flips(far, core):
    return (0, 0) if far == 0 else (1, 1) if far == 3 else (core, 1 - core) if far == 1 else (1 - core, core)


def to_member(block, far):
    def index(side, core, pair):
        return (side * TWIN + core) * SPLIT + pair

    pairs = []
    for side, core, pair in itertools.product(range(SPLIT), range(TWIN), range(SPLIT)):
        over, across = flips(far, core)
        pairs.append((index(side, core, pair), index(side ^ over, core, pair ^ across)))
    return lax.ppermute(block, ("side", "twin", "pair"), pairs)


def run_of(part, far):
    line, core = lax.axis_size("line"), lax.axis_index("twin")
    over, across = flips(far, core)
    place = lax.rem(lax.axis_index("line") + line - part // TWIN, line)
    side, pair = lax.axis_index("side") ^ over, lax.axis_index("pair") ^ across
    return ((place * SPLIT + pair) * SPLIT + side) * TWIN + (core ^ (part % TWIN))


def front_body(shard, both, mine, arrived):
    rows, half = mine.shape[0], both.shape[0]
    first = lax.axis_index("side") * half
    copies = []
    for target, start in ((both, first), (mine, first + lax.axis_index("twin") * rows)):
        source = shard.at[pl.ds(pl.multiple_of(start, rows), target.shape[0])]
        copies.append(pltpu.make_async_copy(source, target, arrived.at[len(copies)]))
    for copy in copies:
        copy.start()
    for copy in copies:
        copy.wait()


def pack_body(tokens, *blocks):
    parts = lax.axis_size("line") * TWIN
    run = blocks[0].shape[1] // parts
    for far, block in enumerate(blocks):
        for part in range(parts):
            start = pl.multiple_of(run_of(part, far) * run, run)
            block[:, part * run : (part + 1) * run] = tokens[:, pl.ds(start, run)]


def unpack_body(fars, *refs):
    blocks = refs[: len(fars)]
    whole, done = refs[-2:]
    parts = lax.axis_size("line") * TWIN
    run = blocks[0].shape[1] // parts
    moves = []
    for far, block in zip(fars, blocks):
        for part in range(parts):
            start = pl.multiple_of(run_of(part, far) * run, run)
            moves.append((block.at[:, pl.ds(part * run, run)], whole.at[:, pl.ds(start, run)]))
    copies = [pltpu.make_async_copy(*move, done.at[i]) for i, move in enumerate(moves)]
    for copy in copies:
        copy.start()
    for copy in copies:
        copy.wait()


def unpack(fars, blocks, shape, whole=None):
    vmem, hbm = pl.BlockSpec(memory_space=pltpu.VMEM), pl.BlockSpec(memory_space=pl.ANY)
    held = [] if whole is None else [whole]
    return pl.pallas_call(
        functools.partial(unpack_body, fars),
        name="unpack",
        out_shape=shape,
        in_specs=[vmem] * len(blocks) + [hbm] * len(held),
        out_specs=hbm,
        input_output_aliases={len(blocks): 0} if held else {},
        scratch_shapes=[pltpu.SemaphoreType.DMA((len(blocks) * lax.axis_size("line") * TWIN,))],
        compiler_params=pltpu.CompilerParams(vmem_limit_bytes=32 << 20),
        cost_estimate=pl.CostEstimate(flops=0, bytes_accessed=0, transcendentals=0),
    )(*blocks, *held)


def split_runs(tokens, outer):
    tok_rows, width = tokens.shape
    inner = lax.axis_size("line") * lax.axis_size("pair")
    near = SPLIT * TWIN
    cut = tokens.reshape(tok_rows, inner, outer, near, width // (inner * outer * near))
    return cut.transpose(0, 1, 3, 2, 4).reshape(tok_rows, width)


def join_runs(tokens, outer):
    tok_rows, width = tokens.shape
    inner = lax.axis_size("line") * lax.axis_size("pair")
    near = SPLIT * TWIN
    cut = tokens.reshape(tok_rows, inner, near, outer, width // (inner * outer * near))
    return cut.transpose(0, 1, 3, 2, 4).reshape(tok_rows, width)


def parted(block, step):
    line = lax.axis_size("line")
    to = [core * line + (i + (line - step if core else step)) % line for core in range(TWIN) for i in range(line)]
    return lax.ppermute(block, ("twin", "line"), list(enumerate(to)))


def cuts(rows, count):
    unit = math.gcd(rows, 64)
    ends = [-(-rows // unit * i // count) * unit for i in range(count + 1)]
    return list(zip(ends, ends[1:]))


def relay_body(count, *refs):
    rows = jnp.concatenate([ref[...] for ref in refs[:-count]], axis=0)
    for (start, end), out in zip(cuts(rows.shape[0], count), refs[-count:]):
        out[...] = rows[start:end]


def join_body(line, count, *refs):
    both, *pieces, whole = refs
    others = jnp.concatenate([piece[...] for piece in pieces[-count:]], axis=0)
    pieces = pieces[:-count]
    rows = whole.shape[0] // (line * TWIN)
    core = lax.axis_index("twin")

    def put(step, twin_run, piece):
        part = step * TWIN + (twin_run ^ core)
        whole[pl.ds(pl.multiple_of(part * rows, rows), rows), :] = piece

    def put_both(step, piece):
        for twin_run in range(TWIN):
            put(step, twin_run, piece[twin_run * rows : (twin_run + 1) * rows])

    put_both(0, both[...])
    for step in range(1, (line + 1) // 2):
        at = (step - 1) * TWIN * rows
        put_both(jnp.where(core == 0, step, line - step), pieces[step - 1][...])
        put_both(jnp.where(core == 0, line - step, step), others[at : at + TWIN * rows])
    if line % 2 == 0:
        put(line // 2, core, pieces[-1][...])
        put(line // 2, 1 - core, others[others.shape[0] - rows :])


def share_body(block, weight, out):
    out[...] = jnp.dot(block[...], weight[...], preferred_element_type=f32).astype(out.dtype)


def columns_body(grad, weight, out):
    out[...] = lax.dot_general(
        grad[...], weight[...], (((1,), (1,)), ((), ())), preferred_element_type=f32
    ).astype(out.dtype)


def add_body(first, second, out):
    out[...] = (first[...].astype(f32) + second[...].astype(f32)).astype(out.dtype)


def emit_body(held, out):
    out[...] = held[...]


def norm_body(*refs):
    *shares, cotangent, key_out, key_grad = refs
    for head in range(key_out.shape[1] // HEAD_DIM):
        at = slice(head * HEAD_DIM, (head + 1) * HEAD_DIM)
        raw = sum(share[:, at].astype(f32) for share in shares)
        inverse = lax.rsqrt(jnp.mean(raw * raw, axis=-1, keepdims=True) + epsilon)
        normed = raw * inverse
        upstream = cotangent[:, at].astype(f32)
        projected = jnp.mean(upstream * normed, axis=-1, keepdims=True)
        key_out[:, at] = normed.astype(bf16)
        key_grad[:, at] = (inverse * (upstream - normed * projected)).astype(bf16)


def terms_body(grad_scale, *refs):
    blocks, grads, (kept, *leaving) = refs[:MEMBERS], refs[MEMBERS : 2 * MEMBERS], refs[2 * MEMBERS :]
    tokens = jnp.concatenate([block[...] for block in blocks], axis=0)
    grad = jnp.concatenate([grad[...] for grad in grads], axis=0)
    line, rows, _ = kept.shape
    total = lax.dot_general(tokens, grad, (((0,), (0,)), ((), ())), preferred_element_type=f32)
    total = total * grad_scale
    others = []
    for step in range(line):
        start = step * TWIN * rows
        kept[step] = total[start : start + rows]
        others.append(total[start + rows : start + TWIN * rows].astype(bf16))
    others = jnp.concatenate(others, axis=0)
    for (start, end), piece in zip(cuts(line * rows, len(leaving)), leaving):
        piece[...] = others[start:end]


def merge_body(count, kept, *refs):
    others = jnp.concatenate([piece[...] for piece in refs[:count]], axis=0)
    own, *leaving = refs[count:]
    rows = own.shape[0]
    for step in range(kept.shape[0]):
        piece = kept[step] + others[step * rows : (step + 1) * rows].astype(f32)
        if step == 0:
            own[...] = piece
        else:
            leaving[step - 1][...] = piece.astype(bf16)


def sum_body(*refs):
    refs[-1][...] = sum(ref[...].astype(f32) for ref in refs[:-1])


def per_device(tokens, key_weight, cotangent):
    tok_rows, width = tokens.shape
    shard_rows, key_cols = key_weight.shape
    outer, line = lax.axis_size("outer"), lax.axis_size("line")
    parts = line * TWIN
    rows = shard_rows // (SPLIT * TWIN)
    owned = width // MEMBERS
    grad_scale = 1.0 / math.sqrt(tok_rows * outer * TWIN * MEMBERS * line)
    flops = 2 * tok_rows * owned * key_cols
    shape = jax.ShapeDtypeStruct
    block_shape, head_shape = shape((tok_rows, owned), bf16), shape((tok_rows, key_cols), bf16)
    if outer > 1:
        cut = key_weight.reshape(outer, SPLIT * TWIN, rows // outer, key_cols)
        key_weight = cut.transpose(1, 0, 2, 3).reshape(shard_rows, key_cols)
        tokens = split_runs(tokens, outer)

    both, mine = local_call(
        "front",
        front_body,
        [shape((TWIN * rows, key_cols), bf16), shape((rows, key_cols), bf16)],
        key_weight,
        space=pltpu.HBM,
        scratch=[pltpu.SemaphoreType.DMA((2,))],
        room=53.4,
    )
    packed = local_call("pack", pack_body, [block_shape] * MEMBERS, tokens)
    blocks = [packed[0]] + [to_member(packed[far], far) for far in range(1, MEMBERS)]
    passed = [parted(both, step) for step in range(1, (line + 1) // 2)]
    if line % 2 == 0:
        passed.append(rotated(mine, "line", line // 2))
    pieces = [both]
    reach = shard_rows // SPLIT * (line - 1) // TWIN
    relayed = local_call(
        "relay",
        functools.partial(relay_body, 2),
        [shape((end - start, key_cols), bf16) for start, end in cuts(reach, 2)],
        *passed,
        flops=8 * flops,
    )
    theirs = [to_twin(piece) for piece in relayed]
    theirs, blocks = lax.optimization_barrier((theirs, blocks))
    weight = local_call(
        "join",
        functools.partial(join_body, line, 2),
        shape((owned, key_cols), bf16),
        both,
        *passed,
        *theirs,
    )

    def share(far, kind):
        shaped = shape((tok_rows, key_cols), kind)
        return local_call("share", share_body, shaped, blocks[far], weight, flops=flops)

    shares = [to_member(share(far, bf16), far) for far in (3, 1, 2)]
    normed, key_grad = local_call("norm", norm_body, [head_shape] * 2, share(0, f32), *shares, cotangent)
    key_out = local_call("emit", emit_body, head_shape, normed)

    grad_3, grad_1, grad_2 = (to_member(key_grad, far) for far in (3, 1, 2))

    def columns(grad):
        return local_call("columns", columns_body, block_shape, grad, weight, moved=0)

    column_0, column_1 = columns(key_grad), columns(grad_1)
    back_1 = to_member(column_1, 1)
    column_0, _, key_out, grad_2, grad_3 = lax.optimization_barrier(
        (column_0, column_1, key_out, grad_2, grad_3)
    )
    terms = local_call(
        "terms",
        functools.partial(terms_body, grad_scale),
        [shape((line, rows, key_cols), f32)]
        + [shape((end - start, key_cols), bf16) for start, end in cuts(line * rows, 3)],
        *blocks,
        key_grad,
        grad_1,
        grad_2,
        grad_3,
        moved=0,
    )
    kept, *theirs = terms
    theirs = [to_twin(piece) for piece in theirs]
    column_2, column_3 = columns(grad_2), columns(grad_3)
    theirs, back_1, column_2, column_3 = lax.optimization_barrier((theirs, back_1, column_2, column_3))
    sums = local_call(
        "merge",
        functools.partial(merge_body, 3),
        [shape((rows, key_cols), f32)] + [shape((rows, key_cols), bf16)] * (line - 1),
        kept,
        *theirs,
        moved=0,
    )
    met = [sums[0]] + [rotated(sums[step], "line", -step) for step in range(1, line)]
    input_grad = unpack((0, 1), (column_0, back_1), shape((tok_rows, width), bf16))
    met, input_grad = lax.optimization_barrier((met, input_grad))
    weight_grad = local_call("final_sum", sum_body, shape((rows, key_cols), f32), *met, flops=16 * flops)
    if outer > 1:
        weight_grad = lax.psum_scatter(weight_grad, "outer", scatter_dimension=0, tiled=True)

    back_2 = to_member(column_2, 2)
    column_3, back_1, back_2 = lax.optimization_barrier((column_3, back_1, back_2))
    back_3 = to_member(column_3, 3)
    back_2, back_3, weight_grad = lax.optimization_barrier((back_2, back_3, weight_grad))
    input_grad = unpack((2, 3), (back_2, back_3), shape((tok_rows, width), bf16), input_grad)
    if outer > 1:
        input_grad = join_runs(input_grad, outer)
    return (key_out, input_grad, weight_grad)


def solution(mesh):
    replicas, group = mesh.shape["dp"], mesh.shape["inner"]
    fine = Mesh(
        mesh.devices.reshape(replicas // (SPLIT * TWIN), SPLIT, TWIN, group // SPLIT, SPLIT),
        ("outer", "side", "twin", "line", "pair"),
    )
    rows = P(("outer", "side", "twin", "line", "pair"), None)
    return jax.shard_map(
        per_device,
        mesh=fine,
        in_specs=(rows, P(("line", "pair"), None), rows),
        out_specs=(rows, rows, P(("line", "pair", "outer", "side", "twin"), None)),
        check_vma=False,
    )
```

```python
import functools
import math

import jax
import jax.numpy as jnp
from jax import lax
from jax.experimental import pallas as pl
from jax.experimental.pallas import tpu as pltpu
from jax.sharding import Mesh, PartitionSpec as P

HEAD_DIM = 128


epsilon = 1e-06

SPLIT = 2
TWIN = 2
MEMBERS = SPLIT * SPLIT
bf16, f32 = jnp.bfloat16, jnp.float32


def local_call(name, body, out_shapes, *args, flops=0, space=pltpu.VMEM, scratch=(), room=32, moved=None):
    vmem = pl.BlockSpec(memory_space=pltpu.VMEM)
    many = isinstance(out_shapes, (list, tuple))
    if moved is None:
        moved = sum(math.prod(a.shape) * a.dtype.itemsize for a in args)
    return pl.pallas_call(
        body,
        name=name,
        out_shape=out_shapes,
        in_specs=[pl.BlockSpec(memory_space=space)] * len(args),
        out_specs=[vmem] * len(out_shapes) if many else vmem,
        scratch_shapes=scratch,
        compiler_params=pltpu.CompilerParams(vmem_limit_bytes=int(room * 2**20)),
        cost_estimate=pl.CostEstimate(flops=flops, bytes_accessed=moved, transcendentals=0),
    )(*args)


def rotated(block, axis, step):
    size = lax.axis_size(axis)
    return lax.ppermute(block, axis, [(i, (i + step) % size) for i in range(size)])


def to_twin(block):
    return lax.ppermute(block, "twin", [(0, 1), (1, 0)])


def flips(far):
    return far // SPLIT, far % SPLIT


def to_member(block, far):
    return lax.ppermute(block, ("side", "pair"), [(i, i ^ far) for i in range(MEMBERS)])


def run_of(part, far):
    line, core = lax.axis_size("line"), lax.axis_index("twin")
    over, across = flips(far)
    place = lax.rem(lax.axis_index("line") + line - part // TWIN, line)
    side, pair = lax.axis_index("side") ^ over, lax.axis_index("pair") ^ across
    return ((place * SPLIT + pair) * SPLIT + side) * TWIN + (core ^ (part % TWIN))


def front_body(shard, both, mine, arrived):
    rows, half = mine.shape[0], both.shape[0]
    first = lax.axis_index("side") * half
    copies = []
    for target, start in ((both, first), (mine, first + lax.axis_index("twin") * rows)):
        source = shard.at[pl.ds(pl.multiple_of(start, rows), target.shape[0])]
        copies.append(pltpu.make_async_copy(source, target, arrived.at[len(copies)]))
    for copy in copies:
        copy.start()
    for copy in copies:
        copy.wait()


def pack_body(tokens, *blocks):
    parts = lax.axis_size("line") * TWIN
    run = blocks[0].shape[1] // parts
    for far, block in enumerate(blocks):
        for part in range(parts):
            start = pl.multiple_of(run_of(part, far) * run, run)
            block[:, part * run : (part + 1) * run] = tokens[:, pl.ds(start, run)]


def unpack_body(fars, *refs):
    blocks = refs[: len(fars)]
    whole, done = refs[-2:]
    parts = lax.axis_size("line") * TWIN
    run = blocks[0].shape[1] // parts
    moves = []
    for far, block in zip(fars, blocks):
        for part in range(parts):
            start = pl.multiple_of(run_of(part, far) * run, run)
            moves.append((block.at[:, pl.ds(part * run, run)], whole.at[:, pl.ds(start, run)]))
    copies = [pltpu.make_async_copy(*move, done.at[i]) for i, move in enumerate(moves)]
    for copy in copies:
        copy.start()
    for copy in copies:
        copy.wait()


def unpack(fars, blocks, shape, whole=None):
    vmem, hbm = pl.BlockSpec(memory_space=pltpu.VMEM), pl.BlockSpec(memory_space=pl.ANY)
    held = [] if whole is None else [whole]
    return pl.pallas_call(
        functools.partial(unpack_body, fars),
        name="unpack",
        out_shape=shape,
        in_specs=[vmem] * len(blocks) + [hbm] * len(held),
        out_specs=hbm,
        input_output_aliases={len(blocks): 0} if held else {},
        scratch_shapes=[pltpu.SemaphoreType.DMA((len(blocks) * lax.axis_size("line") * TWIN,))],
        compiler_params=pltpu.CompilerParams(vmem_limit_bytes=32 << 20),
        cost_estimate=pl.CostEstimate(flops=0, bytes_accessed=0, transcendentals=0),
    )(*blocks, *held)


def split_runs(tokens, outer):
    tok_rows, width = tokens.shape
    inner = lax.axis_size("line") * lax.axis_size("pair")
    near = SPLIT * TWIN
    cut = tokens.reshape(tok_rows, inner, outer, near, width // (inner * outer * near))
    return cut.transpose(0, 1, 3, 2, 4).reshape(tok_rows, width)


def join_runs(tokens, outer):
    tok_rows, width = tokens.shape
    inner = lax.axis_size("line") * lax.axis_size("pair")
    near = SPLIT * TWIN
    cut = tokens.reshape(tok_rows, inner, near, outer, width // (inner * outer * near))
    return cut.transpose(0, 1, 3, 2, 4).reshape(tok_rows, width)


def parted(block, step):
    line = lax.axis_size("line")
    to = [core * line + (i + (line - step if core else step)) % line for core in range(TWIN) for i in range(line)]
    return lax.ppermute(block, ("twin", "line"), list(enumerate(to)))


def cuts(rows, count):
    unit = math.gcd(rows, 64)
    ends = [-(-rows // unit * i // count) * unit for i in range(count + 1)]
    return list(zip(ends, ends[1:]))


def relay_body(count, *refs):
    rows = jnp.concatenate([ref[...] for ref in refs[:-count]], axis=0)
    for (start, end), out in zip(cuts(rows.shape[0], count), refs[-count:]):
        out[...] = rows[start:end]


def join_body(line, count, *refs):
    both, *pieces, whole = refs
    others = jnp.concatenate([piece[...] for piece in pieces[-count:]], axis=0)
    pieces = pieces[:-count]
    rows = whole.shape[0] // (line * TWIN)
    core = lax.axis_index("twin")

    def put(step, twin_run, piece):
        part = step * TWIN + (twin_run ^ core)
        whole[pl.ds(pl.multiple_of(part * rows, rows), rows), :] = piece

    def put_both(step, piece):
        for twin_run in range(TWIN):
            put(step, twin_run, piece[twin_run * rows : (twin_run + 1) * rows])

    put_both(0, both[...])
    for step in range(1, (line + 1) // 2):
        at = (step - 1) * TWIN * rows
        put_both(jnp.where(core == 0, step, line - step), pieces[step - 1][...])
        put_both(jnp.where(core == 0, line - step, step), others[at : at + TWIN * rows])
    if line % 2 == 0:
        put(line // 2, core, pieces[-1][...])
        put(line // 2, 1 - core, others[others.shape[0] - rows :])


def share_body(block, weight, out):
    out[...] = jnp.dot(block[...], weight[...], preferred_element_type=f32).astype(out.dtype)


def columns_body(grad, weight, out):
    out[...] = lax.dot_general(
        grad[...], weight[...], (((1,), (1,)), ((), ())), preferred_element_type=f32
    ).astype(out.dtype)


def add_body(first, second, out):
    out[...] = (first[...].astype(f32) + second[...].astype(f32)).astype(out.dtype)


def emit_body(held, out):
    out[...] = held[...]


def norm_body(*refs):
    *shares, cotangent, key_out, key_grad = refs
    for head in range(key_out.shape[1] // HEAD_DIM):
        at = slice(head * HEAD_DIM, (head + 1) * HEAD_DIM)
        raw = sum(share[:, at].astype(f32) for share in shares)
        inverse = lax.rsqrt(jnp.mean(raw * raw, axis=-1, keepdims=True) + epsilon)
        normed = raw * inverse
        upstream = cotangent[:, at].astype(f32)
        projected = jnp.mean(upstream * normed, axis=-1, keepdims=True)
        key_out[:, at] = normed.astype(bf16)
        key_grad[:, at] = (inverse * (upstream - normed * projected)).astype(bf16)


def terms_body(grad_scale, *refs):
    blocks, grads, (kept, *leaving) = refs[:MEMBERS], refs[MEMBERS : 2 * MEMBERS], refs[2 * MEMBERS :]
    tokens = jnp.concatenate([block[...] for block in blocks], axis=0)
    grad = jnp.concatenate([grad[...] for grad in grads], axis=0)
    line, rows, _ = kept.shape
    total = lax.dot_general(tokens, grad, (((0,), (0,)), ((), ())), preferred_element_type=f32)
    total = total * grad_scale
    others = []
    for step in range(line):
        start = step * TWIN * rows
        kept[step] = total[start : start + rows]
        others.append(total[start + rows : start + TWIN * rows].astype(bf16))
    others = jnp.concatenate(others, axis=0)
    for (start, end), piece in zip(cuts(line * rows, len(leaving)), leaving):
        piece[...] = others[start:end]


def merge_body(count, kept, *refs):
    others = jnp.concatenate([piece[...] for piece in refs[:count]], axis=0)
    own, *leaving = refs[count:]
    rows = own.shape[0]
    for step in range(kept.shape[0]):
        piece = kept[step] + others[step * rows : (step + 1) * rows].astype(f32)
        if step == 0:
            own[...] = piece
        else:
            leaving[step - 1][...] = piece.astype(bf16)


def sum_body(*refs):
    refs[-1][...] = sum(ref[...].astype(f32) for ref in refs[:-1])


def per_device(tokens, key_weight, cotangent):
    tok_rows, width = tokens.shape
    shard_rows, key_cols = key_weight.shape
    outer, line = lax.axis_size("outer"), lax.axis_size("line")
    parts = line * TWIN
    rows = shard_rows // (SPLIT * TWIN)
    owned = width // MEMBERS
    grad_scale = 1.0 / math.sqrt(tok_rows * outer * TWIN * MEMBERS * line)
    flops = 2 * tok_rows * owned * key_cols
    shape = jax.ShapeDtypeStruct
    block_shape, head_shape = shape((tok_rows, owned), bf16), shape((tok_rows, key_cols), bf16)
    if outer > 1:
        cut = key_weight.reshape(outer, SPLIT * TWIN, rows // outer, key_cols)
        key_weight = cut.transpose(1, 0, 2, 3).reshape(shard_rows, key_cols)
        tokens = split_runs(tokens, outer)

    both, mine = local_call(
        "front",
        front_body,
        [shape((TWIN * rows, key_cols), bf16), shape((rows, key_cols), bf16)],
        key_weight,
        space=pltpu.HBM,
        scratch=[pltpu.SemaphoreType.DMA((2,))],
        room=53.4,
    )
    packed = local_call("pack", pack_body, [block_shape] * MEMBERS, tokens)
    blocks = [packed[0]] + [to_member(packed[far], far) for far in range(1, MEMBERS)]
    passed = [parted(both, step) for step in range(1, (line + 1) // 2)]
    if line % 2 == 0:
        passed.append(rotated(mine, "line", line // 2))
    pieces = [both]
    reach = shard_rows // SPLIT * (line - 1) // TWIN
    relayed = local_call(
        "relay",
        functools.partial(relay_body, 2),
        [shape((end - start, key_cols), bf16) for start, end in cuts(reach, 2)],
        *passed,
        flops=8 * flops,
    )
    theirs = [to_twin(piece) for piece in relayed]
    theirs, blocks = lax.optimization_barrier((theirs, blocks))
    weight = local_call(
        "join",
        functools.partial(join_body, line, 2),
        shape((owned, key_cols), bf16),
        both,
        *passed,
        *theirs,
    )

    def share(far, kind):
        shaped = shape((tok_rows, key_cols), kind)
        return local_call("share", share_body, shaped, blocks[far], weight, flops=flops)

    shares = [to_member(share(far, bf16), far) for far in (3, 1, 2)]
    normed, key_grad = local_call("norm", norm_body, [head_shape] * 2, share(0, f32), *shares, cotangent)
    key_out = local_call("emit", emit_body, head_shape, normed)

    grad_3, grad_1, grad_2 = (to_member(key_grad, far) for far in (3, 1, 2))

    def columns(grad):
        return local_call("columns", columns_body, block_shape, grad, weight, moved=0)

    column_0, column_1 = columns(key_grad), columns(grad_1)
    back_1 = to_member(column_1, 1)
    column_0, _, key_out, grad_2, grad_3 = lax.optimization_barrier(
        (column_0, column_1, key_out, grad_2, grad_3)
    )
    terms = local_call(
        "terms",
        functools.partial(terms_body, grad_scale),
        [shape((line, rows, key_cols), f32)]
        + [shape((end - start, key_cols), bf16) for start, end in cuts(line * rows, 3)],
        *blocks,
        key_grad,
        grad_1,
        grad_2,
        grad_3,
        moved=0,
    )
    kept, *theirs = terms
    theirs = [to_twin(piece) for piece in theirs]
    column_2, column_3 = columns(grad_2), columns(grad_3)
    theirs, back_1, column_2, column_3 = lax.optimization_barrier((theirs, back_1, column_2, column_3))
    sums = local_call(
        "merge",
        functools.partial(merge_body, 3),
        [shape((rows, key_cols), f32)] + [shape((rows, key_cols), bf16)] * (line - 1),
        kept,
        *theirs,
        moved=0,
    )
    met = [sums[0]] + [rotated(sums[step], "line", -step) for step in range(1, line)]
    input_grad = unpack((0, 1), (column_0, back_1), shape((tok_rows, width), bf16))
    met, input_grad = lax.optimization_barrier((met, input_grad))
    weight_grad = local_call("final_sum", sum_body, shape((rows, key_cols), f32), *met, flops=16 * flops)
    if outer > 1:
        weight_grad = lax.psum_scatter(weight_grad, "outer", scatter_dimension=0, tiled=True)

    back_2 = to_member(column_2, 2)
    column_3, back_1, back_2 = lax.optimization_barrier((column_3, back_1, back_2))
    back_3 = to_member(column_3, 3)
    back_2, back_3, weight_grad = lax.optimization_barrier((back_2, back_3, weight_grad))
    input_grad = unpack((2, 3), (back_2, back_3), shape((tok_rows, width), bf16), input_grad)
    if outer > 1:
        input_grad = join_runs(input_grad, outer)
    return (key_out, input_grad, weight_grad)


def solution(mesh):
    replicas, group = mesh.shape["dp"], mesh.shape["inner"]
    fine = Mesh(
        mesh.devices.reshape(replicas // (SPLIT * TWIN), SPLIT, TWIN, group // SPLIT, SPLIT),
        ("outer", "side", "twin", "line", "pair"),
    )
    rows = P(("outer", "side", "twin", "line", "pair"), None)
    return jax.shard_map(
        per_device,
        mesh=fine,
        in_specs=(rows, P(("line", "pair"), None), rows),
        out_specs=(rows, rows, P(("line", "pair", "outer", "side", "twin"), None)),
        check_vma=False,
    )
```

```python
import functools
import math

import jax
import jax.numpy as jnp
from jax import lax
from jax.experimental import pallas as pl
from jax.experimental.pallas import tpu as pltpu
from jax.sharding import Mesh, PartitionSpec as P

HEAD_DIM = 128


epsilon = 1e-06

SPLIT = 2
TWIN = 2
MEMBERS = SPLIT * SPLIT
bf16, f32 = jnp.bfloat16, jnp.float32


def local_call(name, body, out_shapes, *args, flops=0, space=pltpu.VMEM, scratch=(), room=32, moved=None):
    vmem = pl.BlockSpec(memory_space=pltpu.VMEM)
    many = isinstance(out_shapes, (list, tuple))
    if moved is None:
        moved = sum(math.prod(a.shape) * a.dtype.itemsize for a in args)
    return pl.pallas_call(
        body,
        name=name,
        out_shape=out_shapes,
        in_specs=[pl.BlockSpec(memory_space=space)] * len(args),
        out_specs=[vmem] * len(out_shapes) if many else vmem,
        scratch_shapes=scratch,
        compiler_params=pltpu.CompilerParams(vmem_limit_bytes=int(room * 2**20)),
        cost_estimate=pl.CostEstimate(flops=flops, bytes_accessed=moved, transcendentals=0),
    )(*args)


def rotated(block, axis, step):
    size = lax.axis_size(axis)
    return lax.ppermute(block, axis, [(i, (i + step) % size) for i in range(size)])


def to_twin(block):
    return lax.ppermute(block, "twin", [(0, 1), (1, 0)])


def flips(far):
    return far // SPLIT, far % SPLIT


def to_member(block, far):
    return lax.ppermute(block, ("side", "pair"), [(i, i ^ far) for i in range(MEMBERS)])


def run_of(part, far):
    line, core = lax.axis_size("line"), lax.axis_index("twin")
    over, across = flips(far)
    place = lax.rem(lax.axis_index("line") + line - part // TWIN, line)
    side, pair = lax.axis_index("side") ^ over, lax.axis_index("pair") ^ across
    return ((place * SPLIT + pair) * SPLIT + side) * TWIN + (core ^ (part % TWIN))


def front_body(shard, both, mine, arrived):
    rows, half = mine.shape[0], both.shape[0]
    first = lax.axis_index("side") * half
    copies = []
    for target, start in ((both, first), (mine, first + lax.axis_index("twin") * rows)):
        source = shard.at[pl.ds(pl.multiple_of(start, rows), target.shape[0])]
        copies.append(pltpu.make_async_copy(source, target, arrived.at[len(copies)]))
    for copy in copies:
        copy.start()
    for copy in copies:
        copy.wait()


def pack_body(tokens, *blocks):
    parts = lax.axis_size("line") * TWIN
    run = blocks[0].shape[1] // parts
    for far, block in enumerate(blocks):
        for part in range(parts):
            start = pl.multiple_of(run_of(part, far) * run, run)
            block[:, part * run : (part + 1) * run] = tokens[:, pl.ds(start, run)]


def unpack_body(fars, *refs):
    blocks = refs[: len(fars)]
    whole, done = refs[-2:]
    parts = lax.axis_size("line") * TWIN
    run = blocks[0].shape[1] // parts
    moves = []
    for far, block in zip(fars, blocks):
        for part in range(parts):
            start = pl.multiple_of(run_of(part, far) * run, run)
            moves.append((block.at[:, pl.ds(part * run, run)], whole.at[:, pl.ds(start, run)]))
    copies = [pltpu.make_async_copy(*move, done.at[i]) for i, move in enumerate(moves)]
    for copy in copies:
        copy.start()
    for copy in copies:
        copy.wait()


def unpack(fars, blocks, shape, whole=None):
    vmem, hbm = pl.BlockSpec(memory_space=pltpu.VMEM), pl.BlockSpec(memory_space=pl.ANY)
    held = [] if whole is None else [whole]
    return pl.pallas_call(
        functools.partial(unpack_body, fars),
        name="unpack",
        out_shape=shape,
        in_specs=[vmem] * len(blocks) + [hbm] * len(held),
        out_specs=hbm,
        input_output_aliases={len(blocks): 0} if held else {},
        scratch_shapes=[pltpu.SemaphoreType.DMA((len(blocks) * lax.axis_size("line") * TWIN,))],
        compiler_params=pltpu.CompilerParams(vmem_limit_bytes=32 << 20),
        cost_estimate=pl.CostEstimate(flops=0, bytes_accessed=0, transcendentals=0),
    )(*blocks, *held)


def split_runs(tokens, outer):
    tok_rows, width = tokens.shape
    inner = lax.axis_size("line") * lax.axis_size("pair")
    near = SPLIT * TWIN
    cut = tokens.reshape(tok_rows, inner, outer, near, width // (inner * outer * near))
    return cut.transpose(0, 1, 3, 2, 4).reshape(tok_rows, width)


def join_runs(tokens, outer):
    tok_rows, width = tokens.shape
    inner = lax.axis_size("line") * lax.axis_size("pair")
    near = SPLIT * TWIN
    cut = tokens.reshape(tok_rows, inner, near, outer, width // (inner * outer * near))
    return cut.transpose(0, 1, 3, 2, 4).reshape(tok_rows, width)


def parted(block, step):
    line = lax.axis_size("line")
    to = [core * line + (i + (line - step if core else step)) % line for core in range(TWIN) for i in range(line)]
    return lax.ppermute(block, ("twin", "line"), list(enumerate(to)))


def cuts(rows, count):
    unit = math.gcd(rows, 64)
    ends = [-(-rows // unit * i // count) * unit for i in range(count + 1)]
    return list(zip(ends, ends[1:]))


def relay_body(count, *refs):
    rows = jnp.concatenate([ref[...] for ref in refs[:-count]], axis=0)
    for (start, end), out in zip(cuts(rows.shape[0], count), refs[-count:]):
        out[...] = rows[start:end]


def join_body(line, count, *refs):
    both, *pieces, whole = refs
    others = jnp.concatenate([piece[...] for piece in pieces[-count:]], axis=0)
    pieces = pieces[:-count]
    rows = whole.shape[0] // (line * TWIN)
    core = lax.axis_index("twin")

    def put(step, twin_run, piece):
        part = step * TWIN + (twin_run ^ core)
        whole[pl.ds(pl.multiple_of(part * rows, rows), rows), :] = piece

    def put_both(step, piece):
        for twin_run in range(TWIN):
            put(step, twin_run, piece[twin_run * rows : (twin_run + 1) * rows])

    put_both(0, both[...])
    for step in range(1, (line + 1) // 2):
        at = (step - 1) * TWIN * rows
        put_both(jnp.where(core == 0, step, line - step), pieces[step - 1][...])
        put_both(jnp.where(core == 0, line - step, step), others[at : at + TWIN * rows])
    if line % 2 == 0:
        put(line // 2, core, pieces[-1][...])
        put(line // 2, 1 - core, others[others.shape[0] - rows :])


def share_body(block, weight, out):
    out[...] = jnp.dot(block[...], weight[...], preferred_element_type=f32).astype(out.dtype)


def columns_body(grad, weight, out):
    out[...] = lax.dot_general(
        grad[...], weight[...], (((1,), (1,)), ((), ())), preferred_element_type=f32
    ).astype(out.dtype)


def add_body(first, second, out):
    out[...] = (first[...].astype(f32) + second[...].astype(f32)).astype(out.dtype)


def emit_body(held, out):
    out[...] = held[...]


def norm_body(*refs):
    *shares, cotangent, key_out, key_grad = refs
    for head in range(key_out.shape[1] // HEAD_DIM):
        at = slice(head * HEAD_DIM, (head + 1) * HEAD_DIM)
        raw = sum(share[:, at].astype(f32) for share in shares)
        inverse = lax.rsqrt(jnp.mean(raw * raw, axis=-1, keepdims=True) + epsilon)
        normed = raw * inverse
        upstream = cotangent[:, at].astype(f32)
        projected = jnp.mean(upstream * normed, axis=-1, keepdims=True)
        key_out[:, at] = normed.astype(bf16)
        key_grad[:, at] = (inverse * (upstream - normed * projected)).astype(bf16)


def terms_body(grad_scale, *refs):
    blocks, grads, (kept, *leaving) = refs[:MEMBERS], refs[MEMBERS : 2 * MEMBERS], refs[2 * MEMBERS :]
    tokens = jnp.concatenate([block[...] for block in blocks], axis=0)
    grad = jnp.concatenate([grad[...] for grad in grads], axis=0)
    line, rows, _ = kept.shape
    total = lax.dot_general(tokens, grad, (((0,), (0,)), ((), ())), preferred_element_type=f32)
    total = total * grad_scale
    others = []
    for step in range(line):
        start = step * TWIN * rows
        kept[step] = total[start : start + rows]
        others.append(total[start + rows : start + TWIN * rows].astype(bf16))
    others = jnp.concatenate(others, axis=0)
    for (start, end), piece in zip(cuts(line * rows, len(leaving)), leaving):
        piece[...] = others[start:end]


def merge_body(count, kept, *refs):
    others = jnp.concatenate([piece[...] for piece in refs[:count]], axis=0)
    own, *leaving = refs[count:]
    rows = own.shape[0]
    for step in range(kept.shape[0]):
        piece = kept[step] + others[step * rows : (step + 1) * rows].astype(f32)
        if step == 0:
            own[...] = piece
        else:
            leaving[step - 1][...] = piece.astype(bf16)


def sum_body(*refs):
    refs[-1][...] = sum(ref[...].astype(f32) for ref in refs[:-1])


def per_device(tokens, key_weight, cotangent):
    tok_rows, width = tokens.shape
    shard_rows, key_cols = key_weight.shape
    outer, line = lax.axis_size("outer"), lax.axis_size("line")
    parts = line * TWIN
    rows = shard_rows // (SPLIT * TWIN)
    owned = width // MEMBERS
    grad_scale = 1.0 / math.sqrt(tok_rows * outer * TWIN * MEMBERS * line)
    flops = 2 * tok_rows * owned * key_cols
    shape = jax.ShapeDtypeStruct
    block_shape, head_shape = shape((tok_rows, owned), bf16), shape((tok_rows, key_cols), bf16)
    if outer > 1:
        cut = key_weight.reshape(outer, SPLIT * TWIN, rows // outer, key_cols)
        key_weight = cut.transpose(1, 0, 2, 3).reshape(shard_rows, key_cols)
        tokens = split_runs(tokens, outer)

    both, mine = local_call(
        "front",
        front_body,
        [shape((TWIN * rows, key_cols), bf16), shape((rows, key_cols), bf16)],
        key_weight,
        space=pltpu.HBM,
        scratch=[pltpu.SemaphoreType.DMA((2,))],
        room=53.4,
    )
    packed = local_call("pack", pack_body, [block_shape] * MEMBERS, tokens)
    blocks = [packed[0], None, None, None]
    for far in (3, 1, 2):
        blocks[far] = to_member(packed[far], far)
    passed = [parted(both, step) for step in range(1, (line + 1) // 2)]
    if line % 2 == 0:
        passed.append(rotated(mine, "line", line // 2))
    pieces = [both]
    reach = shard_rows // SPLIT * (line - 1) // TWIN
    relayed = local_call(
        "relay",
        functools.partial(relay_body, 2),
        [shape((end - start, key_cols), bf16) for start, end in cuts(reach, 2)],
        *passed,
        flops=8 * flops,
    )
    theirs = [to_twin(piece) for piece in relayed]
    *blocks, theirs = lax.optimization_barrier((*blocks[::-1], theirs))
    blocks = blocks[::-1]
    weight = local_call(
        "join",
        functools.partial(join_body, line, 2),
        shape((owned, key_cols), bf16),
        both,
        *passed,
        *theirs,
    )

    def share(far, kind):
        shaped = shape((tok_rows, key_cols), kind)
        return local_call("share", share_body, shaped, blocks[far], weight, flops=flops)

    shares = [to_member(share(far, bf16), far) for far in (3, 1, 2)]
    normed, key_grad = local_call("norm", norm_body, [head_shape] * 2, share(0, f32), *shares, cotangent)
    key_out = local_call("emit", emit_body, head_shape, normed)

    grad_3, grad_1, grad_2 = (to_member(key_grad, far) for far in (3, 1, 2))

    def columns(grad, **cost):
        return local_call("columns", columns_body, block_shape, grad, weight, **cost)

    column_0, column_3 = columns(key_grad, flops=flops), columns(grad_3, flops=flops)
    column_0, column_3, key_out, grad_1, grad_2 = lax.optimization_barrier(
        (column_0, column_3, key_out, grad_1, grad_2)
    )
    kept, *theirs = local_call(
        "terms",
        functools.partial(terms_body, grad_scale),
        [shape((line, rows, key_cols), f32)]
        + [shape((end - start, key_cols), bf16) for start, end in cuts(line * rows, 2)],
        *blocks,
        key_grad,
        grad_1,
        grad_2,
        grad_3,
        moved=0,
    )
    theirs = [to_twin(piece) for piece in theirs]
    sums = local_call(
        "merge",
        functools.partial(merge_body, 2),
        [shape((rows, key_cols), f32)] + [shape((rows, key_cols), bf16)] * (line - 1),
        kept,
        *theirs,
        moved=0,
    )

    met = [sums[0]] + [rotated(sums[step], "line", -step) for step in range(1, line)]
    back_1, back_2 = to_member(columns(grad_1, flops=flops), 1), to_member(columns(grad_2, flops=flops), 2)
    column_3, back_1, back_2, _ = lax.optimization_barrier((column_3, back_1, back_2, sums))
    back_3 = to_member(column_3, 3)
    input_grad = unpack((0, 1, 2), (column_0, back_1, back_2), shape((tok_rows, width), bf16))
    met, input_grad = lax.optimization_barrier((met, input_grad))
    weight_grad = local_call("final_sum", sum_body, shape((rows, key_cols), f32), *met, flops=24 * flops)
    back_3, weight_grad = lax.optimization_barrier((back_3, weight_grad))
    if outer > 1:
        weight_grad = lax.psum_scatter(weight_grad, "outer", scatter_dimension=0, tiled=True)
    input_grad = unpack((3,), (back_3,), shape((tok_rows, width), bf16), input_grad)
    if outer > 1:
        input_grad = join_runs(input_grad, outer)
    return (key_out, input_grad, weight_grad)


def solution(mesh):
    replicas, group = mesh.shape["dp"], mesh.shape["inner"]
    fine = Mesh(
        mesh.devices.reshape(replicas // (SPLIT * TWIN), SPLIT, TWIN, group // SPLIT, SPLIT),
        ("outer", "side", "twin", "line", "pair"),
    )
    rows = P(("outer", "side", "twin", "line", "pair"), None)
    return jax.shard_map(
        per_device,
        mesh=fine,
        in_specs=(rows, P(("line", "pair"), None), rows),
        out_specs=(rows, rows, P(("line", "pair", "outer", "side", "twin"), None)),
        check_vma=False,
    )
```

```python
import functools
import math

import jax
import jax.numpy as jnp
from jax import lax
from jax.experimental import pallas as pl
from jax.experimental.pallas import tpu as pltpu
from jax.sharding import Mesh, PartitionSpec as P

HEAD_DIM = 128


epsilon = 1e-06

SPLIT = 2
TWIN = 2
MEMBERS = SPLIT * SPLIT
bf16, f32 = jnp.bfloat16, jnp.float32


def local_call(name, body, out_shapes, *args, flops=0, space=pltpu.VMEM, scratch=(), room=32, moved=None):
    vmem = pl.BlockSpec(memory_space=pltpu.VMEM)
    many = isinstance(out_shapes, (list, tuple))
    if moved is None:
        moved = sum(math.prod(a.shape) * a.dtype.itemsize for a in args)
    return pl.pallas_call(
        body,
        name=name,
        out_shape=out_shapes,
        in_specs=[pl.BlockSpec(memory_space=space)] * len(args),
        out_specs=[vmem] * len(out_shapes) if many else vmem,
        scratch_shapes=scratch,
        compiler_params=pltpu.CompilerParams(vmem_limit_bytes=int(room * 2**20)),
        cost_estimate=pl.CostEstimate(flops=flops, bytes_accessed=moved, transcendentals=0),
    )(*args)


def rotated(block, axis, step):
    size = lax.axis_size(axis)
    return lax.ppermute(block, axis, [(i, (i + step) % size) for i in range(size)])


def to_twin(block):
    return lax.ppermute(block, "twin", [(0, 1), (1, 0)])


def flips(far):
    return far // SPLIT, far % SPLIT


def to_member(block, far):
    return lax.ppermute(block, ("side", "pair"), [(i, i ^ far) for i in range(MEMBERS)])


def run_of(part, far):
    line, core = lax.axis_size("line"), lax.axis_index("twin")
    over, across = flips(far)
    place = lax.rem(lax.axis_index("line") + line - part // TWIN, line)
    side, pair = lax.axis_index("side") ^ over, lax.axis_index("pair") ^ across
    return ((place * SPLIT + pair) * SPLIT + side) * TWIN + (core ^ (part % TWIN))


def front_body(shard, both, mine, arrived):
    rows, half = mine.shape[0], both.shape[0]
    first = lax.axis_index("side") * half
    copies = []
    for target, start in ((both, first), (mine, first + lax.axis_index("twin") * rows)):
        source = shard.at[pl.ds(pl.multiple_of(start, rows), target.shape[0])]
        copies.append(pltpu.make_async_copy(source, target, arrived.at[len(copies)]))
    for copy in copies:
        copy.start()
    for copy in copies:
        copy.wait()


def pack_body(tokens, *blocks):
    parts = lax.axis_size("line") * TWIN
    run = blocks[0].shape[1] // parts
    for far, block in enumerate(blocks):
        for part in range(parts):
            start = pl.multiple_of(run_of(part, far) * run, run)
            block[:, part * run : (part + 1) * run] = tokens[:, pl.ds(start, run)]


def unpack_body(fars, *refs):
    blocks = refs[: len(fars)]
    whole, done = refs[-2:]
    parts = lax.axis_size("line") * TWIN
    run = blocks[0].shape[1] // parts
    moves = []
    for far, block in zip(fars, blocks):
        for part in range(parts):
            start = pl.multiple_of(run_of(part, far) * run, run)
            moves.append((block.at[:, pl.ds(part * run, run)], whole.at[:, pl.ds(start, run)]))
    copies = [pltpu.make_async_copy(*move, done.at[i]) for i, move in enumerate(moves)]
    for copy in copies:
        copy.start()
    for copy in copies:
        copy.wait()


def unpack(fars, blocks, shape, whole=None):
    vmem, hbm = pl.BlockSpec(memory_space=pltpu.VMEM), pl.BlockSpec(memory_space=pl.ANY)
    held = [] if whole is None else [whole]
    return pl.pallas_call(
        functools.partial(unpack_body, fars),
        name="unpack",
        out_shape=shape,
        in_specs=[vmem] * len(blocks) + [hbm] * len(held),
        out_specs=hbm,
        input_output_aliases={len(blocks): 0} if held else {},
        scratch_shapes=[pltpu.SemaphoreType.DMA((len(blocks) * lax.axis_size("line") * TWIN,))],
        compiler_params=pltpu.CompilerParams(vmem_limit_bytes=32 << 20),
        cost_estimate=pl.CostEstimate(flops=0, bytes_accessed=0, transcendentals=0),
    )(*blocks, *held)


def split_runs(tokens, outer):
    tok_rows, width = tokens.shape
    inner = lax.axis_size("line") * lax.axis_size("pair")
    near = SPLIT * TWIN
    cut = tokens.reshape(tok_rows, inner, outer, near, width // (inner * outer * near))
    return cut.transpose(0, 1, 3, 2, 4).reshape(tok_rows, width)


def join_runs(tokens, outer):
    tok_rows, width = tokens.shape
    inner = lax.axis_size("line") * lax.axis_size("pair")
    near = SPLIT * TWIN
    cut = tokens.reshape(tok_rows, inner, near, outer, width // (inner * outer * near))
    return cut.transpose(0, 1, 3, 2, 4).reshape(tok_rows, width)


def parted(block, step):
    line = lax.axis_size("line")
    to = [core * line + (i + (line - step if core else step)) % line for core in range(TWIN) for i in range(line)]
    return lax.ppermute(block, ("twin", "line"), list(enumerate(to)))


def cuts(rows, count):
    unit = math.gcd(rows, 64)
    ends = [-(-rows // unit * i // count) * unit for i in range(count + 1)]
    return list(zip(ends, ends[1:]))


def relay_body(count, *refs):
    rows = jnp.concatenate([ref[...] for ref in refs[:-count]], axis=0)
    for (start, end), out in zip(cuts(rows.shape[0], count), refs[-count:]):
        out[...] = rows[start:end]


def join_body(line, count, *refs):
    both, *pieces, whole = refs
    others = jnp.concatenate([piece[...] for piece in pieces[-count:]], axis=0)
    pieces = pieces[:-count]
    rows = whole.shape[0] // (line * TWIN)
    core = lax.axis_index("twin")

    def put(step, twin_run, piece):
        part = step * TWIN + (twin_run ^ core)
        whole[pl.ds(pl.multiple_of(part * rows, rows), rows), :] = piece

    def put_both(step, piece):
        for twin_run in range(TWIN):
            put(step, twin_run, piece[twin_run * rows : (twin_run + 1) * rows])

    put_both(0, both[...])
    for step in range(1, (line + 1) // 2):
        at = (step - 1) * TWIN * rows
        put_both(jnp.where(core == 0, step, line - step), pieces[step - 1][...])
        put_both(jnp.where(core == 0, line - step, step), others[at : at + TWIN * rows])
    if line % 2 == 0:
        put(line // 2, core, pieces[-1][...])
        put(line // 2, 1 - core, others[others.shape[0] - rows :])


def share_body(*refs):
    *blocks, weight = refs[: len(refs) // 2 + 1]
    outs = refs[len(blocks) + 1 :]
    stacked = jnp.concatenate([block[...] for block in blocks], axis=0)
    product = jnp.dot(stacked, weight[...], preferred_element_type=f32)
    for i, out in enumerate(outs):
        out[...] = product[i * out.shape[0] : (i + 1) * out.shape[0]].astype(out.dtype)


def columns_body(*refs):
    *grads, weight = refs[: len(refs) // 2 + 1]
    outs = refs[len(grads) + 1 :]
    stacked = jnp.concatenate([grad[...] for grad in grads], axis=0)
    product = lax.dot_general(
        stacked, weight[...], (((1,), (1,)), ((), ())), preferred_element_type=f32
    )
    for i, out in enumerate(outs):
        out[...] = product[i * out.shape[0] : (i + 1) * out.shape[0]].astype(out.dtype)


def emit_body(held, out):
    out[...] = held[...]


def norm_body(*refs):
    *shares, cotangent, key_out, key_grad = refs
    for head in range(key_out.shape[1] // HEAD_DIM):
        at = slice(head * HEAD_DIM, (head + 1) * HEAD_DIM)
        raw = sum(share[:, at].astype(f32) for share in shares)
        inverse = lax.rsqrt(jnp.mean(raw * raw, axis=-1, keepdims=True) + epsilon)
        normed = raw * inverse
        upstream = cotangent[:, at].astype(f32)
        projected = jnp.mean(upstream * normed, axis=-1, keepdims=True)
        key_out[:, at] = normed.astype(bf16)
        key_grad[:, at] = (inverse * (upstream - normed * projected)).astype(bf16)


def terms_body(grad_scale, *refs):
    blocks, grads, (kept, *leaving) = refs[:MEMBERS], refs[MEMBERS : 2 * MEMBERS], refs[2 * MEMBERS :]
    tokens = jnp.concatenate([block[...] for block in blocks], axis=0)
    grad = jnp.concatenate([grad[...] for grad in grads], axis=0)
    line, rows, _ = kept.shape
    total = lax.dot_general(tokens, grad, (((0,), (0,)), ((), ())), preferred_element_type=f32)
    total = total * grad_scale
    others = []
    for step in range(line):
        start = step * TWIN * rows
        kept[step] = total[start : start + rows]
        others.append(total[start + rows : start + TWIN * rows].astype(bf16))
    others = jnp.concatenate(others, axis=0)
    for (start, end), piece in zip(cuts(line * rows, len(leaving)), leaving):
        piece[...] = others[start:end]


def merge_body(count, kept, *refs):
    others = jnp.concatenate([piece[...] for piece in refs[:count]], axis=0)
    own, *leaving = refs[count:]
    rows = own.shape[0]
    for step in range(kept.shape[0]):
        piece = kept[step] + others[step * rows : (step + 1) * rows].astype(f32)
        if step == 0:
            own[...] = piece
        else:
            leaving[step - 1][...] = piece.astype(bf16)


def sum_body(*refs):
    refs[-1][...] = sum(ref[...].astype(f32) for ref in refs[:-1])


def per_device(tokens, key_weight, cotangent):
    tok_rows, width = tokens.shape
    shard_rows, key_cols = key_weight.shape
    outer, line = lax.axis_size("outer"), lax.axis_size("line")
    parts = line * TWIN
    rows = shard_rows // (SPLIT * TWIN)
    owned = width // MEMBERS
    grad_scale = 1.0 / math.sqrt(tok_rows * outer * TWIN * MEMBERS * line)
    flops = 2 * tok_rows * owned * key_cols
    shape = jax.ShapeDtypeStruct
    block_shape, head_shape = shape((tok_rows, owned), bf16), shape((tok_rows, key_cols), bf16)
    if outer > 1:
        cut = key_weight.reshape(outer, SPLIT * TWIN, rows // outer, key_cols)
        key_weight = cut.transpose(1, 0, 2, 3).reshape(shard_rows, key_cols)
        tokens = split_runs(tokens, outer)

    both, mine = local_call(
        "front",
        front_body,
        [shape((TWIN * rows, key_cols), bf16), shape((rows, key_cols), bf16)],
        key_weight,
        space=pltpu.HBM,
        scratch=[pltpu.SemaphoreType.DMA((2,))],
        room=53.4,
    )
    packed = local_call("pack", pack_body, [block_shape] * MEMBERS, tokens)
    blocks = [packed[0], None, None, None]
    for far in (3, 1, 2):
        blocks[far] = to_member(packed[far], far)
    passed = [parted(both, step) for step in range(1, (line + 1) // 2)]
    if line % 2 == 0:
        passed.append(rotated(mine, "line", line // 2))
    pieces = [both]
    reach = shard_rows // SPLIT * (line - 1) // TWIN
    relayed = local_call(
        "relay",
        functools.partial(relay_body, 2),
        [shape((end - start, key_cols), bf16) for start, end in cuts(reach, 2)],
        *passed,
        flops=8 * flops,
    )
    theirs = [to_twin(piece) for piece in relayed]
    *blocks, theirs = lax.optimization_barrier((*blocks[::-1], theirs))
    blocks = blocks[::-1]
    weight = local_call(
        "join",
        functools.partial(join_body, line, 2),
        shape((owned, key_cols), bf16),
        both,
        *passed,
        *theirs,
    )

    def share(fars, kind):
        shaped = [shape((tok_rows, key_cols), kind)] * len(fars)
        return local_call("share", share_body, shaped, *[blocks[far] for far in fars], weight, flops=flops)

    order = (3, 1, 2)
    shares = [to_member(part, far) for far, part in zip(order, share(order, bf16))]
    normed, key_grad = local_call("norm", norm_body, [head_shape] * 2, *share((0,), f32), *shares, cotangent)
    key_out = local_call("emit", emit_body, head_shape, normed)

    grad_3, grad_1, grad_2 = (to_member(key_grad, far) for far in (3, 1, 2))

    def columns(*grads):
        return local_call("columns", columns_body, [block_shape] * len(grads), *grads, weight, flops=flops)

    (column_0,), (column_3,) = columns(key_grad), columns(grad_3)
    column_0, column_3, key_out, grad_1, grad_2 = lax.optimization_barrier(
        (column_0, column_3, key_out, grad_1, grad_2)
    )
    kept, *theirs = local_call(
        "terms",
        functools.partial(terms_body, grad_scale),
        [shape((line, rows, key_cols), f32)]
        + [shape((end - start, key_cols), bf16) for start, end in cuts(line * rows, 2)],
        *blocks,
        key_grad,
        grad_1,
        grad_2,
        grad_3,
        moved=0,
    )
    theirs = [to_twin(piece) for piece in theirs]
    sums = local_call(
        "merge",
        functools.partial(merge_body, 2),
        [shape((rows, key_cols), f32)] + [shape((rows, key_cols), bf16)] * (line - 1),
        kept,
        *theirs,
        moved=0,
    )

    met = [sums[0]] + [rotated(sums[step], "line", -step) for step in range(1, line)]
    back_1, back_2 = (to_member(column, far) for far, column in zip((1, 2), columns(grad_1, grad_2)))
    column_3, back_2, _ = lax.optimization_barrier((column_3, back_2, sums))
    back_3 = to_member(column_3, 3)
    input_grad = unpack((0, 1, 2), (column_0, back_1, back_2), shape((tok_rows, width), bf16))
    met, input_grad = lax.optimization_barrier((met, input_grad))
    weight_grad = local_call("final_sum", sum_body, shape((rows, key_cols), f32), *met, flops=24 * flops)
    back_3, weight_grad = lax.optimization_barrier((back_3, weight_grad))
    if outer > 1:
        weight_grad = lax.psum_scatter(weight_grad, "outer", scatter_dimension=0, tiled=True)
    input_grad = unpack((3,), (back_3,), shape((tok_rows, width), bf16), input_grad)
    if outer > 1:
        input_grad = join_runs(input_grad, outer)
    return (key_out, input_grad, weight_grad)


def solution(mesh):
    replicas, group = mesh.shape["dp"], mesh.shape["inner"]
    fine = Mesh(
        mesh.devices.reshape(replicas // (SPLIT * TWIN), SPLIT, TWIN, group // SPLIT, SPLIT),
        ("outer", "side", "twin", "line", "pair"),
    )
    rows = P(("outer", "side", "twin", "line", "pair"), None)
    return jax.shard_map(
        per_device,
        mesh=fine,
        in_specs=(rows, P(("line", "pair"), None), rows),
        out_specs=(rows, rows, P(("line", "pair", "outer", "side", "twin"), None)),
        check_vma=False,
    )
```

```python
import functools
import math

import jax
import jax.numpy as jnp
from jax import lax
from jax.experimental import pallas as pl
from jax.experimental.pallas import tpu as pltpu
from jax.sharding import Mesh, PartitionSpec as P

HEAD_DIM = 128


epsilon = 1e-06

SPLIT = 2
TWIN = 2
MEMBERS = SPLIT * SPLIT
bf16, f32 = jnp.bfloat16, jnp.float32


def local_call(name, body, out_shapes, *args, flops=0, space=pltpu.VMEM, scratch=(), room=32, moved=None):
    vmem = pl.BlockSpec(memory_space=pltpu.VMEM)
    many = isinstance(out_shapes, (list, tuple))
    if moved is None:
        moved = sum(math.prod(a.shape) * a.dtype.itemsize for a in args)
    return pl.pallas_call(
        body,
        name=name,
        out_shape=out_shapes,
        in_specs=[pl.BlockSpec(memory_space=space)] * len(args),
        out_specs=[vmem] * len(out_shapes) if many else vmem,
        scratch_shapes=scratch,
        compiler_params=pltpu.CompilerParams(vmem_limit_bytes=int(room * 2**20)),
        cost_estimate=pl.CostEstimate(flops=flops, bytes_accessed=moved, transcendentals=0),
    )(*args)


def along(block, step):
    return lax.ppermute(block, "line", [(i, i ^ step) for i in range(lax.axis_size("line"))])


def to_twin(block):
    return lax.ppermute(block, "twin", [(0, 1), (1, 0)])


def flips(far):
    return far // SPLIT, far % SPLIT


def to_member(block, far):
    return lax.ppermute(block, ("side", "pair"), [(i, i ^ far) for i in range(MEMBERS)])


def run_of(part, far):
    core = lax.axis_index("twin")
    over, across = flips(far)
    place = lax.axis_index("line") ^ (part // TWIN)
    side, pair = lax.axis_index("side") ^ over, lax.axis_index("pair") ^ across
    return ((place * SPLIT + pair) * SPLIT + side) * TWIN + (core ^ (part % TWIN))


def front_body(shard, both, mine, arrived):
    rows, half = mine.shape[0], both.shape[0]
    first = lax.axis_index("side") * half
    copies = []
    for target, start in ((both, first), (mine, first + lax.axis_index("twin") * rows)):
        source = shard.at[pl.ds(pl.multiple_of(start, rows), target.shape[0])]
        copies.append(pltpu.make_async_copy(source, target, arrived.at[len(copies)]))
    for copy in copies:
        copy.start()
    for copy in copies:
        copy.wait()


def pack_body(tokens, *blocks):
    parts = lax.axis_size("line") * TWIN
    run = blocks[0].shape[1] // parts
    for far, block in enumerate(blocks):
        for part in range(parts):
            start = pl.multiple_of(run_of(part, far) * run, run)
            block[:, part * run : (part + 1) * run] = tokens[:, pl.ds(start, run)]


def unpack_moves(far, block, whole):
    parts = lax.axis_size("line") * TWIN
    run = block.shape[1] // parts
    for part in range(parts):
        start = pl.multiple_of(run_of(part, far) * run, run)
        yield block.at[:, pl.ds(part * run, run)], whole.at[:, pl.ds(start, run)]


def run_copies(moves, done):
    copies = [pltpu.make_async_copy(*move, done.at[i]) for i, move in enumerate(moves)]
    for copy in copies:
        copy.start()
    for copy in copies:
        copy.wait()


def unpack_body(*refs):
    *blocks, whole, done = refs
    run_copies([move for far, block in enumerate(blocks) for move in unpack_moves(far, block, whole)], done)


def finish_body(block, total, _, whole, weight_grad, done):
    run_copies([(total, weight_grad), *unpack_moves(MEMBERS - 1, block, whole)], done)


def placing_call(name, body, out_shapes, blocks, held=()):
    parts = lax.axis_size("line") * TWIN
    return pl.pallas_call(
        body,
        name=name,
        out_shape=out_shapes,
        in_specs=[pl.BlockSpec(memory_space=pltpu.VMEM)] * len(blocks)
        + [pl.BlockSpec(memory_space=pl.ANY)] * len(held),
        out_specs=[pl.BlockSpec(memory_space=pl.ANY)] * len(out_shapes),
        input_output_aliases={len(blocks): 0} if held else {},
        scratch_shapes=[pltpu.SemaphoreType.DMA((len(blocks) * parts,))],
        compiler_params=pltpu.CompilerParams(vmem_limit_bytes=32 << 20),
        cost_estimate=pl.CostEstimate(flops=0, bytes_accessed=0, transcendentals=0),
    )(*blocks, *held)


def split_runs(tokens, outer):
    tok_rows, width = tokens.shape
    inner = lax.axis_size("line") * lax.axis_size("pair")
    near = SPLIT * TWIN
    cut = tokens.reshape(tok_rows, inner, outer, near, width // (inner * outer * near))
    return cut.transpose(0, 1, 3, 2, 4).reshape(tok_rows, width)


def join_runs(tokens, outer):
    tok_rows, width = tokens.shape
    inner = lax.axis_size("line") * lax.axis_size("pair")
    near = SPLIT * TWIN
    cut = tokens.reshape(tok_rows, inner, near, outer, width // (inner * outer * near))
    return cut.transpose(0, 1, 3, 2, 4).reshape(tok_rows, width)


def parted(block, step):
    line = lax.axis_size("line")
    to = [core * line + (i ^ (line - step if core else step)) for core in range(TWIN) for i in range(line)]
    return lax.ppermute(block, ("twin", "line"), list(enumerate(to)))


def cuts(rows, count):
    unit = math.gcd(rows, 64)
    ends = [-(-rows // unit * i // count) * unit for i in range(count + 1)]
    return list(zip(ends, ends[1:]))


def relay_body(count, *refs):
    rows = jnp.concatenate([ref[...] for ref in refs[:-count]], axis=0)
    for (start, end), out in zip(cuts(rows.shape[0], count), refs[-count:]):
        out[...] = rows[start:end]


def join_body(line, count, *refs):
    both, *pieces, whole = refs
    others = jnp.concatenate([piece[...] for piece in pieces[-count:]], axis=0)
    pieces = pieces[:-count]
    rows = whole.shape[0] // (line * TWIN)
    core = lax.axis_index("twin")

    def put(step, twin_run, piece):
        part = step * TWIN + (twin_run ^ core)
        whole[pl.ds(pl.multiple_of(part * rows, rows), rows), :] = piece

    def put_both(step, piece):
        for twin_run in range(TWIN):
            put(step, twin_run, piece[twin_run * rows : (twin_run + 1) * rows])

    put_both(0, both[...])
    for step in range(1, (line + 1) // 2):
        at = (step - 1) * TWIN * rows
        put_both(jnp.where(core == 0, step, line - step), pieces[step - 1][...])
        put_both(jnp.where(core == 0, line - step, step), others[at : at + TWIN * rows])
    if line % 2 == 0:
        put(line // 2, core, pieces[-1][...])
        put(line // 2, 1 - core, others[others.shape[0] - rows :])


def share_body(*refs):
    *blocks, weight = refs[: len(refs) // 2 + 1]
    outs = refs[len(blocks) + 1 :]
    stacked = jnp.concatenate([block[...] for block in blocks], axis=0)
    product = jnp.dot(stacked, weight[...], preferred_element_type=f32)
    for i, out in enumerate(outs):
        out[...] = product[i * out.shape[0] : (i + 1) * out.shape[0]].astype(out.dtype)


def columns_body(*refs):
    *grads, weight = refs[: len(refs) // 2 + 1]
    outs = refs[len(grads) + 1 :]
    stacked = jnp.concatenate([grad[...] for grad in grads], axis=0)
    product = lax.dot_general(
        stacked, weight[...], (((1,), (1,)), ((), ())), preferred_element_type=f32
    )
    for i, out in enumerate(outs):
        out[...] = product[i * out.shape[0] : (i + 1) * out.shape[0]].astype(out.dtype)


def emit_body(held, out):
    out[...] = held[...]


def norm_body(*refs):
    *shares, cotangent, key_out, key_grad = refs
    for head in range(key_out.shape[1] // HEAD_DIM):
        at = slice(head * HEAD_DIM, (head + 1) * HEAD_DIM)
        raw = sum(share[:, at].astype(f32) for share in shares)
        inverse = lax.rsqrt(jnp.mean(raw * raw, axis=-1, keepdims=True) + epsilon)
        normed = raw * inverse
        upstream = cotangent[:, at].astype(f32)
        projected = jnp.mean(upstream * normed, axis=-1, keepdims=True)
        key_out[:, at] = normed.astype(bf16)
        key_grad[:, at] = (inverse * (upstream - normed * projected)).astype(bf16)


def terms_body(grad_scale, *refs):
    blocks, grads, (kept, *leaving) = refs[:MEMBERS], refs[MEMBERS : 2 * MEMBERS], refs[2 * MEMBERS :]
    tokens = jnp.concatenate([block[...] for block in blocks], axis=0)
    grad = jnp.concatenate([grad[...] for grad in grads], axis=0)
    line, rows, _ = kept.shape
    total = lax.dot_general(tokens, grad, (((0,), (0,)), ((), ())), preferred_element_type=f32)
    total = total * grad_scale
    others = []
    for step in range(line):
        start = step * TWIN * rows
        kept[step] = total[start : start + rows]
        others.append(total[start + rows : start + TWIN * rows].astype(bf16))
    others = jnp.concatenate(others, axis=0)
    for (start, end), piece in zip(cuts(line * rows, len(leaving)), leaving):
        piece[...] = others[start:end]


def merge_body(count, kept, *refs):
    others = jnp.concatenate([piece[...] for piece in refs[:count]], axis=0)
    own, *leaving = refs[count:]
    rows = own.shape[0]
    for step in range(kept.shape[0]):
        piece = kept[step] + others[step * rows : (step + 1) * rows].astype(f32)
        if step == 0:
            own[...] = piece
        else:
            leaving[-step][...] = piece.astype(bf16)


def sum_body(*refs):
    refs[-1][...] = sum(ref[...].astype(f32) for ref in refs[:-1])


def per_device(tokens, key_weight, cotangent):
    tok_rows, width = tokens.shape
    shard_rows, key_cols = key_weight.shape
    outer, line = lax.axis_size("outer"), lax.axis_size("line")
    parts = line * TWIN
    rows = shard_rows // (SPLIT * TWIN)
    owned = width // MEMBERS
    grad_scale = 1.0 / math.sqrt(tok_rows * outer * TWIN * MEMBERS * line)
    flops = 2 * tok_rows * owned * key_cols
    shape = jax.ShapeDtypeStruct
    block_shape, head_shape = shape((tok_rows, owned), bf16), shape((tok_rows, key_cols), bf16)
    if outer > 1:
        cut = key_weight.reshape(outer, SPLIT * TWIN, rows // outer, key_cols)
        key_weight = cut.transpose(1, 0, 2, 3).reshape(shard_rows, key_cols)
        tokens = split_runs(tokens, outer)

    both, mine = local_call(
        "front",
        front_body,
        [shape((TWIN * rows, key_cols), bf16), shape((rows, key_cols), bf16)],
        key_weight,
        space=pltpu.HBM,
        scratch=[pltpu.SemaphoreType.DMA((2,))],
        room=53.4,
    )
    packed = local_call("pack", pack_body, [block_shape] * MEMBERS, tokens)
    blocks = [packed[0], None, None, None]
    for far in (3, 1, 2):
        blocks[far] = to_member(packed[far], far)
    passed = [parted(both, step) for step in range(1, (line + 1) // 2)]
    if line % 2 == 0:
        passed.append(along(mine, line // 2))
    pieces = [both]
    reach = shard_rows // SPLIT * (line - 1) // TWIN
    relayed = local_call(
        "relay",
        functools.partial(relay_body, 2),
        [shape((end - start, key_cols), bf16) for start, end in cuts(reach, 2)],
        *passed,
        flops=8 * flops,
    )
    theirs = [to_twin(piece) for piece in relayed]
    *blocks, theirs = lax.optimization_barrier((*blocks[::-1], theirs))
    blocks = blocks[::-1]
    weight = local_call(
        "join",
        functools.partial(join_body, line, 2),
        shape((owned, key_cols), bf16),
        both,
        *passed,
        *theirs,
    )

    def share(fars, kind):
        shaped = [shape((tok_rows, key_cols), kind)] * len(fars)
        return local_call("share", share_body, shaped, *[blocks[far] for far in fars], weight, flops=flops)

    order = (3, 1, 2)
    shares = [to_member(part, far) for far, part in zip(order, share(order, bf16))]
    normed, key_grad = local_call("norm", norm_body, [head_shape] * 2, *share((0,), f32), *shares, cotangent)
    key_out = local_call("emit", emit_body, head_shape, normed)

    grad_3, grad_1, grad_2 = (to_member(key_grad, far) for far in (3, 1, 2))

    def columns(*grads):
        return local_call("columns", columns_body, [block_shape] * len(grads), *grads, weight, flops=flops)

    (column_0,), (column_3,) = columns(key_grad), columns(grad_3)
    column_0, column_3, key_out, grad_1, grad_2 = lax.optimization_barrier(
        (column_0, column_3, key_out, grad_1, grad_2)
    )
    kept, *theirs = local_call(
        "terms",
        functools.partial(terms_body, grad_scale),
        [shape((line, rows, key_cols), f32)]
        + [shape((end - start, key_cols), bf16) for start, end in cuts(line * rows, 2)],
        *blocks,
        key_grad,
        grad_1,
        grad_2,
        grad_3,
        moved=0,
    )
    theirs = [to_twin(piece) for piece in theirs]
    sums = local_call(
        "merge",
        functools.partial(merge_body, 2),
        [shape((rows, key_cols), f32)] + [shape((rows, key_cols), bf16)] * (line - 1),
        kept,
        *theirs,
        moved=0,
    )

    met = [sums[0]] + [along(sums[line - step], step) for step in range(line - 1, 0, -1)]
    back_1, back_2 = (to_member(column, far) for far, column in zip((1, 2), columns(grad_1, grad_2)))
    column_3, back_2, _ = lax.optimization_barrier((column_3, back_2, sums))
    back_3 = to_member(column_3, 3)
    whole_shape = shape((tok_rows, width), bf16)
    (input_grad,) = placing_call("unpack", unpack_body, [whole_shape], (column_0, back_1, back_2))
    met, input_grad = lax.optimization_barrier((met, input_grad))
    total = local_call("final_sum", sum_body, shape((rows, key_cols), f32), *met, flops=24 * flops)
    input_grad, weight_grad = placing_call(
        "finish", finish_body, [whole_shape, shape(total.shape, f32)], (back_3, total), (input_grad,)
    )
    if outer > 1:
        weight_grad = lax.psum_scatter(weight_grad, "outer", scatter_dimension=0, tiled=True)
    if outer > 1:
        input_grad = join_runs(input_grad, outer)
    return (key_out, input_grad, weight_grad)


def solution(mesh):
    replicas, group = mesh.shape["dp"], mesh.shape["inner"]
    fine = Mesh(
        mesh.devices.reshape(replicas // (SPLIT * TWIN), SPLIT, TWIN, group // SPLIT, SPLIT),
        ("outer", "side", "twin", "line", "pair"),
    )
    rows = P(("outer", "side", "twin", "line", "pair"), None)
    return jax.shard_map(
        per_device,
        mesh=fine,
        in_specs=(rows, P(("line", "pair"), None), rows),
        out_specs=(rows, rows, P(("line", "pair", "outer", "side", "twin"), None)),
        check_vma=False,
    )
```

```python
import functools
import math

import jax
import jax.numpy as jnp
from jax import lax
from jax.experimental import pallas as pl
from jax.experimental.pallas import tpu as pltpu
from jax.sharding import Mesh, PartitionSpec as P

HEAD_DIM = 128


epsilon = 1e-06

SPLIT = 2
TWIN = 2
MEMBERS = SPLIT * SPLIT
bf16, f32 = jnp.bfloat16, jnp.float32


def local_call(name, body, out_shapes, *args, flops=0, space=pltpu.VMEM, scratch=(), room=32, moved=None):
    vmem = pl.BlockSpec(memory_space=pltpu.VMEM)
    many = isinstance(out_shapes, (list, tuple))
    if moved is None:
        moved = sum(math.prod(a.shape) * a.dtype.itemsize for a in args)
    return pl.pallas_call(
        body,
        name=name,
        out_shape=out_shapes,
        in_specs=[pl.BlockSpec(memory_space=space)] * len(args),
        out_specs=[vmem] * len(out_shapes) if many else vmem,
        scratch_shapes=scratch,
        compiler_params=pltpu.CompilerParams(vmem_limit_bytes=int(room * 2**20)),
        cost_estimate=pl.CostEstimate(flops=flops, bytes_accessed=moved, transcendentals=0),
    )(*args)


def along(block, step):
    return lax.ppermute(block, "line", [(i, i ^ step) for i in range(lax.axis_size("line"))])


def to_twin(block):
    return lax.ppermute(block, "twin", [(0, 1), (1, 0)])


def flips(far):
    return far // SPLIT, far % SPLIT


def to_member(block, far):
    return lax.ppermute(block, ("side", "pair"), [(i, i ^ far) for i in range(MEMBERS)])


def run_of(part, far):
    core = lax.axis_index("twin")
    over, across = flips(far)
    place = lax.axis_index("line") ^ (part // TWIN)
    side, pair = lax.axis_index("side") ^ over, lax.axis_index("pair") ^ across
    return ((place * SPLIT + pair) * SPLIT + side) * TWIN + (core ^ (part % TWIN))


def front_body(tokens, shard, both, mine, *refs):
    *blocks, arrived = refs
    rows, half = mine.shape[0], both.shape[0]
    first = lax.axis_index("side") * half
    moves = []
    for target, start in ((both, first), (mine, first + lax.axis_index("twin") * rows)):
        moves.append((shard.at[pl.ds(pl.multiple_of(start, rows), target.shape[0])], target))
    parts = lax.axis_size("line") * TWIN
    run = blocks[0].shape[1] // parts
    for far, block in enumerate(blocks):
        for part in range(parts):
            start = pl.multiple_of(run_of(part, far) * run, run)
            moves.append((tokens.at[:, pl.ds(start, run)], block.at[:, pl.ds(part * run, run)]))
    copies = [pltpu.make_async_copy(*move, arrived.at[i]) for i, move in enumerate(moves)]
    for copy in copies:
        copy.start()
    for copy in copies:
        copy.wait()


def unpack_moves(far, block, whole):
    parts = lax.axis_size("line") * TWIN
    run = block.shape[1] // parts
    for part in range(parts):
        start = pl.multiple_of(run_of(part, far) * run, run)
        yield block.at[:, pl.ds(part * run, run)], whole.at[:, pl.ds(start, run)]


def run_copies(moves, done):
    copies = [pltpu.make_async_copy(*move, done.at[i]) for i, move in enumerate(moves)]
    for copy in copies:
        copy.start()
    for copy in copies:
        copy.wait()


def unpack_body(*refs):
    *blocks, whole, done = refs
    run_copies([move for far, block in enumerate(blocks) for move in unpack_moves(far, block, whole)], done)


def finish_body(block, total, _, whole, weight_grad, done):
    run_copies([(total, weight_grad), *unpack_moves(MEMBERS - 1, block, whole)], done)


def placing_call(name, body, out_shapes, blocks, held=()):
    parts = lax.axis_size("line") * TWIN
    return pl.pallas_call(
        body,
        name=name,
        out_shape=out_shapes,
        in_specs=[pl.BlockSpec(memory_space=pltpu.VMEM)] * len(blocks)
        + [pl.BlockSpec(memory_space=pl.ANY)] * len(held),
        out_specs=[pl.BlockSpec(memory_space=pl.ANY)] * len(out_shapes),
        input_output_aliases={len(blocks): 0} if held else {},
        scratch_shapes=[pltpu.SemaphoreType.DMA((len(blocks) * parts,))],
        compiler_params=pltpu.CompilerParams(vmem_limit_bytes=32 << 20),
        cost_estimate=pl.CostEstimate(flops=0, bytes_accessed=0, transcendentals=0),
    )(*blocks, *held)


def split_runs(tokens, outer):
    tok_rows, width = tokens.shape
    inner = lax.axis_size("line") * lax.axis_size("pair")
    near = SPLIT * TWIN
    cut = tokens.reshape(tok_rows, inner, outer, near, width // (inner * outer * near))
    return cut.transpose(0, 1, 3, 2, 4).reshape(tok_rows, width)


def join_runs(tokens, outer):
    tok_rows, width = tokens.shape
    inner = lax.axis_size("line") * lax.axis_size("pair")
    near = SPLIT * TWIN
    cut = tokens.reshape(tok_rows, inner, near, outer, width // (inner * outer * near))
    return cut.transpose(0, 1, 3, 2, 4).reshape(tok_rows, width)


def parted(block, step):
    line = lax.axis_size("line")
    to = [core * line + (i ^ (line - step if core else step)) for core in range(TWIN) for i in range(line)]
    return lax.ppermute(block, ("twin", "line"), list(enumerate(to)))


def cuts(rows, count):
    unit = math.gcd(rows, 64)
    ends = [-(-rows // unit * i // count) * unit for i in range(count + 1)]
    return list(zip(ends, ends[1:]))


def relay_body(count, *refs):
    rows = jnp.concatenate([ref[...] for ref in refs[:-count]], axis=0)
    for (start, end), out in zip(cuts(rows.shape[0], count), refs[-count:]):
        out[...] = rows[start:end]


def join_body(line, count, *refs):
    both, *pieces, whole = refs
    others = jnp.concatenate([piece[...] for piece in pieces[-count:]], axis=0)
    pieces = pieces[:-count]
    rows = whole.shape[0] // (line * TWIN)
    core = lax.axis_index("twin")

    def put(step, twin_run, piece):
        part = step * TWIN + (twin_run ^ core)
        whole[pl.ds(pl.multiple_of(part * rows, rows), rows), :] = piece

    def put_both(step, piece):
        for twin_run in range(TWIN):
            put(step, twin_run, piece[twin_run * rows : (twin_run + 1) * rows])

    put_both(0, both[...])
    for step in range(1, (line + 1) // 2):
        at = (step - 1) * TWIN * rows
        put_both(jnp.where(core == 0, step, line - step), pieces[step - 1][...])
        put_both(jnp.where(core == 0, line - step, step), others[at : at + TWIN * rows])
    if line % 2 == 0:
        put(line // 2, core, pieces[-1][...])
        put(line // 2, 1 - core, others[others.shape[0] - rows :])


def share_body(*refs):
    *blocks, weight = refs[: len(refs) // 2 + 1]
    outs = refs[len(blocks) + 1 :]
    stacked = jnp.concatenate([block[...] for block in blocks], axis=0)
    product = jnp.dot(stacked, weight[...], preferred_element_type=f32)
    for i, out in enumerate(outs):
        out[...] = product[i * out.shape[0] : (i + 1) * out.shape[0]].astype(out.dtype)


def columns_body(*refs):
    *grads, weight = refs[: len(refs) // 2 + 1]
    outs = refs[len(grads) + 1 :]
    stacked = jnp.concatenate([grad[...] for grad in grads], axis=0)
    product = lax.dot_general(
        stacked, weight[...], (((1,), (1,)), ((), ())), preferred_element_type=f32
    )
    for i, out in enumerate(outs):
        out[...] = product[i * out.shape[0] : (i + 1) * out.shape[0]].astype(out.dtype)


def emit_body(held, out):
    out[...] = held[...]


def norm_body(*refs):
    *shares, cotangent, key_out, key_grad = refs
    for head in range(key_out.shape[1] // HEAD_DIM):
        at = slice(head * HEAD_DIM, (head + 1) * HEAD_DIM)
        raw = sum(share[:, at].astype(f32) for share in shares)
        inverse = lax.rsqrt(jnp.mean(raw * raw, axis=-1, keepdims=True) + epsilon)
        normed = raw * inverse
        upstream = cotangent[:, at].astype(f32)
        projected = jnp.mean(upstream * normed, axis=-1, keepdims=True)
        key_out[:, at] = normed.astype(bf16)
        key_grad[:, at] = (inverse * (upstream - normed * projected)).astype(bf16)


def terms_body(grad_scale, *refs):
    blocks, grads, (kept, *leaving) = refs[:MEMBERS], refs[MEMBERS : 2 * MEMBERS], refs[2 * MEMBERS :]
    tokens = jnp.concatenate([block[...] for block in blocks], axis=0)
    grad = jnp.concatenate([grad[...] for grad in grads], axis=0)
    line, rows, _ = kept.shape
    total = lax.dot_general(tokens, grad, (((0,), (0,)), ((), ())), preferred_element_type=f32)
    total = total * grad_scale
    others = []
    for step in range(line):
        start = step * TWIN * rows
        kept[step] = total[start : start + rows]
        others.append(total[start + rows : start + TWIN * rows].astype(bf16))
    others = jnp.concatenate(others, axis=0)
    for (start, end), piece in zip(cuts(line * rows, len(leaving)), leaving):
        piece[...] = others[start:end]


def merge_body(count, kept, *refs):
    others = jnp.concatenate([piece[...] for piece in refs[:count]], axis=0)
    own, *leaving = refs[count:]
    rows = own.shape[0]
    for step in range(kept.shape[0]):
        piece = kept[step] + others[step * rows : (step + 1) * rows].astype(f32)
        if step == 0:
            own[...] = piece
        else:
            leaving[-step][...] = piece.astype(bf16)


def sum_body(*refs):
    refs[-1][...] = sum(ref[...].astype(f32) for ref in refs[:-1])


def per_device(tokens, key_weight, cotangent):
    tok_rows, width = tokens.shape
    shard_rows, key_cols = key_weight.shape
    outer, line = lax.axis_size("outer"), lax.axis_size("line")
    parts = line * TWIN
    rows = shard_rows // (SPLIT * TWIN)
    owned = width // MEMBERS
    grad_scale = 1.0 / math.sqrt(tok_rows * outer * TWIN * MEMBERS * line)
    flops = 2 * tok_rows * owned * key_cols
    shape = jax.ShapeDtypeStruct
    block_shape, head_shape = shape((tok_rows, owned), bf16), shape((tok_rows, key_cols), bf16)
    if outer > 1:
        cut = key_weight.reshape(outer, SPLIT * TWIN, rows // outer, key_cols)
        key_weight = cut.transpose(1, 0, 2, 3).reshape(shard_rows, key_cols)
        tokens = split_runs(tokens, outer)

    both, mine, *packed = local_call(
        "front",
        front_body,
        [shape((TWIN * rows, key_cols), bf16), shape((rows, key_cols), bf16)] + [block_shape] * MEMBERS,
        tokens,
        key_weight,
        space=pltpu.HBM,
        room=53,
        scratch=[pltpu.SemaphoreType.DMA((2 + MEMBERS * parts,))],
    )
    blocks = [packed[0], None, None, None]
    for far in (3, 1, 2):
        blocks[far] = to_member(packed[far], far)
    passed = [parted(both, step) for step in range(1, (line + 1) // 2)]
    if line % 2 == 0:
        passed.append(along(mine, line // 2))
    pieces = [both]
    reach = shard_rows // SPLIT * (line - 1) // TWIN
    blocks[3], *passed = lax.optimization_barrier((blocks[3], *passed))
    relayed = local_call(
        "relay",
        functools.partial(relay_body, 2),
        [shape((end - start, key_cols), bf16) for start, end in cuts(reach, 2)],
        *passed,
        flops=8 * flops,
    )
    theirs = [to_twin(piece) for piece in relayed]
    *blocks, theirs = lax.optimization_barrier((*blocks[::-1], theirs))
    blocks = blocks[::-1]
    weight = local_call(
        "join",
        functools.partial(join_body, line, 2),
        shape((owned, key_cols), bf16),
        both,
        *passed,
        *theirs,
    )

    def share(fars, kind):
        shaped = [shape((tok_rows, key_cols), kind)] * len(fars)
        return local_call("share", share_body, shaped, *[blocks[far] for far in fars], weight, flops=flops)

    order = (3, 1, 2)
    shares = [to_member(part, far) for far, part in zip(order, share(order, bf16))]
    normed, key_grad = local_call("norm", norm_body, [head_shape] * 2, *share((0,), f32), *shares, cotangent)
    key_out = local_call("emit", emit_body, head_shape, normed)

    grad_3, grad_1, grad_2 = (to_member(key_grad, far) for far in (3, 1, 2))

    def columns(*grads):
        return local_call("columns", columns_body, [block_shape] * len(grads), *grads, weight, flops=flops)

    (column_0,), (column_3,) = columns(key_grad), columns(grad_3)
    column_0, column_3, key_out, grad_1, grad_2 = lax.optimization_barrier(
        (column_0, column_3, key_out, grad_1, grad_2)
    )
    kept, *theirs = local_call(
        "terms",
        functools.partial(terms_body, grad_scale),
        [shape((line, rows, key_cols), f32)]
        + [shape((end - start, key_cols), bf16) for start, end in cuts(line * rows, 2)],
        *blocks,
        key_grad,
        grad_1,
        grad_2,
        grad_3,
        moved=0,
    )
    theirs = [to_twin(piece) for piece in theirs]
    sums = local_call(
        "merge",
        functools.partial(merge_body, 2),
        [shape((rows, key_cols), f32)] + [shape((rows, key_cols), bf16)] * (line - 1),
        kept,
        *theirs,
        moved=0,
    )

    met = [sums[0]] + [along(sums[line - step], step) for step in range(line - 1, 0, -1)]
    back_1, back_2 = (to_member(column, far) for far, column in zip((1, 2), columns(grad_1, grad_2)))
    column_3, back_2, _ = lax.optimization_barrier((column_3, back_2, sums))
    back_3 = to_member(column_3, 3)
    whole_shape = shape((tok_rows, width), bf16)
    (input_grad,) = placing_call("unpack", unpack_body, [whole_shape], (column_0, back_1, back_2))
    met, input_grad = lax.optimization_barrier((met, input_grad))
    total = local_call("final_sum", sum_body, shape((rows, key_cols), f32), *met, flops=24 * flops)
    input_grad, weight_grad = placing_call(
        "finish", finish_body, [whole_shape, shape(total.shape, f32)], (back_3, total), (input_grad,)
    )
    if outer > 1:
        weight_grad = lax.psum_scatter(weight_grad, "outer", scatter_dimension=0, tiled=True)
    if outer > 1:
        input_grad = join_runs(input_grad, outer)
    return (key_out, input_grad, weight_grad)


def solution(mesh):
    replicas, group = mesh.shape["dp"], mesh.shape["inner"]
    fine = Mesh(
        mesh.devices.reshape(replicas // (SPLIT * TWIN), SPLIT, TWIN, group // SPLIT, SPLIT),
        ("outer", "side", "twin", "line", "pair"),
    )
    rows = P(("outer", "side", "twin", "line", "pair"), None)
    return jax.shard_map(
        per_device,
        mesh=fine,
        in_specs=(rows, P(("line", "pair"), None), rows),
        out_specs=(rows, rows, P(("line", "pair", "outer", "side", "twin"), None)),
        check_vma=False,
    )
```

```python
import functools
import math

import jax
import jax.numpy as jnp
from jax import lax
from jax.experimental import pallas as pl
from jax.experimental.pallas import tpu as pltpu
from jax.sharding import Mesh, PartitionSpec as P

HEAD_DIM = 128


epsilon = 1e-06

SPLIT = 2
TWIN = 2
MEMBERS = SPLIT * SPLIT
bf16, f32 = jnp.bfloat16, jnp.float32


def local_call(name, body, out_shapes, *args, flops=0, space=pltpu.VMEM, scratch=(), room=32, moved=None):
    vmem = pl.BlockSpec(memory_space=pltpu.VMEM)
    many = isinstance(out_shapes, (list, tuple))
    if moved is None:
        moved = sum(math.prod(a.shape) * a.dtype.itemsize for a in args)
    return pl.pallas_call(
        body,
        name=name,
        out_shape=out_shapes,
        in_specs=[pl.BlockSpec(memory_space=space)] * len(args),
        out_specs=[vmem] * len(out_shapes) if many else vmem,
        scratch_shapes=scratch,
        compiler_params=pltpu.CompilerParams(vmem_limit_bytes=int(room * 2**20)),
        cost_estimate=pl.CostEstimate(flops=flops, bytes_accessed=moved, transcendentals=0),
    )(*args)


def along(block, step):
    return lax.ppermute(block, "line", [(i, i ^ step) for i in range(lax.axis_size("line"))])


def to_twin(block):
    return lax.ppermute(block, "twin", [(0, 1), (1, 0)])


def flips(far):
    return far // SPLIT, far % SPLIT


def to_member(block, far):
    return lax.ppermute(block, ("side", "pair"), [(i, i ^ far) for i in range(MEMBERS)])


def run_of(part, far):
    core = lax.axis_index("twin")
    over, across = flips(far)
    place = lax.axis_index("line") ^ (part // TWIN)
    side, pair = lax.axis_index("side") ^ over, lax.axis_index("pair") ^ across
    return ((place * SPLIT + pair) * SPLIT + side) * TWIN + (core ^ (part % TWIN))


def front_body(tokens, shard, both, mine, *refs):
    *blocks, arrived = refs
    rows, half = mine.shape[0], both.shape[0]
    first = lax.axis_index("side") * half
    moves = []
    for target, start in ((both, first), (mine, first + lax.axis_index("twin") * rows)):
        moves.append((shard.at[pl.ds(pl.multiple_of(start, rows), target.shape[0])], target))
    parts = lax.axis_size("line") * TWIN
    run = blocks[0].shape[1] // parts
    for far, block in enumerate(blocks):
        for part in range(parts):
            start = pl.multiple_of(run_of(part, far) * run, run)
            moves.append((tokens.at[:, pl.ds(start, run)], block.at[:, pl.ds(part * run, run)]))
    copies = [pltpu.make_async_copy(*move, arrived.at[i]) for i, move in enumerate(moves)]
    for copy in copies:
        copy.start()
    for copy in copies:
        copy.wait()


def unpack_moves(far, block, whole):
    parts = lax.axis_size("line") * TWIN
    run = block.shape[1] // parts
    for part in range(parts):
        start = pl.multiple_of(run_of(part, far) * run, run)
        yield block.at[:, pl.ds(part * run, run)], whole.at[:, pl.ds(start, run)]


def run_copies(moves, done):
    copies = [pltpu.make_async_copy(*move, done.at[i]) for i, move in enumerate(moves)]
    for copy in copies:
        copy.start()
    for copy in copies:
        copy.wait()


def unpack_body(*refs):
    *blocks, whole, done = refs
    run_copies([move for far, block in enumerate(blocks) for move in unpack_moves(far, block, whole)], done)


def finish_body(block, total, _, whole, weight_grad, done):
    run_copies([(total, weight_grad), *unpack_moves(MEMBERS - 1, block, whole)], done)


def placing_call(name, body, out_shapes, blocks, held=()):
    parts = lax.axis_size("line") * TWIN
    return pl.pallas_call(
        body,
        name=name,
        out_shape=out_shapes,
        in_specs=[pl.BlockSpec(memory_space=pltpu.VMEM)] * len(blocks)
        + [pl.BlockSpec(memory_space=pl.ANY)] * len(held),
        out_specs=[pl.BlockSpec(memory_space=pl.ANY)] * len(out_shapes),
        input_output_aliases={len(blocks): 0} if held else {},
        scratch_shapes=[pltpu.SemaphoreType.DMA((len(blocks) * parts,))],
        compiler_params=pltpu.CompilerParams(vmem_limit_bytes=32 << 20),
        cost_estimate=pl.CostEstimate(flops=0, bytes_accessed=0, transcendentals=0),
    )(*blocks, *held)


def split_runs(tokens, outer):
    tok_rows, width = tokens.shape
    inner = lax.axis_size("line") * lax.axis_size("pair")
    near = SPLIT * TWIN
    cut = tokens.reshape(tok_rows, inner, outer, near, width // (inner * outer * near))
    return cut.transpose(0, 1, 3, 2, 4).reshape(tok_rows, width)


def join_runs(tokens, outer):
    tok_rows, width = tokens.shape
    inner = lax.axis_size("line") * lax.axis_size("pair")
    near = SPLIT * TWIN
    cut = tokens.reshape(tok_rows, inner, near, outer, width // (inner * outer * near))
    return cut.transpose(0, 1, 3, 2, 4).reshape(tok_rows, width)


def parted(block, step):
    line = lax.axis_size("line")
    to = [core * line + (i ^ (line - step if core else step)) for core in range(TWIN) for i in range(line)]
    return lax.ppermute(block, ("twin", "line"), list(enumerate(to)))


def cuts(rows, count):
    unit = math.gcd(rows, 64)
    ends = [-(-rows // unit * i // count) * unit for i in range(count + 1)]
    return list(zip(ends, ends[1:]))


def relay_body(count, *refs):
    rows = jnp.concatenate([ref[...] for ref in refs[:-count]], axis=0)
    for (start, end), out in zip(cuts(rows.shape[0], count), refs[-count:]):
        out[...] = rows[start:end]


def join_body(line, count, *refs):
    both, *pieces, whole = refs
    others = jnp.concatenate([piece[...] for piece in pieces[-count:]], axis=0)
    pieces = pieces[:-count]
    rows = whole.shape[0] // (line * TWIN)
    core = lax.axis_index("twin")

    def put(step, twin_run, piece):
        part = step * TWIN + (twin_run ^ core)
        whole[pl.ds(pl.multiple_of(part * rows, rows), rows), :] = piece

    def put_both(step, piece):
        for twin_run in range(TWIN):
            put(step, twin_run, piece[twin_run * rows : (twin_run + 1) * rows])

    put_both(0, both[...])
    for step in range(1, (line + 1) // 2):
        at = (step - 1) * TWIN * rows
        put_both(jnp.where(core == 0, step, line - step), pieces[step - 1][...])
        put_both(jnp.where(core == 0, line - step, step), others[at : at + TWIN * rows])
    if line % 2 == 0:
        put(line // 2, core, pieces[-1][...])
        put(line // 2, 1 - core, others[others.shape[0] - rows :])


def share_body(*refs):
    *blocks, weight = refs[: len(refs) // 2 + 1]
    outs = refs[len(blocks) + 1 :]
    stacked = jnp.concatenate([block[...] for block in blocks], axis=0)
    product = jnp.dot(stacked, weight[...], preferred_element_type=f32)
    for i, out in enumerate(outs):
        out[...] = product[i * out.shape[0] : (i + 1) * out.shape[0]].astype(out.dtype)


def columns_body(*refs):
    *grads, weight = refs[: len(refs) // 2 + 1]
    outs = refs[len(grads) + 1 :]
    stacked = jnp.concatenate([grad[...] for grad in grads], axis=0)
    product = lax.dot_general(
        stacked, weight[...], (((1,), (1,)), ((), ())), preferred_element_type=f32
    )
    for i, out in enumerate(outs):
        out[...] = product[i * out.shape[0] : (i + 1) * out.shape[0]].astype(out.dtype)


def emit_body(held, out):
    out[...] = held[...]


def norm_body(*refs):
    *shares, cotangent, key_out, key_grad = refs
    for head in range(key_out.shape[1] // HEAD_DIM):
        at = slice(head * HEAD_DIM, (head + 1) * HEAD_DIM)
        raw = sum(share[:, at].astype(f32) for share in shares)
        inverse = lax.rsqrt(jnp.mean(raw * raw, axis=-1, keepdims=True) + epsilon)
        normed = raw * inverse
        upstream = cotangent[:, at].astype(f32)
        projected = jnp.mean(upstream * normed, axis=-1, keepdims=True)
        key_out[:, at] = normed.astype(bf16)
        key_grad[:, at] = (inverse * (upstream - normed * projected)).astype(bf16)


def terms_body(grad_scale, *refs):
    blocks, grads, (kept, *leaving) = refs[:MEMBERS], refs[MEMBERS : 2 * MEMBERS], refs[2 * MEMBERS :]
    tokens = jnp.concatenate([block[...] for block in blocks], axis=0)
    grad = jnp.concatenate([grad[...] for grad in grads], axis=0)
    line, rows, _ = kept.shape
    total = lax.dot_general(tokens, grad, (((0,), (0,)), ((), ())), preferred_element_type=f32)
    total = total * grad_scale
    others = []
    for step in range(line):
        start = step * TWIN * rows
        kept[step] = total[start : start + rows]
        others.append(total[start + rows : start + TWIN * rows].astype(bf16))
    others = jnp.concatenate(others, axis=0)
    for (start, end), piece in zip(cuts(line * rows, len(leaving)), leaving):
        piece[...] = others[start:end]


def merge_body(count, kept, *refs):
    others = jnp.concatenate([piece[...] for piece in refs[:count]], axis=0)
    own, *leaving = refs[count:]
    rows = own.shape[0]
    for step in range(kept.shape[0]):
        piece = kept[step] + others[step * rows : (step + 1) * rows].astype(f32)
        if step == 0:
            own[...] = piece
        else:
            leaving[-step][...] = piece.astype(bf16)


def sum_body(*refs):
    refs[-1][...] = sum(ref[...].astype(f32) for ref in refs[:-1])


def per_device(tokens, key_weight, cotangent):
    tok_rows, width = tokens.shape
    shard_rows, key_cols = key_weight.shape
    outer, line = lax.axis_size("outer"), lax.axis_size("line")
    parts = line * TWIN
    rows = shard_rows // (SPLIT * TWIN)
    owned = width // MEMBERS
    grad_scale = 1.0 / math.sqrt(tok_rows * outer * TWIN * MEMBERS * line)
    flops = 2 * tok_rows * owned * key_cols
    shape = jax.ShapeDtypeStruct
    block_shape, head_shape = shape((tok_rows, owned), bf16), shape((tok_rows, key_cols), bf16)
    if outer > 1:
        cut = key_weight.reshape(outer, SPLIT * TWIN, rows // outer, key_cols)
        key_weight = cut.transpose(1, 0, 2, 3).reshape(shard_rows, key_cols)
        tokens = split_runs(tokens, outer)

    both, mine, *packed = local_call(
        "front",
        front_body,
        [shape((TWIN * rows, key_cols), bf16), shape((rows, key_cols), bf16)] + [block_shape] * MEMBERS,
        tokens,
        key_weight,
        space=pltpu.HBM,
        room=53,
        scratch=[pltpu.SemaphoreType.DMA((2 + MEMBERS * parts,))],
    )
    blocks = [packed[0], None, None, None]
    for far in (3, 1, 2):
        blocks[far] = to_member(packed[far], far)
    passed = [parted(both, step) for step in range(1, (line + 1) // 2)]
    if line % 2 == 0:
        passed.append(along(mine, line // 2))
    pieces = [both]
    reach = shard_rows // SPLIT * (line - 1) // TWIN
    blocks[3], *passed = lax.optimization_barrier((blocks[3], *passed))
    relayed = local_call(
        "relay",
        functools.partial(relay_body, 2),
        [shape((end - start, key_cols), bf16) for start, end in cuts(reach, 2)],
        *passed,
        flops=8 * flops,
    )
    theirs = [to_twin(piece) for piece in relayed]
    *blocks, theirs = lax.optimization_barrier((*blocks[::-1], theirs))
    blocks = blocks[::-1]
    weight = local_call(
        "join",
        functools.partial(join_body, line, 2),
        shape((owned, key_cols), bf16),
        both,
        *passed,
        *theirs,
    )

    def share(fars, kind):
        shaped = [shape((tok_rows, key_cols), kind)] * len(fars)
        return local_call("share", share_body, shaped, *[blocks[far] for far in fars], weight, flops=flops)

    order = (3, 1, 2)
    shares = [to_member(part, far) for far, part in zip(order, share(order, bf16))]
    normed, key_grad = local_call("norm", norm_body, [head_shape] * 2, *share((0,), f32), *shares, cotangent)
    key_out = local_call("emit", emit_body, head_shape, normed)

    grad_3, grad_1, grad_2 = (to_member(key_grad, far) for far in (3, 1, 2))

    def columns(*grads):
        return local_call("columns", columns_body, [block_shape] * len(grads), *grads, weight, flops=flops)

    (column_0,), (column_3,) = columns(key_grad), columns(grad_3)
    column_0, column_3, key_out, grad_1, grad_2 = lax.optimization_barrier(
        (column_0, column_3, key_out, grad_1, grad_2)
    )
    kept, *theirs = local_call(
        "terms",
        functools.partial(terms_body, grad_scale),
        [shape((line, rows, key_cols), f32)]
        + [shape((end - start, key_cols), bf16) for start, end in cuts(line * rows, 2)],
        *blocks,
        key_grad,
        grad_1,
        grad_2,
        grad_3,
        moved=0,
    )
    theirs = [to_twin(piece) for piece in theirs]
    sums = local_call(
        "merge",
        functools.partial(merge_body, 2),
        [shape((rows, key_cols), f32)] + [shape((rows, key_cols), bf16)] * (line - 1),
        kept,
        *theirs,
        moved=0,
    )

    back_1, back_2 = (to_member(column, far) for far, column in zip((1, 2), columns(grad_1, grad_2)))
    column_3, _ = lax.optimization_barrier((column_3, sums))
    back_3 = to_member(column_3, 3)
    *sums, closest = sums
    closest, back_2 = lax.optimization_barrier((closest, back_2))
    met = [sums[0]] + [along(piece, line - i) for i, piece in enumerate(sums) if i]
    whole_shape = shape((tok_rows, width), bf16)
    (input_grad,) = placing_call("unpack", unpack_body, [whole_shape], (column_0, back_1, back_2))
    met, input_grad = lax.optimization_barrier((met, input_grad))
    sum_shape = shape((rows, key_cols), f32)
    far_sum = local_call("far_sum", sum_body, sum_shape, *met, flops=24 * flops)
    total = local_call("final_sum", sum_body, sum_shape, far_sum, along(closest, 1), moved=0)
    input_grad, weight_grad = placing_call(
        "finish", finish_body, [whole_shape, shape(total.shape, f32)], (back_3, total), (input_grad,)
    )
    if outer > 1:
        weight_grad = lax.psum_scatter(weight_grad, "outer", scatter_dimension=0, tiled=True)
    if outer > 1:
        input_grad = join_runs(input_grad, outer)
    return (key_out, input_grad, weight_grad)


def solution(mesh):
    replicas, group = mesh.shape["dp"], mesh.shape["inner"]
    fine = Mesh(
        mesh.devices.reshape(replicas // (SPLIT * TWIN), SPLIT, TWIN, group // SPLIT, SPLIT),
        ("outer", "side", "twin", "line", "pair"),
    )
    rows = P(("outer", "side", "twin", "line", "pair"), None)
    return jax.shard_map(
        per_device,
        mesh=fine,
        in_specs=(rows, P(("line", "pair"), None), rows),
        out_specs=(rows, rows, P(("line", "pair", "outer", "side", "twin"), None)),
        check_vma=False,
    )
```

```python
import functools
import math

import jax
import jax.numpy as jnp
from jax import lax
from jax.experimental import pallas as pl
from jax.experimental.pallas import tpu as pltpu
from jax.sharding import Mesh, PartitionSpec as P

HEAD_DIM = 128


epsilon = 1e-06

SPLIT = 2
TWIN = 2
MEMBERS = SPLIT * SPLIT
bf16, f32 = jnp.bfloat16, jnp.float32


def local_call(name, body, out_shapes, *args, flops=0, space=pltpu.VMEM, scratch=(), room=32, moved=None):
    vmem = pl.BlockSpec(memory_space=pltpu.VMEM)
    many = isinstance(out_shapes, (list, tuple))
    if moved is None:
        moved = sum(math.prod(a.shape) * a.dtype.itemsize for a in args)
    return pl.pallas_call(
        body,
        name=name,
        out_shape=out_shapes,
        in_specs=[pl.BlockSpec(memory_space=space)] * len(args),
        out_specs=[vmem] * len(out_shapes) if many else vmem,
        scratch_shapes=scratch,
        compiler_params=pltpu.CompilerParams(vmem_limit_bytes=int(room * 2**20)),
        cost_estimate=pl.CostEstimate(flops=flops, bytes_accessed=moved, transcendentals=0),
    )(*args)


def along(block, step):
    return lax.ppermute(block, "line", [(i, i ^ step) for i in range(lax.axis_size("line"))])


def to_twin(block):
    return lax.ppermute(block, "twin", [(0, 1), (1, 0)])


def flips(far):
    return far // SPLIT, far % SPLIT


def to_member(block, far):
    return lax.ppermute(block, ("side", "pair"), [(i, i ^ far) for i in range(MEMBERS)])


def run_of(part, far):
    core = lax.axis_index("twin")
    over, across = flips(far)
    place = lax.axis_index("line") ^ (part // TWIN)
    side, pair = lax.axis_index("side") ^ over, lax.axis_index("pair") ^ across
    return ((place * SPLIT + pair) * SPLIT + side) * TWIN + (core ^ (part % TWIN))


def front_body(tokens, shard, both, mine, *refs):
    *blocks, arrived = refs
    rows, half = mine.shape[0], both.shape[0]
    first = lax.axis_index("side") * half
    moves = []
    for target, start in ((both, first), (mine, first + lax.axis_index("twin") * rows)):
        moves.append((shard.at[pl.ds(pl.multiple_of(start, rows), target.shape[0])], target))
    parts = lax.axis_size("line") * TWIN
    run = blocks[0].shape[1] // parts
    for far, block in enumerate(blocks):
        for part in range(parts):
            start = pl.multiple_of(run_of(part, far) * run, run)
            moves.append((tokens.at[:, pl.ds(start, run)], block.at[:, pl.ds(part * run, run)]))
    copies = [pltpu.make_async_copy(*move, arrived.at[i]) for i, move in enumerate(moves)]
    for copy in copies:
        copy.start()
    for copy in copies:
        copy.wait()


def unpack_moves(far, block, whole):
    parts = lax.axis_size("line") * TWIN
    run = block.shape[1] // parts
    for part in range(parts):
        start = pl.multiple_of(run_of(part, far) * run, run)
        yield block.at[:, pl.ds(part * run, run)], whole.at[:, pl.ds(start, run)]


def run_copies(moves, done):
    copies = [pltpu.make_async_copy(*move, done.at[i]) for i, move in enumerate(moves)]
    for copy in copies:
        copy.start()
    for copy in copies:
        copy.wait()


def unpack_body(fars, *refs):
    *blocks, whole, done = refs
    run_copies([move for far, block in zip(fars, blocks) for move in unpack_moves(far, block, whole)], done)


def finish_body(fars, *refs):
    *blocks, total, _, whole, weight_grad, done = refs
    moves = [move for far, block in zip(fars, blocks) for move in unpack_moves(far, block, whole)]
    run_copies([(total, weight_grad), *moves], done)


def placing_call(name, body, out_shapes, blocks, held=()):
    parts = lax.axis_size("line") * TWIN
    return pl.pallas_call(
        body,
        name=name,
        out_shape=out_shapes,
        in_specs=[pl.BlockSpec(memory_space=pltpu.VMEM)] * len(blocks)
        + [pl.BlockSpec(memory_space=pl.ANY)] * len(held),
        out_specs=[pl.BlockSpec(memory_space=pl.ANY)] * len(out_shapes),
        input_output_aliases={len(blocks): 0} if held else {},
        scratch_shapes=[pltpu.SemaphoreType.DMA((len(blocks) * parts,))],
        compiler_params=pltpu.CompilerParams(vmem_limit_bytes=32 << 20),
        cost_estimate=pl.CostEstimate(flops=0, bytes_accessed=0, transcendentals=0),
    )(*blocks, *held)


def split_runs(tokens, outer):
    tok_rows, width = tokens.shape
    inner = lax.axis_size("line") * lax.axis_size("pair")
    near = SPLIT * TWIN
    cut = tokens.reshape(tok_rows, inner, outer, near, width // (inner * outer * near))
    return cut.transpose(0, 1, 3, 2, 4).reshape(tok_rows, width)


def join_runs(tokens, outer):
    tok_rows, width = tokens.shape
    inner = lax.axis_size("line") * lax.axis_size("pair")
    near = SPLIT * TWIN
    cut = tokens.reshape(tok_rows, inner, near, outer, width // (inner * outer * near))
    return cut.transpose(0, 1, 3, 2, 4).reshape(tok_rows, width)


def parted(block, step):
    line = lax.axis_size("line")
    to = [core * line + (i ^ (line - step if core else step)) for core in range(TWIN) for i in range(line)]
    return lax.ppermute(block, ("twin", "line"), list(enumerate(to)))


def cuts(rows, count):
    unit = math.gcd(rows, 64)
    ends = [-(-rows // unit * i // count) * unit for i in range(count + 1)]
    return list(zip(ends, ends[1:]))


def relay_body(count, *refs):
    rows = jnp.concatenate([ref[...] for ref in refs[:-count]], axis=0)
    for (start, end), out in zip(cuts(rows.shape[0], count), refs[-count:]):
        out[...] = rows[start:end]


def join_body(line, count, *refs):
    both, *pieces, whole = refs
    others = jnp.concatenate([piece[...] for piece in pieces[-count:]], axis=0)
    pieces = pieces[:-count]
    rows = whole.shape[0] // (line * TWIN)
    core = lax.axis_index("twin")

    def put(step, twin_run, piece):
        part = step * TWIN + (twin_run ^ core)
        whole[pl.ds(pl.multiple_of(part * rows, rows), rows), :] = piece

    def put_both(step, piece):
        for twin_run in range(TWIN):
            put(step, twin_run, piece[twin_run * rows : (twin_run + 1) * rows])

    put_both(0, both[...])
    for step in range(1, (line + 1) // 2):
        at = (step - 1) * TWIN * rows
        put_both(jnp.where(core == 0, step, line - step), pieces[step - 1][...])
        put_both(jnp.where(core == 0, line - step, step), others[at : at + TWIN * rows])
    if line % 2 == 0:
        put(line // 2, core, pieces[-1][...])
        put(line // 2, 1 - core, others[others.shape[0] - rows :])


def share_body(*refs):
    *blocks, weight = refs[: len(refs) // 2 + 1]
    outs = refs[len(blocks) + 1 :]
    stacked = jnp.concatenate([block[...] for block in blocks], axis=0)
    product = jnp.dot(stacked, weight[...], preferred_element_type=f32)
    for i, out in enumerate(outs):
        out[...] = product[i * out.shape[0] : (i + 1) * out.shape[0]].astype(out.dtype)


def columns_body(*refs):
    *grads, weight = refs[: len(refs) // 2 + 1]
    outs = refs[len(grads) + 1 :]
    stacked = jnp.concatenate([grad[...] for grad in grads], axis=0)
    product = lax.dot_general(
        stacked, weight[...], (((1,), (1,)), ((), ())), preferred_element_type=f32
    )
    for i, out in enumerate(outs):
        out[...] = product[i * out.shape[0] : (i + 1) * out.shape[0]].astype(out.dtype)


def emit_body(held, out):
    out[...] = held[...]


def norm_body(*refs):
    *shares, cotangent, key_out, key_grad = refs
    for head in range(key_out.shape[1] // HEAD_DIM):
        at = slice(head * HEAD_DIM, (head + 1) * HEAD_DIM)
        raw = sum(share[:, at].astype(f32) for share in shares)
        inverse = lax.rsqrt(jnp.mean(raw * raw, axis=-1, keepdims=True) + epsilon)
        normed = raw * inverse
        upstream = cotangent[:, at].astype(f32)
        projected = jnp.mean(upstream * normed, axis=-1, keepdims=True)
        key_out[:, at] = normed.astype(bf16)
        key_grad[:, at] = (inverse * (upstream - normed * projected)).astype(bf16)


def terms_body(grad_scale, *refs):
    blocks, grads, (kept, *leaving) = refs[:MEMBERS], refs[MEMBERS : 2 * MEMBERS], refs[2 * MEMBERS :]
    tokens = jnp.concatenate([block[...] for block in blocks], axis=0)
    grad = jnp.concatenate([grad[...] for grad in grads], axis=0)
    line, rows, _ = kept.shape
    total = lax.dot_general(tokens, grad, (((0,), (0,)), ((), ())), preferred_element_type=f32)
    total = total * grad_scale
    others = []
    for step in range(line):
        start = step * TWIN * rows
        kept[step] = total[start : start + rows]
        others.append(total[start + rows : start + TWIN * rows].astype(bf16))
    others = jnp.concatenate(others, axis=0)
    for (start, end), piece in zip(cuts(line * rows, len(leaving)), leaving):
        piece[...] = others[start:end]


def merge_body(count, kept, *refs):
    others = jnp.concatenate([piece[...] for piece in refs[:count]], axis=0)
    own, *leaving = refs[count:]
    rows = own.shape[0]
    for step in range(kept.shape[0]):
        piece = kept[step] + others[step * rows : (step + 1) * rows].astype(f32)
        if step == 0:
            own[...] = piece
        else:
            leaving[-step][...] = piece.astype(bf16)


def sum_body(*refs):
    refs[-1][...] = sum(ref[...].astype(f32) for ref in refs[:-1])


def per_device(tokens, key_weight, cotangent):
    tok_rows, width = tokens.shape
    shard_rows, key_cols = key_weight.shape
    outer, line = lax.axis_size("outer"), lax.axis_size("line")
    parts = line * TWIN
    rows = shard_rows // (SPLIT * TWIN)
    owned = width // MEMBERS
    grad_scale = 1.0 / math.sqrt(tok_rows * outer * TWIN * MEMBERS * line)
    flops = 2 * tok_rows * owned * key_cols
    shape = jax.ShapeDtypeStruct
    block_shape, head_shape = shape((tok_rows, owned), bf16), shape((tok_rows, key_cols), bf16)
    if outer > 1:
        cut = key_weight.reshape(outer, SPLIT * TWIN, rows // outer, key_cols)
        key_weight = cut.transpose(1, 0, 2, 3).reshape(shard_rows, key_cols)
        tokens = split_runs(tokens, outer)

    both, mine, *packed = local_call(
        "front",
        front_body,
        [shape((TWIN * rows, key_cols), bf16), shape((rows, key_cols), bf16)] + [block_shape] * MEMBERS,
        tokens,
        key_weight,
        space=pltpu.HBM,
        room=53,
        scratch=[pltpu.SemaphoreType.DMA((2 + MEMBERS * parts,))],
    )
    blocks = [packed[0], None, None, None]
    for far in (3, 1, 2):
        blocks[far] = to_member(packed[far], far)
    passed = [parted(both, step) for step in range(1, (line + 1) // 2)]
    if line % 2 == 0:
        passed.append(along(mine, line // 2))
    pieces = [both]
    reach = shard_rows // SPLIT * (line - 1) // TWIN
    blocks[3], *passed = lax.optimization_barrier((blocks[3], *passed))
    relayed = local_call(
        "relay",
        functools.partial(relay_body, 2),
        [shape((end - start, key_cols), bf16) for start, end in cuts(reach, 2)],
        *passed,
        flops=8 * flops,
    )
    theirs = [to_twin(piece) for piece in relayed]
    *blocks, theirs = lax.optimization_barrier((*blocks[::-1], theirs))
    blocks = blocks[::-1]
    weight = local_call(
        "join",
        functools.partial(join_body, line, 2),
        shape((owned, key_cols), bf16),
        both,
        *passed,
        *theirs,
    )

    def share(fars, kind):
        shaped = [shape((tok_rows, key_cols), kind)] * len(fars)
        return local_call("share", share_body, shaped, *[blocks[far] for far in fars], weight, flops=flops)

    order = (3, 1, 2)
    shares = [to_member(part, far) for far, part in zip(order, share(order, bf16))]
    normed, key_grad = local_call("norm", norm_body, [head_shape] * 2, *share((0,), f32), *shares, cotangent)
    key_out = local_call("emit", emit_body, head_shape, normed)

    grad_3, grad_1, grad_2 = (to_member(key_grad, far) for far in (3, 1, 2))

    def columns(*grads):
        return local_call("columns", columns_body, [block_shape] * len(grads), *grads, weight, flops=flops)

    (column_0,), (column_3,) = columns(key_grad), columns(grad_3)
    column_0, column_3, key_out, grad_1, grad_2 = lax.optimization_barrier(
        (column_0, column_3, key_out, grad_1, grad_2)
    )
    kept, *theirs = local_call(
        "terms",
        functools.partial(terms_body, grad_scale),
        [shape((line, rows, key_cols), f32)]
        + [shape((end - start, key_cols), bf16) for start, end in cuts(line * rows, 2)],
        *blocks,
        key_grad,
        grad_1,
        grad_2,
        grad_3,
        moved=0,
    )
    theirs = [to_twin(piece) for piece in theirs]
    sums = local_call(
        "merge",
        functools.partial(merge_body, 2),
        [shape((rows, key_cols), f32)] + [shape((rows, key_cols), bf16)] * (line - 1),
        kept,
        *theirs,
        moved=0,
    )

    back_1, back_2 = (to_member(column, far) for far, column in zip((1, 2), columns(grad_1, grad_2)))
    column_3, _ = lax.optimization_barrier((column_3, sums))
    back_3 = to_member(column_3, 3)
    *sums, closest = sums
    closest, back_2 = lax.optimization_barrier((closest, back_2))
    met = [sums[0]] + [along(piece, line - i) for i, piece in enumerate(sums) if i]
    whole_shape = shape((tok_rows, width), bf16)
    (input_grad,) = placing_call(
        "unpack", functools.partial(unpack_body, (0, 2)), [whole_shape], (column_0, back_2)
    )
    met, back_1, input_grad = lax.optimization_barrier((met, back_1, input_grad))
    sum_shape = shape((rows, key_cols), f32)
    far_sum = local_call("far_sum", sum_body, sum_shape, *met, flops=24 * flops)
    total = local_call("final_sum", sum_body, sum_shape, far_sum, along(closest, 1), moved=0)
    input_grad, weight_grad = placing_call(
        "finish",
        functools.partial(finish_body, (1, 3)),
        [whole_shape, shape(total.shape, f32)],
        (back_1, back_3, total),
        (input_grad,),
    )
    if outer > 1:
        weight_grad = lax.psum_scatter(weight_grad, "outer", scatter_dimension=0, tiled=True)
    if outer > 1:
        input_grad = join_runs(input_grad, outer)
    return (key_out, input_grad, weight_grad)


def solution(mesh):
    replicas, group = mesh.shape["dp"], mesh.shape["inner"]
    fine = Mesh(
        mesh.devices.reshape(replicas // (SPLIT * TWIN), SPLIT, TWIN, group // SPLIT, SPLIT),
        ("outer", "side", "twin", "line", "pair"),
    )
    rows = P(("outer", "side", "twin", "line", "pair"), None)
    return jax.shard_map(
        per_device,
        mesh=fine,
        in_specs=(rows, P(("line", "pair"), None), rows),
        out_specs=(rows, rows, P(("line", "pair", "outer", "side", "twin"), None)),
        check_vma=False,
    )
```

```python
import functools
import math

import jax
import jax.numpy as jnp
from jax import lax
from jax.experimental import pallas as pl
from jax.experimental.pallas import tpu as pltpu
from jax.sharding import Mesh, PartitionSpec as P

HEAD_DIM = 128


epsilon = 1e-06

SPLIT = 2
TWIN = 2
MEMBERS = SPLIT * SPLIT
MIXED = (4, 5)
bf16, f32 = jnp.bfloat16, jnp.float32


def local_call(name, body, out_shapes, *args, flops=0, space=pltpu.VMEM, scratch=(), room=32, moved=None):
    vmem = pl.BlockSpec(memory_space=pltpu.VMEM)
    many = isinstance(out_shapes, (list, tuple))
    if moved is None:
        moved = sum(math.prod(a.shape) * a.dtype.itemsize for a in args)
    return pl.pallas_call(
        body,
        name=name,
        out_shape=out_shapes,
        in_specs=[pl.BlockSpec(memory_space=space)] * len(args),
        out_specs=[vmem] * len(out_shapes) if many else vmem,
        scratch_shapes=scratch,
        compiler_params=pltpu.CompilerParams(vmem_limit_bytes=int(room * 2**20)),
        cost_estimate=pl.CostEstimate(flops=flops, bytes_accessed=moved, transcendentals=0),
    )(*args)


def along(block, step):
    return lax.ppermute(block, "line", [(i, i ^ step) for i in range(lax.axis_size("line"))])


def to_twin(block):
    return lax.ppermute(block, "twin", [(0, 1), (1, 0)])


def flips(far):
    if far in MIXED:
        core = lax.axis_index("twin")
        return (1 - core, core) if far == MIXED[0] else (core, 1 - core)
    return far // SPLIT, far % SPLIT


def to_member(block, far):
    return lax.ppermute(block, ("side", "pair"), [(i, i ^ far) for i in range(MEMBERS)])


def to_mixed(block, far):
    def index(side, core, pair):
        return (side * TWIN + core) * SPLIT + pair

    pairs = []
    for i in range(MEMBERS * TWIN):
        side, core, pair = i // (TWIN * SPLIT), i // SPLIT % TWIN, i % SPLIT
        over = 1 - core if far == MIXED[0] else core
        pairs.append((i, index(side ^ over, core, pair ^ (1 - over))))
    return lax.ppermute(block, ("side", "twin", "pair"), pairs)


def run_of(part, far):
    core = lax.axis_index("twin")
    over, across = flips(far)
    place = lax.axis_index("line") ^ (part // TWIN)
    side, pair = lax.axis_index("side") ^ over, lax.axis_index("pair") ^ across
    return ((place * SPLIT + pair) * SPLIT + side) * TWIN + (core ^ (part % TWIN))


def front_body(tokens, shard, both, mine, *refs):
    *blocks, arrived = refs
    rows, half = mine.shape[0], both.shape[0]
    first = lax.axis_index("side") * half
    moves = []
    for target, start in ((both, first), (mine, first + lax.axis_index("twin") * rows)):
        moves.append((shard.at[pl.ds(pl.multiple_of(start, rows), target.shape[0])], target))
    parts = lax.axis_size("line") * TWIN
    run = blocks[0].shape[1] // parts
    for far, block in enumerate(blocks):
        for part in range(parts):
            start = pl.multiple_of(run_of(part, far) * run, run)
            moves.append((tokens.at[:, pl.ds(start, run)], block.at[:, pl.ds(part * run, run)]))
    copies = [pltpu.make_async_copy(*move, arrived.at[i]) for i, move in enumerate(moves)]
    for copy in copies:
        copy.start()
    for copy in copies:
        copy.wait()


def unpack_moves(far, block, whole):
    parts = lax.axis_size("line") * TWIN
    run = block.shape[1] // parts
    for part in range(parts):
        start = pl.multiple_of(run_of(part, far) * run, run)
        yield block.at[:, pl.ds(part * run, run)], whole.at[:, pl.ds(start, run)]


def run_copies(moves, done):
    copies = [pltpu.make_async_copy(*move, done.at[i]) for i, move in enumerate(moves)]
    for copy in copies:
        copy.start()
    for copy in copies:
        copy.wait()


def unpack_body(fars, *refs):
    *blocks, whole, done = refs
    run_copies([move for far, block in zip(fars, blocks) for move in unpack_moves(far, block, whole)], done)


def finish_body(fars, *refs):
    *blocks, total, _, whole, weight_grad, done = refs
    moves = [move for far, block in zip(fars, blocks) for move in unpack_moves(far, block, whole)]
    run_copies([(total, weight_grad), *moves], done)


def placing_call(name, body, out_shapes, blocks, held=()):
    parts = lax.axis_size("line") * TWIN
    return pl.pallas_call(
        body,
        name=name,
        out_shape=out_shapes,
        in_specs=[pl.BlockSpec(memory_space=pltpu.VMEM)] * len(blocks)
        + [pl.BlockSpec(memory_space=pl.ANY)] * len(held),
        out_specs=[pl.BlockSpec(memory_space=pl.ANY)] * len(out_shapes),
        input_output_aliases={len(blocks): 0} if held else {},
        scratch_shapes=[pltpu.SemaphoreType.DMA((len(blocks) * parts,))],
        compiler_params=pltpu.CompilerParams(vmem_limit_bytes=32 << 20),
        cost_estimate=pl.CostEstimate(flops=0, bytes_accessed=0, transcendentals=0),
    )(*blocks, *held)


def split_runs(tokens, outer):
    tok_rows, width = tokens.shape
    inner = lax.axis_size("line") * lax.axis_size("pair")
    near = SPLIT * TWIN
    cut = tokens.reshape(tok_rows, inner, outer, near, width // (inner * outer * near))
    return cut.transpose(0, 1, 3, 2, 4).reshape(tok_rows, width)


def join_runs(tokens, outer):
    tok_rows, width = tokens.shape
    inner = lax.axis_size("line") * lax.axis_size("pair")
    near = SPLIT * TWIN
    cut = tokens.reshape(tok_rows, inner, near, outer, width // (inner * outer * near))
    return cut.transpose(0, 1, 3, 2, 4).reshape(tok_rows, width)


def parted(block, step):
    line = lax.axis_size("line")
    to = [core * line + (i ^ (line - step if core else step)) for core in range(TWIN) for i in range(line)]
    return lax.ppermute(block, ("twin", "line"), list(enumerate(to)))


def cuts(rows, count):
    unit = math.gcd(rows, 64)
    ends = [-(-rows // unit * i // count) * unit for i in range(count + 1)]
    return list(zip(ends, ends[1:]))


def relay_body(count, *refs):
    rows = jnp.concatenate([ref[...] for ref in refs[:-count]], axis=0)
    for (start, end), out in zip(cuts(rows.shape[0], count), refs[-count:]):
        out[...] = rows[start:end]


def join_body(line, count, *refs):
    both, *pieces, whole = refs
    others = jnp.concatenate([piece[...] for piece in pieces[-count:]], axis=0)
    pieces = pieces[:-count]
    rows = whole.shape[0] // (line * TWIN)
    core = lax.axis_index("twin")

    def put(step, twin_run, piece):
        part = step * TWIN + (twin_run ^ core)
        whole[pl.ds(pl.multiple_of(part * rows, rows), rows), :] = piece

    def put_both(step, piece):
        for twin_run in range(TWIN):
            put(step, twin_run, piece[twin_run * rows : (twin_run + 1) * rows])

    put_both(0, both[...])
    for step in range(1, (line + 1) // 2):
        at = (step - 1) * TWIN * rows
        put_both(jnp.where(core == 0, step, line - step), pieces[step - 1][...])
        put_both(jnp.where(core == 0, line - step, step), others[at : at + TWIN * rows])
    if line % 2 == 0:
        put(line // 2, core, pieces[-1][...])
        put(line // 2, 1 - core, others[others.shape[0] - rows :])


def share_body(*refs):
    *blocks, weight = refs[: len(refs) // 2 + 1]
    outs = refs[len(blocks) + 1 :]
    stacked = jnp.concatenate([block[...] for block in blocks], axis=0)
    product = jnp.dot(stacked, weight[...], preferred_element_type=f32)
    for i, out in enumerate(outs):
        out[...] = product[i * out.shape[0] : (i + 1) * out.shape[0]].astype(out.dtype)


def columns_body(*refs):
    *grads, weight = refs[: len(refs) // 2 + 1]
    outs = refs[len(grads) + 1 :]
    stacked = jnp.concatenate([grad[...] for grad in grads], axis=0)
    product = lax.dot_general(
        stacked, weight[...], (((1,), (1,)), ((), ())), preferred_element_type=f32
    )
    for i, out in enumerate(outs):
        out[...] = product[i * out.shape[0] : (i + 1) * out.shape[0]].astype(out.dtype)


def mixed_columns_body(grad_1, grad_2, weight, first, second):
    rows = first.shape[0]
    stacked = jnp.concatenate([grad_1[...], grad_2[...]], axis=0)
    product = lax.dot_general(
        stacked, weight[...], (((1,), (1,)), ((), ())), preferred_element_type=f32
    )
    core = lax.axis_index("twin")
    first[...] = jnp.where(core == 0, product[rows:], product[:rows]).astype(first.dtype)
    second[...] = jnp.where(core == 0, product[:rows], product[rows:]).astype(second.dtype)


def emit_body(held, out):
    out[...] = held[...]


def norm_body(*refs):
    *shares, cotangent, key_out, key_grad = refs
    for head in range(key_out.shape[1] // HEAD_DIM):
        at = slice(head * HEAD_DIM, (head + 1) * HEAD_DIM)
        raw = sum(share[:, at].astype(f32) for share in shares)
        inverse = lax.rsqrt(jnp.mean(raw * raw, axis=-1, keepdims=True) + epsilon)
        normed = raw * inverse
        upstream = cotangent[:, at].astype(f32)
        projected = jnp.mean(upstream * normed, axis=-1, keepdims=True)
        key_out[:, at] = normed.astype(bf16)
        key_grad[:, at] = (inverse * (upstream - normed * projected)).astype(bf16)


def terms_body(grad_scale, *refs):
    blocks, grads, (kept, *leaving) = refs[:MEMBERS], refs[MEMBERS : 2 * MEMBERS], refs[2 * MEMBERS :]
    tokens = jnp.concatenate([block[...] for block in blocks], axis=0)
    grad = jnp.concatenate([grad[...] for grad in grads], axis=0)
    line, rows, _ = kept.shape
    total = lax.dot_general(tokens, grad, (((0,), (0,)), ((), ())), preferred_element_type=f32)
    total = total * grad_scale
    others = []
    for step in range(line):
        start = step * TWIN * rows
        kept[step] = total[start : start + rows]
        others.append(total[start + rows : start + TWIN * rows].astype(bf16))
    others = jnp.concatenate(others, axis=0)
    for (start, end), piece in zip(cuts(line * rows, len(leaving)), leaving):
        piece[...] = others[start:end]


def merge_body(count, kept, *refs):
    others = jnp.concatenate([piece[...] for piece in refs[:count]], axis=0)
    own, *leaving = refs[count:]
    rows = own.shape[0]
    for step in range(kept.shape[0]):
        piece = kept[step] + others[step * rows : (step + 1) * rows].astype(f32)
        if step == 0:
            own[...] = piece
        else:
            leaving[-step][...] = piece.astype(bf16)


def sum_body(*refs):
    refs[-1][...] = sum(ref[...].astype(f32) for ref in refs[:-1])


def per_device(tokens, key_weight, cotangent):
    tok_rows, width = tokens.shape
    shard_rows, key_cols = key_weight.shape
    outer, line = lax.axis_size("outer"), lax.axis_size("line")
    parts = line * TWIN
    rows = shard_rows // (SPLIT * TWIN)
    owned = width // MEMBERS
    grad_scale = 1.0 / math.sqrt(tok_rows * outer * TWIN * MEMBERS * line)
    flops = 2 * tok_rows * owned * key_cols
    shape = jax.ShapeDtypeStruct
    block_shape, head_shape = shape((tok_rows, owned), bf16), shape((tok_rows, key_cols), bf16)
    if outer > 1:
        cut = key_weight.reshape(outer, SPLIT * TWIN, rows // outer, key_cols)
        key_weight = cut.transpose(1, 0, 2, 3).reshape(shard_rows, key_cols)
        tokens = split_runs(tokens, outer)

    both, mine, *packed = local_call(
        "front",
        front_body,
        [shape((TWIN * rows, key_cols), bf16), shape((rows, key_cols), bf16)] + [block_shape] * MEMBERS,
        tokens,
        key_weight,
        space=pltpu.HBM,
        room=53,
        scratch=[pltpu.SemaphoreType.DMA((2 + MEMBERS * parts,))],
    )
    blocks = [packed[0], None, None, None]
    for far in (3, 1, 2):
        blocks[far] = to_member(packed[far], far)
    passed = [parted(both, step) for step in range(1, (line + 1) // 2)]
    if line % 2 == 0:
        passed.append(along(mine, line // 2))
    pieces = [both]
    reach = shard_rows // SPLIT * (line - 1) // TWIN
    blocks[3], *passed = lax.optimization_barrier((blocks[3], *passed))
    relayed = local_call(
        "relay",
        functools.partial(relay_body, 2),
        [shape((end - start, key_cols), bf16) for start, end in cuts(reach, 2)],
        *passed,
        flops=8 * flops,
    )
    theirs = [to_twin(piece) for piece in relayed]
    *blocks, theirs = lax.optimization_barrier((*blocks[::-1], theirs))
    blocks = blocks[::-1]
    weight = local_call(
        "join",
        functools.partial(join_body, line, 2),
        shape((owned, key_cols), bf16),
        both,
        *passed,
        *theirs,
    )

    def share(fars, kind):
        shaped = [shape((tok_rows, key_cols), kind)] * len(fars)
        return local_call("share", share_body, shaped, *[blocks[far] for far in fars], weight, flops=flops)

    order = (3, 1, 2)
    shares = [to_member(part, far) for far, part in zip(order, share(order, bf16))]
    normed, key_grad = local_call("norm", norm_body, [head_shape] * 2, *share((0,), f32), *shares, cotangent)
    key_out = local_call("emit", emit_body, head_shape, normed)

    grad_3, grad_1, grad_2 = (to_member(key_grad, far) for far in (3, 1, 2))

    def columns(*grads):
        return local_call("columns", columns_body, [block_shape] * len(grads), *grads, weight, flops=flops)

    (column_0,), (column_3,) = columns(key_grad), columns(grad_3)
    column_0, column_3, key_out, grad_1, grad_2 = lax.optimization_barrier(
        (column_0, column_3, key_out, grad_1, grad_2)
    )
    kept, *theirs = local_call(
        "terms",
        functools.partial(terms_body, grad_scale),
        [shape((line, rows, key_cols), f32)]
        + [shape((end - start, key_cols), bf16) for start, end in cuts(line * rows, 2)],
        *blocks,
        key_grad,
        grad_1,
        grad_2,
        grad_3,
        moved=0,
    )
    theirs = [to_twin(piece) for piece in theirs]
    sums = local_call(
        "merge",
        functools.partial(merge_body, 2),
        [shape((rows, key_cols), f32)] + [shape((rows, key_cols), bf16)] * (line - 1),
        kept,
        *theirs,
        moved=0,
    )

    mixed = local_call(
        "columns", mixed_columns_body, [block_shape] * 2, grad_1, grad_2, weight, flops=flops
    )
    back_2, back_1 = (to_mixed(column, far) for far, column in zip(MIXED, mixed))
    column_3, _ = lax.optimization_barrier((column_3, sums))
    back_3 = to_member(column_3, 3)
    *sums, closest = sums
    closest, back_2 = lax.optimization_barrier((closest, back_2))
    met = [sums[0]] + [along(piece, line - i) for i, piece in enumerate(sums) if i]
    whole_shape = shape((tok_rows, width), bf16)
    (input_grad,) = placing_call(
        "unpack", functools.partial(unpack_body, (0, MIXED[0])), [whole_shape], (column_0, back_2)
    )
    met, back_1, input_grad = lax.optimization_barrier((met, back_1, input_grad))
    sum_shape = shape((rows, key_cols), f32)
    far_sum = local_call("far_sum", sum_body, sum_shape, *met, flops=24 * flops)
    total = local_call("final_sum", sum_body, sum_shape, far_sum, along(closest, 1), moved=0)
    input_grad, weight_grad = placing_call(
        "finish",
        functools.partial(finish_body, (MIXED[1], 3)),
        [whole_shape, shape(total.shape, f32)],
        (back_1, back_3, total),
        (input_grad,),
    )
    if outer > 1:
        weight_grad = lax.psum_scatter(weight_grad, "outer", scatter_dimension=0, tiled=True)
    if outer > 1:
        input_grad = join_runs(input_grad, outer)
    return (key_out, input_grad, weight_grad)


def solution(mesh):
    replicas, group = mesh.shape["dp"], mesh.shape["inner"]
    fine = Mesh(
        mesh.devices.reshape(replicas // (SPLIT * TWIN), SPLIT, TWIN, group // SPLIT, SPLIT),
        ("outer", "side", "twin", "line", "pair"),
    )
    rows = P(("outer", "side", "twin", "line", "pair"), None)
    return jax.shard_map(
        per_device,
        mesh=fine,
        in_specs=(rows, P(("line", "pair"), None), rows),
        out_specs=(rows, rows, P(("line", "pair", "outer", "side", "twin"), None)),
        check_vma=False,
    )
```

```python
import functools
import math

import jax
import jax.numpy as jnp
from jax import lax
from jax.experimental import pallas as pl
from jax.experimental.pallas import tpu as pltpu
from jax.sharding import Mesh, PartitionSpec as P

HEAD_DIM = 128


epsilon = 1e-06

SPLIT = 2
TWIN = 2
MEMBERS = SPLIT * SPLIT
MIXED = (4, 5)
bf16, f32 = jnp.bfloat16, jnp.float32


def local_call(name, body, out_shapes, *args, flops=0, space=pltpu.VMEM, scratch=(), room=32, moved=None):
    vmem = pl.BlockSpec(memory_space=pltpu.VMEM)
    many = isinstance(out_shapes, (list, tuple))
    if moved is None:
        moved = sum(math.prod(a.shape) * a.dtype.itemsize for a in args)
    return pl.pallas_call(
        body,
        name=name,
        out_shape=out_shapes,
        in_specs=[pl.BlockSpec(memory_space=space)] * len(args),
        out_specs=[vmem] * len(out_shapes) if many else vmem,
        scratch_shapes=scratch,
        compiler_params=pltpu.CompilerParams(vmem_limit_bytes=int(room * 2**20)),
        cost_estimate=pl.CostEstimate(flops=flops, bytes_accessed=moved, transcendentals=0),
    )(*args)


def along(block, step):
    return lax.ppermute(block, "line", [(i, i ^ step) for i in range(lax.axis_size("line"))])


def to_twin(block):
    return lax.ppermute(block, "twin", [(0, 1), (1, 0)])


def flips(far):
    if far in MIXED:
        core = lax.axis_index("twin")
        return (1 - core, core) if far == MIXED[0] else (core, 1 - core)
    return far // SPLIT, far % SPLIT


def to_member(block, far):
    return lax.ppermute(block, ("side", "pair"), [(i, i ^ far) for i in range(MEMBERS)])


def to_mixed(block, far):
    def index(side, core, pair):
        return (side * TWIN + core) * SPLIT + pair

    pairs = []
    for i in range(MEMBERS * TWIN):
        side, core, pair = i // (TWIN * SPLIT), i // SPLIT % TWIN, i % SPLIT
        over = 1 - core if far == MIXED[0] else core
        pairs.append((i, index(side ^ over, core, pair ^ (1 - over))))
    return lax.ppermute(block, ("side", "twin", "pair"), pairs)


def run_of(part, far):
    core = lax.axis_index("twin")
    over, across = flips(far)
    place = lax.axis_index("line") ^ (part // TWIN)
    side, pair = lax.axis_index("side") ^ over, lax.axis_index("pair") ^ across
    return ((place * SPLIT + pair) * SPLIT + side) * TWIN + (core ^ (part % TWIN))


def front_body(tokens, shard, both, mine, *refs):
    *blocks, arrived = refs
    rows, half = mine.shape[0], both.shape[0]
    first = lax.axis_index("side") * half
    moves = []
    for target, start in ((both, first), (mine, first + lax.axis_index("twin") * rows)):
        moves.append((shard.at[pl.ds(pl.multiple_of(start, rows), target.shape[0])], target))
    parts = lax.axis_size("line") * TWIN
    run = blocks[0].shape[1] // parts
    for far, block in enumerate(blocks):
        for part in range(parts):
            start = pl.multiple_of(run_of(part, far) * run, run)
            moves.append((tokens.at[:, pl.ds(start, run)], block.at[:, pl.ds(part * run, run)]))
    copies = [pltpu.make_async_copy(*move, arrived.at[i]) for i, move in enumerate(moves)]
    for copy in copies:
        copy.start()
    for copy in copies:
        copy.wait()


def unpack_moves(far, block, whole):
    parts = lax.axis_size("line") * TWIN
    run = block.shape[1] // parts
    for part in range(parts):
        start = pl.multiple_of(run_of(part, far) * run, run)
        yield block.at[:, pl.ds(part * run, run)], whole.at[:, pl.ds(start, run)]


def run_copies(moves, done):
    copies = [pltpu.make_async_copy(*move, done.at[i]) for i, move in enumerate(moves)]
    for copy in copies:
        copy.start()
    for copy in copies:
        copy.wait()


def unpack_body(fars, *refs):
    *blocks, whole, done = refs
    run_copies([move for far, block in zip(fars, blocks) for move in unpack_moves(far, block, whole)], done)


def finish_body(fars, *refs):
    *blocks, total, _, whole, weight_grad, done = refs
    moves = [move for far, block in zip(fars, blocks) for move in unpack_moves(far, block, whole)]
    run_copies([(total, weight_grad), *moves], done)


def placing_call(name, body, out_shapes, blocks, held=()):
    parts = lax.axis_size("line") * TWIN
    return pl.pallas_call(
        body,
        name=name,
        out_shape=out_shapes,
        in_specs=[pl.BlockSpec(memory_space=pltpu.VMEM)] * len(blocks)
        + [pl.BlockSpec(memory_space=pl.ANY)] * len(held),
        out_specs=[pl.BlockSpec(memory_space=pl.ANY)] * len(out_shapes),
        input_output_aliases={len(blocks): 0} if held else {},
        scratch_shapes=[pltpu.SemaphoreType.DMA((len(blocks) * parts,))],
        compiler_params=pltpu.CompilerParams(vmem_limit_bytes=32 << 20),
        cost_estimate=pl.CostEstimate(flops=0, bytes_accessed=0, transcendentals=0),
    )(*blocks, *held)


def split_runs(tokens, outer):
    tok_rows, width = tokens.shape
    inner = lax.axis_size("line") * lax.axis_size("pair")
    near = SPLIT * TWIN
    cut = tokens.reshape(tok_rows, inner, outer, near, width // (inner * outer * near))
    return cut.transpose(0, 1, 3, 2, 4).reshape(tok_rows, width)


def join_runs(tokens, outer):
    tok_rows, width = tokens.shape
    inner = lax.axis_size("line") * lax.axis_size("pair")
    near = SPLIT * TWIN
    cut = tokens.reshape(tok_rows, inner, near, outer, width // (inner * outer * near))
    return cut.transpose(0, 1, 3, 2, 4).reshape(tok_rows, width)


def parted(block, step):
    line = lax.axis_size("line")
    to = [core * line + (i ^ (line - step if core else step)) for core in range(TWIN) for i in range(line)]
    return lax.ppermute(block, ("twin", "line"), list(enumerate(to)))


def cuts(rows, count):
    unit = math.gcd(rows, 64)
    ends = [-(-rows // unit * i // count) * unit for i in range(count + 1)]
    return list(zip(ends, ends[1:]))


def relay_body(count, *refs):
    rows = jnp.concatenate([ref[...] for ref in refs[:-count]], axis=0)
    for (start, end), out in zip(cuts(rows.shape[0], count), refs[-count:]):
        out[...] = rows[start:end]


def join_body(line, count, *refs):
    both, *pieces, whole = refs
    others = jnp.concatenate([piece[...] for piece in pieces[-count:]], axis=0)
    pieces = pieces[:-count]
    rows = whole.shape[0] // (line * TWIN)
    core = lax.axis_index("twin")

    def put(step, twin_run, piece):
        part = step * TWIN + (twin_run ^ core)
        whole[pl.ds(pl.multiple_of(part * rows, rows), rows), :] = piece

    def put_both(step, piece):
        for twin_run in range(TWIN):
            put(step, twin_run, piece[twin_run * rows : (twin_run + 1) * rows])

    put_both(0, both[...])
    for step in range(1, (line + 1) // 2):
        at = (step - 1) * TWIN * rows
        put_both(jnp.where(core == 0, step, line - step), pieces[step - 1][...])
        put_both(jnp.where(core == 0, line - step, step), others[at : at + TWIN * rows])
    if line % 2 == 0:
        put(line // 2, core, pieces[-1][...])
        put(line // 2, 1 - core, others[others.shape[0] - rows :])


def share_body(*refs):
    *blocks, weight = refs[: len(refs) // 2 + 1]
    outs = refs[len(blocks) + 1 :]
    stacked = jnp.concatenate([block[...] for block in blocks], axis=0)
    product = jnp.dot(stacked, weight[...], preferred_element_type=f32)
    for i, out in enumerate(outs):
        out[...] = product[i * out.shape[0] : (i + 1) * out.shape[0]].astype(out.dtype)


def columns_body(*refs):
    *grads, weight = refs[: len(refs) // 2 + 1]
    outs = refs[len(grads) + 1 :]
    stacked = jnp.concatenate([grad[...] for grad in grads], axis=0)
    product = lax.dot_general(
        stacked, weight[...], (((1,), (1,)), ((), ())), preferred_element_type=f32
    )
    for i, out in enumerate(outs):
        out[...] = product[i * out.shape[0] : (i + 1) * out.shape[0]].astype(out.dtype)


def mixed_columns_body(grad_1, grad_2, weight, first, second):
    rows = first.shape[0]
    stacked = jnp.concatenate([grad_1[...], grad_2[...]], axis=0)
    product = lax.dot_general(
        stacked, weight[...], (((1,), (1,)), ((), ())), preferred_element_type=f32
    )
    core = lax.axis_index("twin")
    first[...] = jnp.where(core == 0, product[rows:], product[:rows]).astype(first.dtype)
    second[...] = jnp.where(core == 0, product[:rows], product[rows:]).astype(second.dtype)


def emit_body(held, out):
    out[...] = held[...]


def norm_body(*refs):
    *shares, cotangent, key_out, key_grad = refs
    for head in range(key_out.shape[1] // HEAD_DIM):
        at = slice(head * HEAD_DIM, (head + 1) * HEAD_DIM)
        raw = sum(share[:, at].astype(f32) for share in shares)
        inverse = lax.rsqrt(jnp.mean(raw * raw, axis=-1, keepdims=True) + epsilon)
        normed = raw * inverse
        upstream = cotangent[:, at].astype(f32)
        projected = jnp.mean(upstream * normed, axis=-1, keepdims=True)
        key_out[:, at] = normed.astype(bf16)
        key_grad[:, at] = (inverse * (upstream - normed * projected)).astype(bf16)


def terms_body(grad_scale, *refs):
    blocks, grads, (kept, *leaving) = refs[:MEMBERS], refs[MEMBERS : 2 * MEMBERS], refs[2 * MEMBERS :]
    tokens = jnp.concatenate([block[...] for block in blocks], axis=0)
    grad = jnp.concatenate([grad[...] for grad in grads], axis=0)
    line, rows, _ = kept.shape
    total = lax.dot_general(tokens, grad, (((0,), (0,)), ((), ())), preferred_element_type=f32)
    total = total * grad_scale
    others = []
    for step in range(line):
        start = step * TWIN * rows
        kept[step] = total[start : start + rows]
        others.append(total[start + rows : start + TWIN * rows].astype(bf16))
    others = jnp.concatenate(others, axis=0)
    for (start, end), piece in zip(cuts(line * rows, len(leaving)), leaving):
        piece[...] = others[start:end]


def merge_body(count, kept, *refs):
    others = jnp.concatenate([piece[...] for piece in refs[:count]], axis=0)
    own, *leaving = refs[count:]
    rows = own.shape[0]
    for step in range(kept.shape[0]):
        piece = kept[step] + others[step * rows : (step + 1) * rows].astype(f32)
        if step == 0:
            own[...] = piece
        else:
            leaving[-step][...] = piece.astype(bf16)


def sum_body(*refs):
    refs[-1][...] = sum(ref[...].astype(f32) for ref in refs[:-1])


def per_device(tokens, key_weight, cotangent):
    tok_rows, width = tokens.shape
    shard_rows, key_cols = key_weight.shape
    outer, line = lax.axis_size("outer"), lax.axis_size("line")
    parts = line * TWIN
    rows = shard_rows // (SPLIT * TWIN)
    owned = width // MEMBERS
    grad_scale = 1.0 / math.sqrt(tok_rows * outer * TWIN * MEMBERS * line)
    flops = 2 * tok_rows * owned * key_cols
    shape = jax.ShapeDtypeStruct
    block_shape, head_shape = shape((tok_rows, owned), bf16), shape((tok_rows, key_cols), bf16)
    if outer > 1:
        cut = key_weight.reshape(outer, SPLIT * TWIN, rows // outer, key_cols)
        key_weight = cut.transpose(1, 0, 2, 3).reshape(shard_rows, key_cols)
        tokens = split_runs(tokens, outer)

    both, mine, *packed = local_call(
        "front",
        front_body,
        [shape((TWIN * rows, key_cols), bf16), shape((rows, key_cols), bf16)] + [block_shape] * MEMBERS,
        tokens,
        key_weight,
        space=pltpu.HBM,
        room=53,
        scratch=[pltpu.SemaphoreType.DMA((2 + MEMBERS * parts,))],
    )
    blocks = [packed[0], None, None, None]
    for far in (3, 1, 2):
        blocks[far] = to_member(packed[far], far)
    passed = [parted(both, step) for step in range(1, (line + 1) // 2)]
    if line % 2 == 0:
        passed.append(along(mine, line // 2))
    pieces = [both]
    reach = shard_rows // SPLIT * (line - 1) // TWIN
    blocks[3], *passed = lax.optimization_barrier((blocks[3], *passed))
    relayed = local_call(
        "relay",
        functools.partial(relay_body, 2),
        [shape((end - start, key_cols), bf16) for start, end in cuts(reach, 2)],
        *passed,
        flops=8 * flops,
    )
    theirs = [to_twin(piece) for piece in relayed]
    *blocks, theirs = lax.optimization_barrier((*blocks[::-1], theirs))
    blocks = blocks[::-1]
    weight = local_call(
        "join",
        functools.partial(join_body, line, 2),
        shape((owned, key_cols), bf16),
        both,
        *passed,
        *theirs,
    )

    def share(fars, kind):
        shaped = [shape((tok_rows, key_cols), kind)] * len(fars)
        return local_call("share", share_body, shaped, *[blocks[far] for far in fars], weight, flops=flops)

    order = (3, 1, 2)
    shares = [to_member(part, far) for far, part in zip(order, share(order, bf16))]
    normed, key_grad = local_call("norm", norm_body, [head_shape] * 2, *share((0,), f32), *shares, cotangent)
    key_out = local_call("emit", emit_body, head_shape, normed)

    grad_3, grad_1, grad_2 = (to_member(key_grad, far) for far in (3, 1, 2))

    def columns(*grads):
        return local_call("columns", columns_body, [block_shape] * len(grads), *grads, weight, flops=flops)

    (column_0,), (column_3,) = columns(key_grad), columns(grad_3)
    column_0, column_3, key_out, grad_1, grad_2 = lax.optimization_barrier(
        (column_0, column_3, key_out, grad_1, grad_2)
    )
    kept, *theirs = local_call(
        "terms",
        functools.partial(terms_body, grad_scale),
        [shape((line, rows, key_cols), f32)]
        + [shape((end - start, key_cols), bf16) for start, end in cuts(line * rows, 2)],
        *blocks,
        key_grad,
        grad_1,
        grad_2,
        grad_3,
        moved=0,
    )
    theirs = [to_twin(piece) for piece in theirs]
    sums = local_call(
        "merge",
        functools.partial(merge_body, 2),
        [shape((rows, key_cols), f32)] + [shape((rows, key_cols), bf16)] * (line - 1),
        kept,
        *theirs,
        moved=0,
    )

    mixed = local_call(
        "columns", mixed_columns_body, [block_shape] * 2, grad_1, grad_2, weight, flops=flops
    )
    back_2, back_1 = (to_mixed(column, far) for far, column in zip(MIXED, mixed))
    column_3, _ = lax.optimization_barrier((column_3, sums))
    back_3 = to_member(column_3, 3)
    *sums, closest = sums
    closest, back_2 = lax.optimization_barrier((closest, back_2))
    met = [sums[0]] + [along(piece, line - i) for i, piece in enumerate(sums) if i]
    whole_shape = shape((tok_rows, width), bf16)
    (input_grad,) = placing_call(
        "unpack", functools.partial(unpack_body, (0, *MIXED)), [whole_shape], (column_0, back_2, back_1)
    )
    met, input_grad = lax.optimization_barrier((met, input_grad))
    sum_shape = shape((rows, key_cols), f32)
    far_sum = local_call("far_sum", sum_body, sum_shape, *met, flops=24 * flops)
    total = local_call("final_sum", sum_body, sum_shape, far_sum, along(closest, 1), moved=0)
    input_grad, weight_grad = placing_call(
        "finish",
        functools.partial(finish_body, (3,)),
        [whole_shape, shape(total.shape, f32)],
        (back_3, total),
        (input_grad,),
    )
    if outer > 1:
        weight_grad = lax.psum_scatter(weight_grad, "outer", scatter_dimension=0, tiled=True)
    if outer > 1:
        input_grad = join_runs(input_grad, outer)
    return (key_out, input_grad, weight_grad)


def solution(mesh):
    replicas, group = mesh.shape["dp"], mesh.shape["inner"]
    fine = Mesh(
        mesh.devices.reshape(replicas // (SPLIT * TWIN), SPLIT, TWIN, group // SPLIT, SPLIT),
        ("outer", "side", "twin", "line", "pair"),
    )
    rows = P(("outer", "side", "twin", "line", "pair"), None)
    return jax.shard_map(
        per_device,
        mesh=fine,
        in_specs=(rows, P(("line", "pair"), None), rows),
        out_specs=(rows, rows, P(("line", "pair", "outer", "side", "twin"), None)),
        check_vma=False,
    )
```
